32 devices in a mesh: dp: 2 (over x), seq: 16 (over z, y, core).
Axes of the slice: x: 2, y: 2, z: 4, core: 2. Of those that a mesh axis runs over, the one named last changes fastest.
Arguments:
- tokens: bfloat16 [4, 8192, 512], P('dp', 'seq'), may hold values from -6 to 6
- cotangent: bfloat16 [4, 8192, 512], P('dp', 'seq'), may hold values from -6 to 6
- gain_attn: float32 [512], replicated, may hold values from 0.5 to 1.5
- shift_attn: float32 [512], replicated, may hold values from -1 to 1
- w_qkv: bfloat16 [512, 1536], replicated, may hold values from -0.25 to 0.25
- b_qkv: float32 [1536], replicated, may hold values from -1 to 1
- w_out: bfloat16 [512, 512], replicated, may hold values from -2 to 2
- b_out: float32 [512], replicated, may hold values from -1 to 1
- gain_ffn: float32 [512], replicated, may hold values from 0.5 to 1.5
- shift_ffn: float32 [512], replicated, may hold values from -1 to 1
- w_up: bfloat16 [512, 2048], replicated, may hold values from -0.25 to 0.25
- b_up: float32 [2048], replicated, may hold values from -1 to 1
- w_down: bfloat16 [2048, 512], replicated, may hold values from -0.125 to 0.125
- b_down: float32 [512], replicated, may hold values from -1 to 1
- tables: bfloat16 [2, 256, 64], replicated, as said below
- pick: int32 [1], replicated, may hold values from 0 to 1023
Outputs:
- block_out: bfloat16 [4, 8192, 512], P('dp', 'seq')
- grad_tokens: bfloat16 [4, 8192, 512], P('dp', 'seq')
- grad_gain_attn: float32 [512], replicated
- grad_shift_attn: float32 [512], replicated
- grad_w_qkv: float32 [512, 1536], replicated
- grad_b_qkv: float32 [1536], replicated
- grad_w_out: float32 [512, 512], replicated
- grad_b_out: float32 [512], replicated
- grad_gain_ffn: float32 [512], replicated
- grad_shift_ffn: float32 [512], replicated
- grad_w_up: float32 [512, 2048], replicated
- grad_b_up: float32 [2048], replicated
- grad_w_down: float32 [2048, 512], replicated
- grad_b_down: float32 [512], replicated
The draws below stay inside these ranges and needn't reach their ends.
Inputs may be any that keep to these rules, and one draw needn't show every extreme that they name: `tables`: each matrix consists of groups of 64 mutually orthogonal rows, each of length sqrt(64).
All inputs are finite; a program needn't handle non-finite values.
Results may differ from the reference program's by a relative error of at most 0.018.
Values sent between devices are 32-bit elements; how exact they have to be, the bound alone decides.
No kernel may reach another device: no remote copies, remote signals or barrier semaphores. Data moves between devices by JAX's collectives and lax.ppermute only.
A program may use at most 256 MiB of HBM per device.

```python
import math
import jax
import jax.numpy as jnp
from jax import lax

D = 512
HEADS = 8
HEAD_DIM = 64
FEATS = 256
FF = 2048
SPAN = 512
LENGTH = 8192
SEQS = 4


def draw_tables(key, part):
    key = jax.random.fold_in(key, 7)
    groups = FEATS // HEAD_DIM
    count = 2 * groups
    perm_key, row_key, col_key = jax.random.split(key, 3)
    orders = jax.vmap(lambda single: jax.random.permutation(single, HEAD_DIM))(jax.random.split(perm_key, count))
    freq = jnp.arange(HEAD_DIM, dtype=jnp.float32)
    spots = orders.astype(jnp.float32)
    angle = math.pi * (2.0 * spots[:, None, :] + 1.0) * freq[None, :, None] / (2.0 * HEAD_DIM)
    weight = jnp.where(freq == 0.0, math.sqrt(1.0 / HEAD_DIM), math.sqrt(2.0 / HEAD_DIM))
    basis = jnp.cos(angle) * weight[None, :, None]
    row_sign = jax.random.rademacher(row_key, (count, HEAD_DIM, 1), jnp.float32)
    col_sign = jax.random.rademacher(col_key, (count, 1, HEAD_DIM), jnp.float32)
    rows = basis * row_sign * col_sign * math.sqrt(HEAD_DIM)
    return rows.reshape(2, FEATS, HEAD_DIM).astype(jnp.bfloat16)


def block_scale(stream_key, dims, cuts, smallest, top_value):
    def one(axis_at, blocks):
        steps = jax.random.uniform(jax.random.fold_in(jax.random.fold_in(stream_key, 6), axis_at), (blocks,), jnp.float32, smallest / len(cuts), top_value / len(cuts))
        return jnp.repeat(jnp.exp(steps), dims[axis_at] // blocks).reshape((-1,) + (1,) * (len(dims) - axis_at - 1))

    level = one(*cuts[0])
    for cut in cuts[1:]:
        level = level * one(*cut)
    return level


def normal_values(key, dims, width, most, cuts=(), kind=jnp.bfloat16):
    factor_of = block_scale(key, dims, cuts, -0.22, 0.18) if cuts else 1.0
    drawn = jax.random.normal(key, dims, jnp.float32) * width * factor_of
    return jnp.minimum(jnp.maximum(drawn, -most), most).astype(kind)


def setup_inputs(seed: int = 0) -> dict:
    keys = jax.random.split(jax.random.key(seed), 17)
    tokens = normal_values(keys[0], (SEQS, LENGTH, D), 1.0, 6.0, ((0, 2), (1, 16)))
    cotangent = normal_values(keys[1], (SEQS, LENGTH, D), 1.0, 6.0, ((0, 2), (1, 16)))
    gain_attn = jnp.clip(1.0 + 0.1 * jax.random.normal(keys[2], (D,), jnp.float32), 0.5, 1.5)
    shift_attn = normal_values(keys[3], (D,), 0.2, 1.0, (), jnp.float32)
    w_qkv = normal_values(keys[4], (D, 3 * D), D ** -0.5, 0.25)
    b_qkv = normal_values(keys[5], (3 * D,), 0.2, 1.0, (), jnp.float32)
    w_out = normal_values(keys[6], (D, D), (D // 64) ** -0.5, 2.0)
    b_out = normal_values(keys[7], (D,), 0.2, 1.0, (), jnp.float32)
    gain_ffn = jnp.clip(1.0 + 0.1 * jax.random.normal(keys[8], (D,), jnp.float32), 0.5, 1.5)
    shift_ffn = normal_values(keys[9], (D,), 0.2, 1.0, (), jnp.float32)
    w_up = normal_values(keys[10], (D, FF), D ** -0.5, 0.25)
    b_up = normal_values(keys[11], (FF,), 0.2, 1.0, (), jnp.float32)
    w_down = normal_values(keys[12], (FF, D), FF ** -0.5, 0.125)
    b_down = normal_values(keys[13], (D,), 0.2, 1.0, (), jnp.float32)
    tables = draw_tables(jax.random.fold_in(keys[16], 71), 0)
    pick = jax.random.randint(keys[15], (1,), 0, 1024).astype(jnp.int32)
    return {"tokens": tokens, "cotangent": cotangent, "gain_attn": gain_attn, "shift_attn": shift_attn, "w_qkv": w_qkv, "b_qkv": b_qkv, "w_out": w_out, "b_out": b_out, "gain_ffn": gain_ffn, "shift_ffn": shift_ffn, "w_up": w_up, "b_up": b_up, "w_down": w_down, "b_down": b_down, "tables": tables, "pick": pick}


@jax.custom_vjp
def lower_precision(v):
    return lax.optimization_barrier(v.astype(jnp.bfloat16)).astype(jnp.float32)

@jax.custom_vjp
def lower_precision_backward(v):
    return v

def low_keep(v):
    return (lower_precision(v), None)

def low_pass(kept, grad):
    return (grad,)

def back_keep(v):
    return (v, None)

def back_low(kept, grad):
    return (lower_precision(grad),)
lower_precision.defvjp(low_keep, low_pass)
lower_precision_backward.defvjp(back_keep, back_low)
highest_precision = lax.Precision.HIGHEST

def layer_norm(values, gain, shift):
    center = values - lax.optimization_barrier(jnp.mean(values, axis=-1, keepdims=True))
    spread = lax.optimization_barrier(jnp.mean(center * center, axis=-1, keepdims=True))
    return center * lax.rsqrt(spread + 1e-05) * gain + shift

def feature_map(heads_in, table):
    proj = lower_precision_backward(jnp.einsum('lhd,md->lhm', heads_in, table, precision=highest_precision) * HEAD_DIM ** (-0.25))
    square = lax.optimization_barrier(jnp.sum(heads_in * heads_in, axis=-1, keepdims=True)) * (0.5 * HEAD_DIM ** (-0.5))
    return jnp.exp(proj - square) * FEATS ** (-0.5)

def exclusive_sum(values):
    running = jnp.cumsum(values, axis=0)
    return jnp.concatenate([jnp.zeros_like(values[:1]), running[:-1]], axis=0)

def favor_attention(phi_q, phi_k, value):
    length = phi_q.shape[0]
    blocks = length // SPAN
    query_blocks = phi_q.reshape(blocks, SPAN, HEADS, FEATS)
    key_blocks = phi_k.reshape(blocks, SPAN, HEADS, FEATS)
    value_blocks = value.reshape(blocks, SPAN, HEADS, HEAD_DIM)
    states = lower_precision_backward(jnp.einsum('cjhm,cjhd->chmd', key_blocks, value_blocks, precision=highest_precision))
    norms = lax.optimization_barrier(jnp.sum(key_blocks, axis=1))
    prev_states = lower_precision(exclusive_sum(states))
    prev_norms = lower_precision(exclusive_sum(norms))
    causal = (lax.broadcasted_iota(jnp.int32, (SPAN, SPAN), 0) >= lax.broadcasted_iota(jnp.int32, (SPAN, SPAN), 1)).astype(jnp.float32)

    def one_block(items):
        query_block_rows, block_k, value_block_rows, state_block_rows, block_n = items
        score_matrix = lower_precision_backward(jnp.einsum('ihm,jhm->hij', query_block_rows, block_k, precision=highest_precision) * causal)
        denom = lax.optimization_barrier(jnp.sum(score_matrix, axis=-1)).T + jnp.einsum('ihm,hm->ih', query_block_rows, block_n, precision=highest_precision)
        numerator = lower_precision_backward(jnp.einsum('zke,ezm->kzm', lower_precision(score_matrix), value_block_rows, precision=highest_precision) + jnp.einsum('gtj,tjs->gts', query_block_rows, state_block_rows, precision=highest_precision))
        return numerator / denom[..., None]
    result = lax.map(jax.checkpoint(one_block), (query_blocks, key_blocks, value_blocks, prev_states, prev_norms))
    return result.reshape(length, HEADS * HEAD_DIM)

def sequence_forward(resid_in, gain_attn, shift_attn, w_qkv, b_qkv, w_out, b_out, gain_ffn, shift_ffn, w_up, b_up, w_down, b_down, table):
    normed_low = lower_precision(layer_norm(resid_in, gain_attn, shift_attn))
    projected = lower_precision(lower_precision_backward(jnp.dot(normed_low, w_qkv, precision=highest_precision) + b_qkv))
    query = projected[:, :D].reshape(-1, HEADS, HEAD_DIM)
    key_in = projected[:, D:2 * D].reshape(-1, HEADS, HEAD_DIM)
    value = projected[:, 2 * D:].reshape(-1, HEADS, HEAD_DIM)
    phi_q = lower_precision(feature_map(query, table))
    phi_k = lower_precision(feature_map(key_in, table))
    mixed = lower_precision(favor_attention(phi_q, phi_k, value))
    middle = resid_in + lower_precision_backward(jnp.dot(mixed, w_out, precision=highest_precision)) + b_out
    normed_two = lower_precision(layer_norm(middle, gain_ffn, shift_ffn))
    upper = lower_precision_backward(jnp.dot(normed_two, w_up, precision=highest_precision) + b_up)
    hidden = lower_precision(jax.nn.gelu(upper, approximate=True))
    return middle + jnp.dot(hidden, w_down, precision=highest_precision) + b_down

def reference(tokens, cotangent, gain_attn, shift_attn, w_qkv, b_qkv, w_out, b_out, gain_ffn, shift_ffn, w_up, b_up, w_down, b_down, tables, pick):
    weights = tuple((item.astype(jnp.float32) for item in (gain_attn, shift_attn, w_qkv, b_qkv, w_out, b_out, gain_ffn, shift_ffn, w_up, b_up, w_down, b_down)))
    choice_index = (pick[0] % 2).astype(jnp.int32)
    table = lax.dynamic_index_in_dim(tables, choice_index, 0, keepdims=False).astype(jnp.float32)

    def per_sequence(totals, inputs):
        seq_in, seq_grad = inputs

        def forward(resid_in, *params):
            return sequence_forward(resid_in, *params, table)
        result, pull = jax.vjp(forward, seq_in.astype(jnp.float32), *weights)
        grads = pull(seq_grad.astype(jnp.float32))
        totals = tuple((total + grad for total, grad in zip(totals, grads[1:])))
        return (totals, (result.astype(jnp.bfloat16), grads[0].astype(jnp.bfloat16)))
    zeros = tuple((jnp.zeros(item.shape, jnp.float32) for item in weights))
    totals, (outputs, grad_in) = lax.scan(per_sequence, zeros, (tokens, cotangent))
    return (outputs, grad_in, totals[0], totals[1], totals[2], totals[3], totals[4], totals[5], totals[6], totals[7], totals[8], totals[9], totals[10], totals[11])
```

```python
import functools
import math

import jax
import jax.numpy as jnp
from jax import lax
from jax.experimental import pallas as pl
from jax.experimental.pallas import tpu as pltpu
from jax.sharding import PartitionSpec as P

HEADS = 8
HEAD_DIM = 64
FEATS = 256
PAIRS = HEADS // 2
LANES = 2 * HEAD_DIM
AXES = ("dp", "seq")
BF = jnp.bfloat16
F32 = jnp.float32
Z_SCALE = HEAD_DIM ** (-0.25)
SQ_SCALE = 0.5 * HEAD_DIM ** (-0.5) / Z_SCALE
EXP_SCALE = Z_SCALE * math.log2(math.e)
EXP_SHIFT = 0.5 * math.log2(FEATS)
STATE_ROWS = PAIRS * LANES
SCAN_ROWS = STATE_ROWS + 16
TILE = 256
GELU_A = math.sqrt(2.0 / math.pi)
GELU_B = 0.044715
VMEM = 56 * 1024 * 1024


def dot(a, b):
    return lax.dot_general(a, b, (((1,), (0,)), ((), ())), preferred_element_type=F32)


def dot_nt(a, b):
    return lax.dot_general(a, b, (((1,), (1,)), ((), ())), preferred_element_type=F32)


def dot_tn(a, b):
    return lax.dot_general(a, b, (((0,), (0,)), ((), ())), preferred_element_type=F32)


def lower_half(shape):
    return lax.broadcasted_iota(jnp.int32, shape, 1) < HEAD_DIM


def swap_halves(values):
    return pltpu.roll(values, HEAD_DIM, 1)


def normalise(values):
    center = values - jnp.mean(values, axis=-1, keepdims=True)
    spread = jnp.mean(center * center, axis=-1, keepdims=True)
    scale = lax.rsqrt(spread + 1e-05)
    return center * scale, scale


def normalise_back(grad, unit, scale, gain):
    inner = grad * gain
    first = jnp.mean(inner, axis=-1, keepdims=True)
    second = jnp.mean(inner * unit, axis=-1, keepdims=True)
    return scale * (inner - first - unit * second)


def features(pair, tabs):
    wide = pair.astype(F32)
    square = wide * wide * SQ_SCALE
    high = square.astype(BF).astype(F32)
    low = swap_halves(square - high)
    keep = lower_half(wide.shape)
    even = jnp.where(keep, high, low).astype(BF)
    odd = jnp.where(keep, low, high).astype(BF)
    out = []
    for block, tab in ((even, tabs[0]), (odd, tabs[1])):
        proj = dot_nt(jnp.concatenate([pair, block], axis=1), tab)
        out.append(jnp.exp2(proj * EXP_SCALE - EXP_SHIFT).astype(BF))
    return out


def values_ones(pair):
    keep = lower_half(pair.shape)
    one = jnp.ones_like(pair)
    return jnp.where(keep, pair, one), jnp.where(keep, one, pair)


def causal_rows(first_row, rows, cols):
    return (
        lax.broadcasted_iota(jnp.int32, (rows, cols), 0) + first_row
        >= lax.broadcasted_iota(jnp.int32, (rows, cols), 1)
    )


def state_pair(state, norm, parity):
    wide = jnp.broadcast_to(norm, (HEAD_DIM, norm.shape[1]))
    return jnp.concatenate([state, wide] if parity == 0 else [wide, state], axis=0)


def kv_kernel(x_ref, gain_ref, shift_ref, w_ref, b_ref, tab_ref, h_ref, qkv_ref, phik_ref, state_ref):
    width = x_ref.shape[-1]
    unit, _ = normalise(x_ref[0].astype(F32))
    low = (unit * gain_ref[...] + shift_ref[...]).astype(BF)
    h_ref[0] = low
    qkv_ref[0] = (dot(low, w_ref[...]) + b_ref[...]).astype(BF)
    tabs = (tab_ref[0], tab_ref[1])
    norms = []
    for pair in range(PAIRS):
        key = qkv_ref[0, :, width + pair * LANES : width + (pair + 1) * LANES]
        value = qkv_ref[0, :, 2 * width + pair * LANES : 2 * width + (pair + 1) * LANES]
        phi = features(key, tabs)
        ones = values_ones(value)
        full = []
        for head in range(2):
            at = (2 * pair + head) * FEATS
            phik_ref[0, :, at : at + FEATS] = phi[head]
            full.append(dot_tn(ones[head], phi[head]))
        state_ref[0, pair * LANES : pair * LANES + HEAD_DIM, :] = full[0][:HEAD_DIM]
        state_ref[0, pair * LANES + HEAD_DIM : (pair + 1) * LANES, :] = full[1][HEAD_DIM:]
        norms += [full[0][HEAD_DIM : HEAD_DIM + 1], full[1][0:1]]
    state_ref[0, STATE_ROWS : STATE_ROWS + HEADS, :] = jnp.concatenate(norms, axis=0)
    state_ref[0, STATE_ROWS + HEADS :, :] = jnp.zeros((SCAN_ROWS - STATE_ROWS - HEADS, FEATS), F32)


def local_kernel(q_ref, v_ref, phik_ref, tab_ref, phiq_ref, num_ref):
    phi = features(q_ref[0], (tab_ref[0], tab_ref[1]))
    ones = values_ones(v_ref[0])
    span = q_ref.shape[1]
    for head in range(2):
        phiq_ref[0, :, head * FEATS : (head + 1) * FEATS] = phi[head]
        for row in range(0, span, TILE):
            cols = row + TILE
            keys = phik_ref[0, :cols, head * FEATS : (head + 1) * FEATS]
            scores = dot_nt(phi[head][row : row + TILE], keys)
            scores = jnp.where(causal_rows(row, TILE, cols), scores, 0.0).astype(BF)
            num_ref[0, row : row + TILE, head * LANES : (head + 1) * LANES] = dot(scores, ones[head][:cols])


def middle_kernel(
    per, x_ref, dy_ref, num_ref, phiq_ref, state_ref, w_out_ref, b_out_ref, gain_ref, shift_ref,
    w_up_ref, b_up_ref, w_down_ref, b_down_ref,
    out_ref, hid_ref, dup_ref, h2_ref, att_ref, dy1_ref, dy1_low_ref, dnum_ref, dstate_ref, sums_ref, sum_up_ref,
):
    step = pl.program_id(0)
    width = x_ref.shape[-1]
    att_parts, den_parts = [], []
    for pair in range(PAIRS):
        nums = []
        for head in range(2):
            at = 2 * pair + head
            rows = pair * LANES + head * HEAD_DIM
            state = state_pair(
                state_ref[0, rows : rows + HEAD_DIM, :].astype(BF),
                state_ref[0, STATE_ROWS + at : STATE_ROWS + at + 1, :].astype(BF),
                head,
            )
            nums.append(
                num_ref[:, at * LANES : (at + 1) * LANES]
                + dot_nt(phiq_ref[:, at * FEATS : (at + 1) * FEATS], state)
            )
        keep = lower_half(nums[0].shape)
        den = swap_halves(jnp.where(keep, nums[1], nums[0]))
        recip = 1.0 / den
        att_parts.append(jnp.where(keep, nums[0], nums[1]) * recip)
        den_parts.append(recip)
    mixed = jnp.concatenate([part.astype(BF) for part in att_parts], axis=1)
    att_ref[...] = mixed
    middle = x_ref[...].astype(F32) + dot(mixed, w_out_ref[...]) + b_out_ref[...]
    unit, scale = normalise(middle)
    low = (unit * gain_ref[...] + shift_ref[...]).astype(BF)
    h2_ref[...] = low
    grad_out = dy_ref[...]
    hidden = w_up_ref.shape[1]
    chunk = 512
    result = middle + b_down_ref[...]
    grad_low = jnp.zeros(middle.shape, F32)

    @pl.when(step == 0)
    def _():
        sums_ref[...] = jnp.zeros_like(sums_ref)
        sum_up_ref[...] = jnp.zeros_like(sum_up_ref)

    for at in range(0, hidden, chunk):
        up = dot(low, w_up_ref[:, at : at + chunk]) + b_up_ref[:, at : at + chunk]
        square = up * up
        tanh = jnp.tanh(up * (GELU_A + GELU_A * GELU_B * square))
        half = 0.5 + 0.5 * tanh
        act = (up * half).astype(BF)
        hid_ref[:, at : at + chunk] = act
        slope = half + (0.5 * up) * (1.0 - tanh * tanh) * (GELU_A + 3.0 * GELU_A * GELU_B * square)
        result += dot(act, w_down_ref[at : at + chunk, :])
        dup = (dot_nt(grad_out, w_down_ref[at : at + chunk, :]) * slope).astype(BF)
        dup_ref[:, at : at + chunk] = dup
        grad_low += dot_nt(dup, w_up_ref[:, at : at + chunk])
        sum_up_ref[:, at : at + chunk] += jnp.sum(dup.astype(F32), axis=0, keepdims=True)
    out_ref[...] = result.astype(BF)
    wide = grad_out.astype(F32)
    grad_mid = wide + normalise_back(grad_low, unit, scale, gain_ref[...])
    dy1_ref[...] = grad_mid
    grad_mid_low = grad_mid.astype(BF)
    dy1_low_ref[...] = grad_mid_low
    for row, item in enumerate((wide, grad_mid, grad_low * unit, grad_low)):
        sums_ref[row : row + 1, :] += jnp.sum(item, axis=0, keepdims=True)
    grad_att = dot_nt(grad_mid_low, w_out_ref[...])

    @pl.when(lax.rem(step, per) == 0)
    def _():
        dstate_ref[...] = jnp.zeros_like(dstate_ref)

    for pair in range(PAIRS):
        grad = grad_att[:, pair * LANES : (pair + 1) * LANES] * den_parts[pair]
        keep = lower_half(grad.shape)
        prod = swap_halves(-(grad * att_parts[pair]))
        both = (jnp.where(keep, grad, prod).astype(BF), jnp.where(keep, prod, grad).astype(BF))
        for head in range(2):
            at = 2 * pair + head
            dnum_ref[:, at * LANES : (at + 1) * LANES] = both[head]
            full = dot_tn(both[head], phiq_ref[:, at * FEATS : (at + 1) * FEATS])
            rows = pair * LANES + head * HEAD_DIM
            main = full[:HEAD_DIM] if head == 0 else full[HEAD_DIM:]
            rest = full[HEAD_DIM:] if head == 0 else full[:HEAD_DIM]
            dstate_ref[0, rows : rows + HEAD_DIM, :] += main
            dstate_ref[0, STATE_ROWS + at : STATE_ROWS + at + 1, :] += jnp.sum(rest, axis=0, keepdims=True)


def score_back_kernel(
    q_ref, v_ref, phiq_ref, phik_ref, dnum_ref, state_ref, norm_ref, tab_ref, dq_ref, dphik_ref, dv_ref
):
    span = q_ref.shape[1]
    ones = values_ones(v_ref[0])
    back, dvs = [], []
    for head in range(2):
        phiq = phiq_ref[0, :, head * FEATS : (head + 1) * FEATS]
        phik = phik_ref[0, :, head * FEATS : (head + 1) * FEATS]
        dnum = dnum_ref[0, :, head * LANES : (head + 1) * LANES]
        state = state_pair(
            state_ref[0, head * HEAD_DIM : (head + 1) * HEAD_DIM, :].astype(BF),
            norm_ref[0, pl.ds(2 * pl.program_id(1) + head, 1), :].astype(BF),
            head,
        )
        grads = []
        for row in range(0, span, TILE):
            cols = row + TILE
            mine = dnum[row : row + TILE]
            grad = dot_nt(mine, ones[head][:cols])
            grad = jnp.where(causal_rows(row, TILE, cols), grad, 0.0).astype(BF)
            grad_phi = dot(mine, state) + dot(grad, phik[:cols])
            grads.append((grad_phi * phiq[row : row + TILE].astype(F32)).astype(BF))
        back.append(dot(jnp.concatenate(grads, axis=0), tab_ref[head]))
        dv = []
        for row in range(0, span, TILE):
            count = span - row
            seen = (
                lax.broadcasted_iota(jnp.int32, (TILE, count), 0)
                <= lax.broadcasted_iota(jnp.int32, (TILE, count), 1)
            )
            turned = dot_nt(ones[head][row : row + TILE], dnum[row:])
            turned = jnp.where(seen, turned, 0.0).astype(BF)
            dphik_ref[0, row : row + TILE, head * FEATS : (head + 1) * FEATS] = dot(turned, phiq[row:])
            scores = dot_nt(phik[row : row + TILE], phiq[row:])
            scores = jnp.where(seen, scores, 0.0).astype(BF)
            dv.append(dot(scores, dnum[row:]))
        dvs.append(jnp.concatenate(dv, axis=0))
    keep = lower_half(dvs[0].shape)
    dv_ref[0] = jnp.where(keep, dvs[0], dvs[1])
    dq_ref[0] = finish_back(back, q_ref[0]).astype(BF)


def finish_back(back, pair):
    keep = lower_half(back[0].shape)
    main = jnp.where(keep, back[0], back[1])
    total = swap_halves(jnp.where(keep, back[1], back[0]))
    return main * Z_SCALE - total * pair.astype(F32) * (HEAD_DIM ** (-0.5))


def final_kernel(
    x_ref, dy1_ref, qkv_ref, phik_ref, dq_ref, dphik_ref, dv_ref, later_ref, tab_ref, gain_ref, shift_ref, w_ref,
    dx_ref, dkv_ref, sums_ref, sum_qkv_ref,
):
    width = x_ref.shape[-1]
    grad = dot_nt(dq_ref[0], w_ref[:, :width])

    @pl.when(pl.program_id(0) == 0)
    def _():
        sums_ref[...] = jnp.zeros_like(sums_ref)
        sum_qkv_ref[...] = jnp.zeros_like(sum_qkv_ref)

    for pair in range(PAIRS):
        key = qkv_ref[0, :, width + pair * LANES : width + (pair + 1) * LANES]
        value = qkv_ref[0, :, 2 * width + pair * LANES : 2 * width + (pair + 1) * LANES]
        ones = values_ones(value)
        back, dvs = [], []
        for head in range(2):
            at = 2 * pair + head
            rows = pair * LANES + head * HEAD_DIM
            state = later_ref[0, rows : rows + HEAD_DIM, :].astype(BF)
            norm = later_ref[0, STATE_ROWS + at : STATE_ROWS + at + 1, :]
            high = norm.astype(BF)
            low = (norm - high.astype(F32)).astype(BF)
            rest = jnp.concatenate(
                [high.astype(F32), low.astype(F32), jnp.zeros((HEAD_DIM - 2, FEATS), F32)], axis=0
            ).astype(BF)
            full = jnp.concatenate([state, rest] if head == 0 else [rest, state], axis=0)
            phik = phik_ref[0, :, at * FEATS : (at + 1) * FEATS]
            grad_phi = dphik_ref[0, :, at * FEATS : (at + 1) * FEATS] + dot(ones[head], full)
            inner = (grad_phi * phik.astype(F32)).astype(BF)
            back.append(dot(inner, tab_ref[head]))
            dvs.append(dot_nt(phik, full))
        keep = lower_half(dvs[0].shape)
        dk = finish_back(back, key).astype(BF)
        dv = (dv_ref[0, :, pair * LANES : (pair + 1) * LANES] + jnp.where(keep, dvs[0], dvs[1])).astype(BF)
        dkv_ref[0, :, pair * LANES : (pair + 1) * LANES] = dk
        dkv_ref[0, :, width + pair * LANES : width + (pair + 1) * LANES] = dv
    dkv = dkv_ref[0]
    grad += dot_nt(dkv, w_ref[:, width:])
    unit, scale = normalise(x_ref[0].astype(F32))
    dx_ref[0] = (dy1_ref[0] + normalise_back(grad, unit, scale, gain_ref[...])).astype(BF)
    sums_ref[0:1, :] += jnp.sum(grad * unit, axis=0, keepdims=True)
    sums_ref[1:2, :] += jnp.sum(grad, axis=0, keepdims=True)
    sum_qkv_ref[:, :width] += jnp.sum(dq_ref[0].astype(F32), axis=0, keepdims=True)
    sum_qkv_ref[:, width:] += jnp.sum(dkv.astype(F32), axis=0, keepdims=True)


def whole(shape):
    return pl.BlockSpec(shape, lambda *_: (0,) * len(shape))


def params(count):
    return pltpu.CompilerParams(
        dimension_semantics=("arbitrary",) * count, vmem_limit_bytes=VMEM
    )


def cost(flops, moved, exps=0):
    return pl.CostEstimate(flops=int(flops), bytes_accessed=int(moved), transcendentals=int(exps))


def shape(dims, kind):
    return jax.ShapeDtypeStruct(dims, kind)


def flip(bit, count):
    return [(i, i ^ (1 << bit)) for i in range(count)]


def bit_of(bit):
    place = lax.axis_index("dp") * lax.axis_size("seq") + lax.axis_index("seq")
    return (place >> bit) & 1


def swap_with(values, bit):
    return lax.ppermute(values, AXES, flip(bit, lax.axis_size("dp") * lax.axis_size("seq")))


def scan_blocks(values, bits, split, reverse):
    if not bits:
        return jnp.zeros_like(values)
    bit = bits[0]
    mine = bit_of(bit)
    far = (mine == 0) if reverse else (mine == 1)
    if split:
        half = values.shape[0] // 2
        got = swap_with(lax.dynamic_slice_in_dim(values, (1 - mine) * half, half, 0), bit)
        kept = lax.dynamic_slice_in_dim(values, mine * half, half, 0)
        before = scan_blocks(kept + got, bits[1:], split - 1, reverse)
        ours = before + jnp.where(far, got, 0.0)
        theirs = swap_with(before + jnp.where(far, 0.0, kept), bit)
        return jnp.concatenate(
            [jnp.where(mine == 0, ours, theirs), jnp.where(mine == 0, theirs, ours)], axis=0
        )
    got = swap_with(values, bit)
    part = jnp.where(far, got, 0.0)
    if len(bits) == 1:
        return part
    return part + scan_blocks(values + got, bits[1:], 0, reverse)


def shards(
    tokens, cotangent, gain_attn, shift_attn, w_qkv, b_qkv, w_out, b_out,
    gain_ffn, shift_ffn, w_up, b_up, w_down, b_down, tables, pick,
):
    seqs, span, width = tokens.shape
    hidden = w_up.shape[1]
    rows = seqs * span
    table = lax.dynamic_index_in_dim(tables, pick[0] % 2, 0, keepdims=False)
    none = jnp.zeros_like(table)
    minus = jnp.full((FEATS, LANES), -1.0, BF)
    tab_in = jnp.stack(
        [jnp.concatenate([table, none, minus], axis=1), jnp.concatenate([none, table, minus], axis=1)]
    )
    one = jnp.ones_like(table)
    tab_back = jnp.stack([jnp.concatenate([table, one], axis=1), jnp.concatenate([one, table], axis=1)])
    row = lambda a: a.reshape(1, -1)
    seq_bits = list(range(lax.axis_size("seq").bit_length() - 1))

    three = lambda d: pl.BlockSpec((1,) + d, lambda s: (s, 0, 0))
    h1, qkv, phi_k, state = pl.pallas_call(
        kv_kernel,
        grid=(seqs,),
        in_specs=[
            three((span, width)), whole((1, width)), whole((1, width)), whole((width, 3 * width)),
            whole((1, 3 * width)), whole((2, FEATS, 2 * LANES)),
        ],
        out_specs=[
            three((span, width)), three((span, 3 * width)), three((span, HEADS * FEATS)), three((SCAN_ROWS, FEATS)),
        ],
        out_shape=[
            shape((seqs, span, width), BF), shape((seqs, span, 3 * width), BF),
            shape((seqs, span, HEADS * FEATS), BF), shape((seqs, SCAN_ROWS, FEATS), F32),
        ],
        compiler_params=params(1),
        cost_estimate=cost(5e9, 12e6, 2e6),
        name="keys",
    )(tokens, row(gain_attn), row(shift_attn), w_qkv, row(b_qkv), tab_in)

    before = scan_blocks(state.reshape(seqs * SCAN_ROWS, FEATS), seq_bits, 2, False).reshape(
        seqs, SCAN_ROWS, FEATS
    )

    block = lambda w, at=0: pl.BlockSpec((1, span, w), lambda s, p: (s, 0, at + p))
    phi_q, num = pl.pallas_call(
        local_kernel,
        grid=(seqs, PAIRS),
        in_specs=[block(LANES), block(LANES, 2 * PAIRS), block(2 * FEATS), whole((2, FEATS, 2 * LANES))],
        out_specs=[block(2 * FEATS), block(2 * LANES)],
        out_shape=[shape((seqs, span, HEADS * FEATS), BF), shape((seqs, span, HEADS * LANES), F32)],
        compiler_params=params(2),
        cost_estimate=cost(8e9, 16e6, 2e6),
        name="local",
    )(qkv, qkv, phi_k, tab_in)

    per = span // TILE
    tile = lambda w: pl.BlockSpec((TILE, w), lambda t: (t, 0))
    of_seq = lambda d: pl.BlockSpec((1,) + d, lambda t: (t // per, 0, 0))
    flat = lambda a: a.reshape(rows, a.shape[-1])
    out, hid, dup, h2, att, dy1, dy1_low, dnum, dstate, sums, sum_up = pl.pallas_call(
        functools.partial(middle_kernel, per),
        grid=(seqs * per,),
        in_specs=[
            tile(width), tile(width), tile(HEADS * LANES), tile(HEADS * FEATS), of_seq((SCAN_ROWS, FEATS)),
            whole((width, width)), whole((1, width)), whole((1, width)), whole((1, width)),
            whole((width, hidden)), whole((1, hidden)), whole((hidden, width)), whole((1, width)),
        ],
        out_specs=[
            tile(width), tile(hidden), tile(hidden), tile(width), tile(width), tile(width), tile(width),
            tile(HEADS * LANES), of_seq((SCAN_ROWS, FEATS)), whole((8, width)), whole((1, hidden)),
        ],
        out_shape=[
            shape((rows, width), BF), shape((rows, hidden), BF), shape((rows, hidden), BF), shape((rows, width), BF),
            shape((rows, width), BF), shape((rows, width), F32), shape((rows, width), BF),
            shape((rows, HEADS * LANES), BF), shape((seqs, SCAN_ROWS, FEATS), F32), shape((8, width), F32),
            shape((1, hidden), F32),
        ],
        compiler_params=params(1),
        cost_estimate=cost(20e9, 40e6, 2e6),
        name="middle",
    )(
        flat(tokens), flat(cotangent), flat(num), flat(phi_q), before, w_out, row(b_out), row(gain_ffn),
        row(shift_ffn), w_up, row(b_up), w_down, row(b_down),
    )

    later = scan_blocks(dstate.reshape(seqs * SCAN_ROWS, FEATS), seq_bits, 2, True).reshape(
        seqs, SCAN_ROWS, FEATS
    )
    grad_w_down = dot_tn(hid, flat(cotangent))
    grad_w_up = dot_tn(h2, dup)
    grad_w_out = dot_tn(att, dy1_low)

    dq, dphik, dv = pl.pallas_call(
        score_back_kernel,
        grid=(seqs, PAIRS),
        in_specs=[
            block(LANES), block(LANES, 2 * PAIRS), block(2 * FEATS), block(2 * FEATS), block(2 * LANES),
            pl.BlockSpec((1, LANES, FEATS), lambda s, p: (s, p, 0)),
            pl.BlockSpec((1, HEADS, FEATS), lambda s, p: (s, STATE_ROWS // HEADS, 0)),
            whole((2, FEATS, LANES)),
        ],
        out_specs=[block(LANES), block(2 * FEATS), block(LANES)],
        out_shape=[
            shape((seqs, span, width), BF), shape((seqs, span, HEADS * FEATS), F32), shape((seqs, span, width), F32),
        ],
        compiler_params=params(2),
        cost_estimate=cost(20e9, 30e6),
        name="scores",
    )(qkv, qkv, phi_q, phi_k, dnum.reshape(seqs, span, -1), before, before, tab_back)

    dx, dkv, sums_attn, sum_qkv = pl.pallas_call(
        final_kernel,
        grid=(seqs,),
        in_specs=[
            three((span, width)), three((span, width)), three((span, 3 * width)), three((span, HEADS * FEATS)),
            three((span, width)), three((span, HEADS * FEATS)), three((span, width)), three((SCAN_ROWS, FEATS)),
            whole((2, FEATS, LANES)), whole((1, width)), whole((1, width)), whole((width, 3 * width)),
        ],
        out_specs=[three((span, width)), three((span, 2 * width)), whole((8, width)), whole((1, 3 * width))],
        out_shape=[
            shape((seqs, span, width), BF), shape((seqs, span, 2 * width), BF), shape((8, width), F32),
            shape((1, 3 * width), F32),
        ],
        compiler_params=params(1),
        cost_estimate=cost(8e9, 20e6),
        name="final",
    )(
        tokens, dy1.reshape(seqs, span, width), qkv, phi_k, dq, dphik, dv, later, tab_back, row(gain_attn),
        row(shift_attn), w_qkv,
    )
    grad_w_q = dot_tn(flat(h1), flat(dq))
    grad_w_kv = dot_tn(flat(h1), flat(dkv))
    return finish(
        out.reshape(seqs, span, width), dx, grad_w_down, grad_w_up, grad_w_out, grad_w_q, grad_w_kv,
        sums, sum_up, sums_attn, sum_qkv,
    )


def finish(out, dx, grad_w_down, grad_w_up, grad_w_out, grad_w_q, grad_w_kv, sums, sum_up, sums_attn, sum_qkv):
    total = lax.psum(
        (grad_w_down, grad_w_up, grad_w_out, grad_w_q, grad_w_kv, sums, sum_up, sums_attn, sum_qkv), AXES
    )
    grad_w_down, grad_w_up, grad_w_out, grad_w_q, grad_w_kv, sums, sum_up, sums_attn, sum_qkv = total
    return (
        out, dx, sums_attn[0], sums_attn[1], jnp.concatenate([grad_w_q, grad_w_kv], axis=1), sum_qkv[0],
        grad_w_out, sums[1], sums[2], sums[3], grad_w_up, sum_up[0], grad_w_down, sums[0],
    )


def solution(mesh):
    split = P("dp", "seq", None)
    return jax.shard_map(
        shards,
        mesh=mesh,
        in_specs=(split, split) + (P(),) * 14,
        out_specs=(split, split) + (P(),) * 12,
        check_vma=False,
    )
```

```python
import functools
import math

import jax
import jax.numpy as jnp
from jax import lax
from jax.experimental import pallas as pl
from jax.experimental.pallas import tpu as pltpu
from jax.sharding import PartitionSpec as P

HEADS = 8
HEAD_DIM = 64
FEATS = 256
PAIRS = HEADS // 2
LANES = 2 * HEAD_DIM
AXES = ("x", "z", "y", "c")
BF = jnp.bfloat16
F32 = jnp.float32
Z_SCALE = HEAD_DIM ** (-0.25)
SQ_SCALE = 0.5 * HEAD_DIM ** (-0.5) / Z_SCALE
EXP_SCALE = Z_SCALE * math.log2(math.e)
EXP_SHIFT = 0.5 * math.log2(FEATS)
STATE_ROWS = PAIRS * LANES
SCAN_ROWS = STATE_ROWS + 16
TILE = 256
GELU_A = math.sqrt(2.0 / math.pi)
GELU_B = 0.044715
VMEM = 56 * 1024 * 1024


def dot(a, b):
    return lax.dot_general(a, b, (((1,), (0,)), ((), ())), preferred_element_type=F32)


def dot_nt(a, b):
    return lax.dot_general(a, b, (((1,), (1,)), ((), ())), preferred_element_type=F32)


def dot_tn(a, b):
    return lax.dot_general(a, b, (((0,), (0,)), ((), ())), preferred_element_type=F32)


def lower_half(shape):
    return lax.broadcasted_iota(jnp.int32, shape, 1) < HEAD_DIM


def swap_halves(values):
    return pltpu.roll(values, HEAD_DIM, 1)


def normalise(values):
    center = values - jnp.mean(values, axis=-1, keepdims=True)
    spread = jnp.mean(center * center, axis=-1, keepdims=True)
    scale = lax.rsqrt(spread + 1e-05)
    return center * scale, scale


def normalise_back(grad, unit, scale, gain):
    inner = grad * gain
    first = jnp.mean(inner, axis=-1, keepdims=True)
    second = jnp.mean(inner * unit, axis=-1, keepdims=True)
    return scale * (inner - first - unit * second)


def features(pair, tabs):
    wide = pair.astype(F32)
    square = wide * wide * SQ_SCALE
    high = square.astype(BF).astype(F32)
    low = swap_halves(square - high)
    keep = lower_half(wide.shape)
    even = jnp.where(keep, high, low).astype(BF)
    odd = jnp.where(keep, low, high).astype(BF)
    out = []
    for block, tab in ((even, tabs[0]), (odd, tabs[1])):
        proj = dot_nt(jnp.concatenate([pair, block], axis=1), tab)
        out.append(jnp.exp2(proj * EXP_SCALE - EXP_SHIFT).astype(BF))
    return out


def values_ones(pair):
    keep = lower_half(pair.shape)
    one = jnp.ones_like(pair)
    return jnp.where(keep, pair, one), jnp.where(keep, one, pair)


def causal_rows(first_row, rows, cols):
    return (
        lax.broadcasted_iota(jnp.int32, (rows, cols), 0) + first_row
        >= lax.broadcasted_iota(jnp.int32, (rows, cols), 1)
    )


def state_pair(state, norm, parity):
    wide = jnp.broadcast_to(norm, (HEAD_DIM, norm.shape[1]))
    return jnp.concatenate([state, wide] if parity == 0 else [wide, state], axis=0)


def kv_kernel(x_ref, gain_ref, shift_ref, w_ref, b_ref, tab_ref, h_ref, qkv_ref, phik_ref, state_ref):
    width = x_ref.shape[-1]
    unit, _ = normalise(x_ref[0].astype(F32))
    low = (unit * gain_ref[...] + shift_ref[...]).astype(BF)
    h_ref[0] = low
    qkv_ref[0] = (dot(low, w_ref[...]) + b_ref[...]).astype(BF)
    tabs = (tab_ref[0], tab_ref[1])
    norms = []
    for pair in range(PAIRS):
        key = qkv_ref[0, :, width + pair * LANES : width + (pair + 1) * LANES]
        value = qkv_ref[0, :, 2 * width + pair * LANES : 2 * width + (pair + 1) * LANES]
        phi = features(key, tabs)
        ones = values_ones(value)
        full = []
        for head in range(2):
            at = (2 * pair + head) * FEATS
            phik_ref[0, :, at : at + FEATS] = phi[head]
            full.append(dot_tn(ones[head], phi[head]))
        state_ref[0, pair * LANES : pair * LANES + HEAD_DIM, :] = full[0][:HEAD_DIM]
        state_ref[0, pair * LANES + HEAD_DIM : (pair + 1) * LANES, :] = full[1][HEAD_DIM:]
        norms += [full[0][HEAD_DIM : HEAD_DIM + 1], full[1][0:1]]
    state_ref[0, STATE_ROWS : STATE_ROWS + HEADS, :] = jnp.concatenate(norms, axis=0)
    state_ref[0, STATE_ROWS + HEADS :, :] = jnp.zeros((SCAN_ROWS - STATE_ROWS - HEADS, FEATS), F32)


def local_kernel(q_ref, v_ref, phik_ref, tab_ref, *rest):
    phiq_ref, num_ref = rest[-2:]
    phi = features(q_ref[0], (tab_ref[0], tab_ref[1]))
    ones = values_ones(v_ref[0])
    span = q_ref.shape[1]
    for head in range(2):
        phiq_ref[0, :, head * FEATS : (head + 1) * FEATS] = phi[head]
        for row in range(0, span, TILE):
            cols = row + TILE
            keys = phik_ref[0, :cols, head * FEATS : (head + 1) * FEATS]
            scores = dot_nt(phi[head][row : row + TILE], keys)
            scores = jnp.where(causal_rows(row, TILE, cols), scores, 0.0).astype(BF)
            num_ref[0, row : row + TILE, head * LANES : (head + 1) * LANES] = dot(scores, ones[head][:cols])


def middle_kernel(
    per, x_ref, dy_ref, num_ref, phiq_ref, state_ref, w_out_ref, b_out_ref, gain_ref, shift_ref,
    w_up_ref, b_up_ref, w_down_ref, b_down_ref,
    out_ref, hid_ref, dup_ref, h2_ref, att_ref, dy1_ref, dy1_low_ref, dnum_ref, dstate_ref, sums_ref, sum_up_ref,
):
    step = pl.program_id(0)
    width = x_ref.shape[-1]
    att_parts, den_parts = [], []
    for pair in range(PAIRS):
        nums = []
        for head in range(2):
            at = 2 * pair + head
            rows = pair * LANES + head * HEAD_DIM
            state = state_pair(
                state_ref[0, rows : rows + HEAD_DIM, :].astype(BF),
                state_ref[0, STATE_ROWS + at : STATE_ROWS + at + 1, :].astype(BF),
                head,
            )
            nums.append(
                num_ref[:, at * LANES : (at + 1) * LANES]
                + dot_nt(phiq_ref[:, at * FEATS : (at + 1) * FEATS], state)
            )
        keep = lower_half(nums[0].shape)
        den = swap_halves(jnp.where(keep, nums[1], nums[0]))
        recip = 1.0 / den
        att_parts.append(jnp.where(keep, nums[0], nums[1]) * recip)
        den_parts.append(recip)
    mixed = jnp.concatenate([part.astype(BF) for part in att_parts], axis=1)
    att_ref[...] = mixed
    middle = x_ref[...].astype(F32) + dot(mixed, w_out_ref[...]) + b_out_ref[...]
    unit, scale = normalise(middle)
    low = (unit * gain_ref[...] + shift_ref[...]).astype(BF)
    h2_ref[...] = low
    grad_out = dy_ref[...]
    hidden = w_up_ref.shape[1]
    chunk = 512
    result = middle + b_down_ref[...]
    grad_low = jnp.zeros(middle.shape, F32)

    @pl.when(step == 0)
    def _():
        sums_ref[...] = jnp.zeros_like(sums_ref)
        sum_up_ref[...] = jnp.zeros_like(sum_up_ref)

    for at in range(0, hidden, chunk):
        up = dot(low, w_up_ref[:, at : at + chunk]) + b_up_ref[:, at : at + chunk]
        square = up * up
        tanh = jnp.tanh(up * (GELU_A + GELU_A * GELU_B * square))
        half = 0.5 + 0.5 * tanh
        act = (up * half).astype(BF)
        hid_ref[:, at : at + chunk] = act
        slope = half + (0.5 * up) * (1.0 - tanh * tanh) * (GELU_A + 3.0 * GELU_A * GELU_B * square)
        result += dot(act, w_down_ref[at : at + chunk, :])
        dup = (dot_nt(grad_out, w_down_ref[at : at + chunk, :]) * slope).astype(BF)
        dup_ref[:, at : at + chunk] = dup
        grad_low += dot_nt(dup, w_up_ref[:, at : at + chunk])
        sum_up_ref[:, at : at + chunk] += jnp.sum(dup.astype(F32), axis=0, keepdims=True)
    out_ref[...] = result.astype(BF)
    wide = grad_out.astype(F32)
    grad_mid = wide + normalise_back(grad_low, unit, scale, gain_ref[...])
    dy1_ref[...] = grad_mid
    grad_mid_low = grad_mid.astype(BF)
    dy1_low_ref[...] = grad_mid_low
    for row, item in enumerate((wide, grad_mid, grad_low * unit, grad_low)):
        sums_ref[row : row + 1, :] += jnp.sum(item, axis=0, keepdims=True)
    grad_att = dot_nt(grad_mid_low, w_out_ref[...])

    @pl.when(lax.rem(step, per) == 0)
    def _():
        dstate_ref[...] = jnp.zeros_like(dstate_ref)

    for pair in range(PAIRS):
        grad = grad_att[:, pair * LANES : (pair + 1) * LANES] * den_parts[pair]
        keep = lower_half(grad.shape)
        prod = swap_halves(-(grad * att_parts[pair]))
        both = (jnp.where(keep, grad, prod).astype(BF), jnp.where(keep, prod, grad).astype(BF))
        for head in range(2):
            at = 2 * pair + head
            dnum_ref[:, at * LANES : (at + 1) * LANES] = both[head]
            full = dot_tn(both[head], phiq_ref[:, at * FEATS : (at + 1) * FEATS])
            rows = pair * LANES + head * HEAD_DIM
            main = full[:HEAD_DIM] if head == 0 else full[HEAD_DIM:]
            rest = full[HEAD_DIM:] if head == 0 else full[:HEAD_DIM]
            dstate_ref[0, rows : rows + HEAD_DIM, :] += main
            dstate_ref[0, STATE_ROWS + at : STATE_ROWS + at + 1, :] += jnp.sum(rest, axis=0, keepdims=True)


def score_back_kernel(
    q_ref, v_ref, phiq_ref, phik_ref, dnum_ref, state_ref, norm_ref, tab_ref, *rest
):
    dq_ref, dphik_ref, dv_ref = rest[-3:]
    span = q_ref.shape[1]
    ones = values_ones(v_ref[0])
    back, dvs = [], []
    for head in range(2):
        phiq = phiq_ref[0, :, head * FEATS : (head + 1) * FEATS]
        phik = phik_ref[0, :, head * FEATS : (head + 1) * FEATS]
        dnum = dnum_ref[0, :, head * LANES : (head + 1) * LANES]
        state = state_pair(
            state_ref[0, head * HEAD_DIM : (head + 1) * HEAD_DIM, :].astype(BF),
            norm_ref[0, pl.ds(2 * pl.program_id(0) + head, 1), :].astype(BF),
            head,
        )
        grads = []
        for row in range(0, span, TILE):
            cols = row + TILE
            mine = dnum[row : row + TILE]
            grad = dot_nt(mine, ones[head][:cols])
            grad = jnp.where(causal_rows(row, TILE, cols), grad, 0.0).astype(BF)
            grad_phi = dot(mine, state) + dot(grad, phik[:cols])
            grads.append((grad_phi * phiq[row : row + TILE].astype(F32)).astype(BF))
        back.append(dot(jnp.concatenate(grads, axis=0), tab_ref[head]))
        dv = []
        for row in range(0, span, TILE):
            count = span - row
            seen = (
                lax.broadcasted_iota(jnp.int32, (TILE, count), 0)
                <= lax.broadcasted_iota(jnp.int32, (TILE, count), 1)
            )
            turned = dot_nt(ones[head][row : row + TILE], dnum[row:])
            turned = jnp.where(seen, turned, 0.0).astype(BF)
            dphik_ref[0, row : row + TILE, head * FEATS : (head + 1) * FEATS] = dot(turned, phiq[row:])
            scores = dot_nt(phik[row : row + TILE], phiq[row:])
            scores = jnp.where(seen, scores, 0.0).astype(BF)
            dv.append(dot(scores, dnum[row:]))
        dvs.append(jnp.concatenate(dv, axis=0))
    keep = lower_half(dvs[0].shape)
    dv_ref[0] = jnp.where(keep, dvs[0], dvs[1])
    dq_ref[0] = finish_back(back, q_ref[0]).astype(BF)


def finish_back(back, pair):
    keep = lower_half(back[0].shape)
    main = jnp.where(keep, back[0], back[1])
    total = swap_halves(jnp.where(keep, back[1], back[0]))
    return main * Z_SCALE - total * pair.astype(F32) * (HEAD_DIM ** (-0.5))


def final_kernel(
    x_ref, dy1_ref, qkv_ref, phik_ref, dq_ref, dphik_ref, dv_ref, later_ref, tab_ref, gain_ref, shift_ref, w_ref,
    dx_ref, dqkv_ref, sums_ref, sum_qkv_ref,
):
    width = x_ref.shape[-1]
    grad = dot_nt(dq_ref[0], w_ref[:, :width])

    @pl.when(pl.program_id(0) == 0)
    def _():
        sums_ref[...] = jnp.zeros_like(sums_ref)
        sum_qkv_ref[...] = jnp.zeros_like(sum_qkv_ref)

    for pair in range(PAIRS):
        key = qkv_ref[0, :, width + pair * LANES : width + (pair + 1) * LANES]
        value = qkv_ref[0, :, 2 * width + pair * LANES : 2 * width + (pair + 1) * LANES]
        ones = values_ones(value)
        back, dvs = [], []
        for head in range(2):
            at = 2 * pair + head
            rows = pair * LANES + head * HEAD_DIM
            state = later_ref[0, rows : rows + HEAD_DIM, :].astype(BF)
            norm = later_ref[0, STATE_ROWS + at : STATE_ROWS + at + 1, :]
            high = norm.astype(BF)
            low = (norm - high.astype(F32)).astype(BF)
            rest = jnp.concatenate(
                [high.astype(F32), low.astype(F32), jnp.zeros((HEAD_DIM - 2, FEATS), F32)], axis=0
            ).astype(BF)
            full = jnp.concatenate([state, rest] if head == 0 else [rest, state], axis=0)
            phik = phik_ref[0, :, at * FEATS : (at + 1) * FEATS]
            grad_phi = dphik_ref[0, :, at * FEATS : (at + 1) * FEATS] + dot(ones[head], full)
            inner = (grad_phi * phik.astype(F32)).astype(BF)
            back.append(dot(inner, tab_ref[head]))
            dvs.append(dot_nt(phik, full))
        keep = lower_half(dvs[0].shape)
        dk = finish_back(back, key).astype(BF)
        dv = (dv_ref[0, :, pair * LANES : (pair + 1) * LANES] + jnp.where(keep, dvs[0], dvs[1])).astype(BF)
        dqkv_ref[0, :, width + pair * LANES : width + (pair + 1) * LANES] = dk
        dqkv_ref[0, :, 2 * width + pair * LANES : 2 * width + (pair + 1) * LANES] = dv
    dqkv_ref[0, :, :width] = dq_ref[0]
    dkv = dqkv_ref[0, :, width:]
    grad += dot_nt(dkv, w_ref[:, width:])
    unit, scale = normalise(x_ref[0].astype(F32))
    dx_ref[0] = (dy1_ref[0] + normalise_back(grad, unit, scale, gain_ref[...])).astype(BF)
    sums_ref[0:1, :] += jnp.sum(grad * unit, axis=0, keepdims=True)
    sums_ref[1:2, :] += jnp.sum(grad, axis=0, keepdims=True)
    sum_qkv_ref[:, :width] += jnp.sum(dq_ref[0].astype(F32), axis=0, keepdims=True)
    sum_qkv_ref[:, width:] += jnp.sum(dkv.astype(F32), axis=0, keepdims=True)


def put_chunks(out_ref, values, first, row, rows):
    for chunk in range(values.shape[0] // rows):
        for strip in range(values.shape[1] // LANES):
            at = row + strip * rows
            out_ref[first + chunk, at : at + rows, :] = values[
                chunk * rows : (chunk + 1) * rows, strip * LANES : (strip + 1) * LANES
            ]


def ffn_grads_kernel(downs, ups, half_ref, hid_ref, dy_ref, h2_ref, dup_ref, att_ref, dy1_ref, out_ref):
    step = pl.program_id(0)
    chips = out_ref.shape[0]
    for at in range(downs):

        @pl.when(step == at)
        def _():
            values = dot_tn(hid_ref[...], dy_ref[...])
            put_chunks(out_ref, values, at * chips // downs, 0, values.shape[0] * downs // chips)

    base = dy_ref.shape[1] // LANES * (hid_ref.shape[1] * downs // chips)
    rows = h2_ref.shape[1] // chips
    block = dup_ref.shape[1] // LANES
    for at in range(ups):

        @pl.when(step == downs + at)
        def _():
            put_chunks(out_ref, dot_tn(h2_ref[...], dup_ref[...]), 0, base + at * block * rows, rows)

    @pl.when(step == downs + ups)
    def _():
        put_chunks(out_ref, dot_tn(att_ref[...], dy1_ref[...]), 0, base + ups * block * rows, rows)


def qkv_grads_kernel(steps, half_ref, h1_ref, dqkv_ref, out_ref):
    rows = h1_ref.shape[1] // out_ref.shape[0]
    for at in range(steps):

        @pl.when(pl.program_id(0) == at)
        def _():
            values = dot_tn(h1_ref[...], dqkv_ref[...])
            put_chunks(out_ref, values, 0, at * (dqkv_ref.shape[1] // LANES) * rows, rows)


def place_kernel(counts, rows, meta_ref, *refs):
    out_ref = refs[-1]
    total = sum(counts)
    half_rows = out_ref.shape[0] // 2
    along = refs[0].shape[1]
    for half in range(2):
        base = half_rows * (meta_ref[0] if half == 0 else 1 - meta_ref[0])
        for at in range(total):
            piece = refs[half * total + at]
            first = at < counts[0]
            col = 0 if first else refs[half * total].shape[2] // rows
            for inner in range(piece.shape[0]):
                x, y = (at, inner) if first else (inner, at - counts[0])
                row = (meta_ref[1] ^ x) * counts[1] + (meta_ref[2] ^ y)
                for last in range(along):
                    chip = row * along + (meta_ref[3] ^ last)
                    where = pl.ds(pl.multiple_of(base + chip * rows, rows), rows)
                    for strip in range(piece.shape[2] // rows):
                        out_ref[where, (col + strip) * LANES : (col + strip + 1) * LANES] = piece[
                            inner, last, strip * rows : (strip + 1) * rows, :
                        ]


def unpack_kernel(packed_ref, *out_refs):
    row = 0
    block = packed_ref.shape[0]
    for out_ref in out_refs:
        rows = out_ref.shape[0] // block
        for strip in range(out_ref.shape[1] // LANES):
            for chunk in range(block):
                out_ref[chunk * rows : (chunk + 1) * rows, strip * LANES : (strip + 1) * LANES] = packed_ref[
                    chunk, row : row + rows, :
                ]
            row += rows


def whole(shape):
    return pl.BlockSpec(shape, lambda *_: (0,) * len(shape))


def params(count):
    return pltpu.CompilerParams(
        dimension_semantics=("arbitrary",) * count, vmem_limit_bytes=VMEM
    )


def shape(dims, kind):
    return jax.ShapeDtypeStruct(dims, kind)


def place_of():
    place = 0
    for axis in AXES:
        place = place * lax.axis_size(axis) + lax.axis_index(axis)
    return place


def send(values, mask):
    count = math.prod(lax.axis_size(axis) for axis in AXES)
    return lax.ppermute(values, AXES, [(i, i ^ mask) for i in range(count)])


def bit_of(bit):
    return (place_of() >> bit) & 1


def swap_with(values, bit):
    return send(values, 1 << bit)


def axis_bits(axis):
    at = 0
    for other in reversed(AXES):
        size = lax.axis_size(other).bit_length() - 1
        if other == axis:
            return list(range(at, at + size))
        at += size


def value_of(bits):
    place = place_of()
    return sum(((place >> b) & 1) << i for i, b in enumerate(bits))


def mask_of(bits, value):
    return sum(((value >> i) & 1) << b for i, b in enumerate(bits))


def place_pieces(own, meta, dims):
    both = own[0] + own[1] + own[2]
    chips = len(own[0]) * len(own[1]) * own[0][0].shape[1]
    return pl.pallas_call(
        functools.partial(place_kernel, (len(own[0]), len(own[1])), dims[0] // 2 // chips),
        in_specs=[pl.BlockSpec(memory_space=pltpu.SMEM)] + [pl.BlockSpec(memory_space=pltpu.VMEM)] * len(both),
        out_specs=pl.BlockSpec(memory_space=pltpu.VMEM),
        out_shape=shape(dims, F32),
        compiler_params=pltpu.CompilerParams(vmem_limit_bytes=VMEM),
        name="place",
    )(meta, *both)


def scan_stream(values, bits, split, reverse):
    bit = bits[0]
    mine = bit_of(bit)
    far = (mine == 0) if reverse else (mine == 1)
    if split:
        half = values.shape[0] // 2
        kept = lax.dynamic_slice_in_dim(values, mine * half, half, 0)
        (got,) = yield [(lax.dynamic_slice_in_dim(values, (1 - mine) * half, half, 0), 1 << bit)]
        before = yield from scan_stream(kept + got, bits[1:], split - 1, reverse)
        ours = before + jnp.where(far, got, 0.0)
        (theirs,) = yield [(before + jnp.where(far, 0.0, kept), 1 << bit)]
        return jnp.concatenate(
            [jnp.where(mine == 0, ours, theirs), jnp.where(mine == 0, theirs, ours)], axis=0
        )
    (got,) = yield [(values, 1 << bit)]
    part = jnp.where(far, got, 0.0)
    if len(bits) == 1:
        return part
    rest = yield from scan_stream(values + got, bits[1:], 0, reverse)
    return part + rest


def chunks(parts, axis, bits, rows=None):
    mine = value_of(bits)
    out = []
    for value in range(1 << len(bits)):
        cut = []
        for part in parts:
            start, size = [0] * part.ndim, list(part.shape)
            start[axis], size[axis] = mine ^ value, 1
            if rows:
                start[-2], size[-2] = rows
            cut.append(lax.dynamic_slice(part, start, size))
        out.append(jnp.squeeze(add_all(cut), axis))
    return out


def add_all(items):
    return functools.reduce(jnp.add, items)


def to_partners(items, bits):
    return [(item, mask_of(bits, value + 1)) for value, item in enumerate(items)]


def to_all(item, bits):
    return to_partners([item] * ((1 << len(bits)) - 1), bits)


def scatter_stream(theirs, mine):
    x, y, z = axis_bits("x"), axis_bits("y"), axis_bits("z")
    (got,) = yield [(theirs, 1)]
    parts = [
        item.reshape(1 << len(x), 1 << len(y), 1 << len(z), *item.shape[1:]) for item in (mine()[0], got)
    ]
    cut = theirs.shape[1] // 2
    a, b = chunks(parts, 0, x, (0, cut)), chunks(parts, 1, y, (cut, cut))
    got = yield to_partners(a[1:], x) + to_partners(b[1:], y)
    a = chunks(a[:1] + got[: len(a) - 1], 0, y)
    b = chunks(b[:1] + got[-(len(b) - 1) :], 0, x)
    got = yield to_partners(a[1:], y) + to_partners(b[1:], x)
    parts = [a[:1] + got[: len(a) - 1], b[:1] + got[-(len(b) - 1) :]]
    both = jnp.concatenate([add_all(part) for part in parts], axis=1)
    both = chunks([both], 0, z)
    got = yield to_partners(both[1:], z)
    return add_all(both[:1] + got)


def bucket_stream(theirs, mine):
    x, y, z = axis_bits("x"), axis_bits("y"), axis_bits("z")
    chunk = yield from scatter_stream(theirs, mine)
    got = yield to_all(chunk, z)
    cut = chunk.shape[0] // 2
    a, b = [jnp.stack([item[at : at + cut] for item in [chunk] + got]) for at in (0, cut)]
    got = yield to_all(a, y) + to_all(b, x)
    count = (1 << len(y)) - 1
    a, b = jnp.stack([a] + got[:count]), jnp.stack([b] + got[count:])
    got = yield to_all(a, x) + to_all(b, y)
    count = (1 << len(x)) - 1
    a, b = [a] + got[:count], [b] + got[count:]
    got = yield [(item, 1) for item in a + b]
    return a, b, got


def small_stream(values, bits):
    for bit in bits:
        (got,) = yield [(values, 1 << bit)]
        values = values + got
    return values


class Stream:
    def __init__(self, chain):
        self.chain, self.value, self.flying = chain, None, None
        self.pending = next(chain)

    def feed(self, got):
        self.flying = None
        try:
            self.pending = self.chain.send(got)
        except StopIteration as end:
            self.pending, self.value = None, end.value


def phase(start=(), wait=(), work=None, inputs=()):
    ready = [[item for item, _ in stream.pending] for stream in start]
    ready, inputs = lax.optimization_barrier((ready, tuple(inputs)))
    for stream, items in zip(start, ready):
        stream.flying = [send(item, mask) for item, (_, mask) in zip(items, stream.pending)]
    done = tuple(work(*inputs)) if work else ()
    got, done = lax.optimization_barrier(([stream.flying for stream in wait], done))
    for stream, items in zip(wait, got):
        stream.feed(list(items))
    return done


def of_stages(stream, wait_too=()):
    while stream.pending is not None:
        phase([stream], [stream])
    return stream.value


def ffn_grads(half, chips, hid, dy, h2, dup, att, dy1):
    rows, width = dy.shape
    hidden = hid.shape[1]
    downs, ups = hidden // 2 // width, hidden // width
    packed = (hidden // 2 * width + width // 2 * hidden + width // 2 * width) // chips // LANES
    item = lambda w, index: pl.BlockSpec((rows, w), lambda j, h: (0, index(j, h[0])))
    return pl.pallas_call(
        functools.partial(ffn_grads_kernel, downs, ups),
        grid_spec=pltpu.PrefetchScalarGridSpec(
            num_scalar_prefetch=1,
            grid=(downs + ups + 1,),
            in_specs=[
                item(width, lambda j, h: h * downs + jnp.minimum(j, downs - 1)),
                item(width, lambda j, h: 0),
                item(width // 2, lambda j, h: h),
                item(width, lambda j, h: jnp.clip(j - downs, 0, ups - 1)),
                item(width // 2, lambda j, h: h),
                item(width, lambda j, h: 0),
            ],
            out_specs=pl.BlockSpec((chips, packed, LANES), lambda j, h: (0, 0, 0)),
        ),
        out_shape=shape((chips, packed, LANES), F32),
        compiler_params=params(1),
        name="ffn_grads",
    )(half.astype(jnp.int32).reshape(1), hid, dy, h2, dup, att, dy1)


def qkv_grads(half, chips, h1, dqkv):
    rows, width = h1.shape
    steps = dqkv.shape[1] // width
    packed = width // 2 * dqkv.shape[1] // chips // LANES
    return pl.pallas_call(
        functools.partial(qkv_grads_kernel, steps),
        grid_spec=pltpu.PrefetchScalarGridSpec(
            num_scalar_prefetch=1,
            grid=(steps,),
            in_specs=[
                pl.BlockSpec((rows, width // 2), lambda j, h: (0, h[0])),
                pl.BlockSpec((rows, width), lambda j, h: (0, j)),
            ],
            out_specs=pl.BlockSpec((chips, packed, LANES), lambda j, h: (0, 0, 0)),
        ),
        out_shape=shape((chips, packed, LANES), F32),
        compiler_params=params(1),
        name="qkv_grads",
    )(half.astype(jnp.int32).reshape(1), h1, dqkv)


def unpack(packed, hidden, width):
    devices = packed.shape[0]
    block = 4
    dims = [(hidden, width), (width, hidden), (width, width)]
    return pl.pallas_call(
        unpack_kernel,
        grid=(devices // block,),
        in_specs=[pl.BlockSpec((block,) + packed.shape[1:], lambda t: (t, 0, 0))],
        out_specs=[pl.BlockSpec((rows * block // devices, columns), lambda t: (t, 0)) for rows, columns in dims],
        out_shape=[shape(item, F32) for item in dims],
        compiler_params=params(1),
        name="unpack",
    )(packed)


def seq_block(seq, span, width, at=0):
    return pl.BlockSpec((1, span, width), lambda p: (seq, 0, at + p))


def run_local(seq, qkv, phi_k, tab_in, *old):
    seqs, span, _ = qkv.shape
    block = functools.partial(seq_block, seq, span)
    return pl.pallas_call(
        local_kernel,
        grid=(PAIRS,),
        in_specs=[block(LANES), block(LANES, 2 * PAIRS), block(2 * FEATS), whole((2, FEATS, 2 * LANES))]
        + [pl.BlockSpec(memory_space=pl.ANY)] * len(old),
        out_specs=[block(2 * FEATS), block(2 * LANES)],
        out_shape=[shape((seqs, span, HEADS * FEATS), BF), shape((seqs, span, HEADS * LANES), F32)],
        input_output_aliases={4 + i: i for i in range(len(old))},
        compiler_params=params(1),
        name="local",
    )(qkv, qkv, phi_k, tab_in, *old)


def run_scores(seq, qkv, phi_q, phi_k, dnum, before, tab_back, *old):
    seqs, span, third = qkv.shape
    block = functools.partial(seq_block, seq, span)
    return pl.pallas_call(
        score_back_kernel,
        grid=(PAIRS,),
        in_specs=[
            block(LANES), block(LANES, 2 * PAIRS), block(2 * FEATS), block(2 * FEATS), block(2 * LANES),
            pl.BlockSpec((1, LANES, FEATS), lambda p: (seq, p, 0)),
            pl.BlockSpec((1, HEADS, FEATS), lambda p: (seq, STATE_ROWS // HEADS, 0)),
            whole((2, FEATS, LANES)),
        ]
        + [pl.BlockSpec(memory_space=pl.ANY)] * len(old),
        out_specs=[block(LANES), block(2 * FEATS), block(LANES)],
        out_shape=[
            shape((seqs, span, third // 3), BF), shape((seqs, span, HEADS * FEATS), F32),
            shape((seqs, span, third // 3), F32),
        ],
        input_output_aliases={8 + i: i for i in range(len(old))},
        compiler_params=params(1),
        name="scores",
    )(qkv, qkv, phi_q, phi_k, dnum, before, before, tab_back, *old)


def shards(
    tokens, cotangent, gain_attn, shift_attn, w_qkv, b_qkv, w_out, b_out,
    gain_ffn, shift_ffn, w_up, b_up, w_down, b_down, tables, pick,
):
    seqs, span, width = tokens.shape
    hidden = w_up.shape[1]
    rows = seqs * span
    table = lax.dynamic_index_in_dim(tables, pick[0] % 2, 0, keepdims=False)
    none = jnp.zeros_like(table)
    minus = jnp.full((FEATS, LANES), -1.0, BF)
    tab_in = jnp.stack(
        [jnp.concatenate([table, none, minus], axis=1), jnp.concatenate([none, table, minus], axis=1)]
    )
    one = jnp.ones_like(table)
    tab_back = jnp.stack([jnp.concatenate([table, one], axis=1), jnp.concatenate([one, table], axis=1)])
    row = lambda a: a.reshape(1, -1)
    seq_bits = axis_bits("c") + axis_bits("y") + axis_bits("z")

    three = lambda d: pl.BlockSpec((1,) + d, lambda s: (s, 0, 0))
    h1, qkv, phi_k, state = pl.pallas_call(
        kv_kernel,
        grid=(seqs,),
        in_specs=[
            three((span, width)), whole((1, width)), whole((1, width)), whole((width, 3 * width)),
            whole((1, 3 * width)), whole((2, FEATS, 2 * LANES)),
        ],
        out_specs=[
            three((span, width)), three((span, 3 * width)), three((span, HEADS * FEATS)), three((SCAN_ROWS, FEATS)),
        ],
        out_shape=[
            shape((seqs, span, width), BF), shape((seqs, span, 3 * width), BF),
            shape((seqs, span, HEADS * FEATS), BF), shape((seqs, SCAN_ROWS, FEATS), F32),
        ],
        compiler_params=params(1),
        name="keys",
    )(tokens, row(gain_attn), row(shift_attn), w_qkv, row(b_qkv), tab_in)

    scan = Stream(scan_stream(state.reshape(seqs * SCAN_ROWS, FEATS), seq_bits, 2, False))
    phase([scan], [scan])
    local = None
    for seq in range(seqs):
        work = lambda qkv, phi_k, *old: run_local(seq, qkv, phi_k, tab_in, *old)
        local = phase([scan], [scan], work, (qkv, phi_k) + tuple(local or ()))
    phi_q, num = local
    before = of_stages(scan).reshape(seqs, SCAN_ROWS, FEATS)

    per = span // TILE
    tile = lambda w: pl.BlockSpec((TILE, w), lambda t: (t, 0))
    of_seq = lambda d: pl.BlockSpec((1,) + d, lambda t: (t // per, 0, 0))
    flat = lambda a: a.reshape(rows, a.shape[-1])
    out, hid, dup, h2, att, dy1, dy1_low, dnum, dstate, sums, sum_up = pl.pallas_call(
        functools.partial(middle_kernel, per),
        grid=(seqs * per,),
        in_specs=[
            tile(width), tile(width), tile(HEADS * LANES), tile(HEADS * FEATS), of_seq((SCAN_ROWS, FEATS)),
            whole((width, width)), whole((1, width)), whole((1, width)), whole((1, width)),
            whole((width, hidden)), whole((1, hidden)), whole((hidden, width)), whole((1, width)),
        ],
        out_specs=[
            tile(width), tile(hidden), tile(hidden), tile(width), tile(width), tile(width), tile(width),
            tile(HEADS * LANES), of_seq((SCAN_ROWS, FEATS)), whole((8, width)), whole((1, hidden)),
        ],
        out_shape=[
            shape((rows, width), BF), shape((rows, hidden), BF), shape((rows, hidden), BF), shape((rows, width), BF),
            shape((rows, width), BF), shape((rows, width), F32), shape((rows, width), BF),
            shape((rows, HEADS * LANES), BF), shape((seqs, SCAN_ROWS, FEATS), F32), shape((8, width), F32),
            shape((1, hidden), F32),
        ],
        compiler_params=params(1),
        name="middle",
    )(
        flat(tokens), flat(cotangent), flat(num), flat(phi_q), before, w_out, row(b_out), row(gain_ffn),
        row(shift_ffn), w_up, row(b_up), w_down, row(b_down),
    )

    chips = lax.axis_size("x") * lax.axis_size("y") * lax.axis_size("z")
    fits = width % (16 * chips) == 0
    core = bit_of(0)
    meta = jnp.stack([lax.axis_index(axis) for axis in ("c", "x", "y", "z")]).astype(jnp.int32)
    scan = Stream(scan_stream(dstate.reshape(seqs * SCAN_ROWS, FEATS), seq_bits, 2, True))
    run_back = lambda seq: lambda dnum, *old: run_scores(
        seq, qkv, phi_q, phi_k, dnum.reshape(seqs, span, -1), before, tab_back, *old
    )
    if fits:
        kept = []
        args = (flat(cotangent), h2, dup, att, dy1_low)
        some = lambda half: lambda hid: (ffn_grads(half, chips, hid, *args),)
        (theirs,) = phase([scan], [scan], some(1 - core), (hid,))
        ffn = Stream(scatter_stream(theirs, lambda: kept))
        kept += phase([ffn, scan], [scan], some(core), (hid,))
        phase((), [ffn])
        old = phase([ffn, scan], [scan], run_back(0), (dnum,))
        old = phase([scan], [scan, ffn], run_back(1), (dnum,) + tuple(old))
        phase([ffn, scan], [ffn, scan])
        phase([ffn, scan], [scan])
        later = scan.value
    else:
        old = phase([scan], [scan], run_back(0), (dnum,))
        old = phase([scan], [scan], run_back(1), (dnum,) + tuple(old))
        later = of_stages(scan)
    dq, dphik, dv = old
    later = later.reshape(seqs, SCAN_ROWS, FEATS)

    run_final = lambda dphik: pl.pallas_call(
        final_kernel,
        grid=(seqs,),
        in_specs=[
            three((span, width)), three((span, width)), three((span, 3 * width)), three((span, HEADS * FEATS)),
            three((span, width)), three((span, HEADS * FEATS)), three((span, width)), three((SCAN_ROWS, FEATS)),
            whole((2, FEATS, LANES)), whole((1, width)), whole((1, width)), whole((width, 3 * width)),
        ],
        out_specs=[three((span, width)), three((span, 3 * width)), whole((8, width)), whole((1, 3 * width))],
        out_shape=[
            shape((seqs, span, width), BF), shape((seqs, span, 3 * width), BF), shape((8, width), F32),
            shape((1, 3 * width), F32),
        ],
        compiler_params=params(1),
        name="final",
    )(
        tokens, dy1.reshape(seqs, span, width), qkv, phi_k, dq, dphik, dv, later, tab_back, row(gain_attn),
        row(shift_attn), w_qkv,
    )
    join = lambda sums_attn, sum_qkv: jnp.concatenate(
        [sums[:4].reshape(-1), sum_up.reshape(-1), sums_attn[:2].reshape(-1), sum_qkv.reshape(-1)]
    ).reshape(-1, LANES)
    all_bits = [bit for axis in reversed(AXES) for bit in axis_bits(axis)]
    if fits:
        dx, dqkv, sums_attn, sum_qkv = phase((), [ffn], run_final, (dphik,))
        chunk = ffn.value
        packed = lax.all_gather(chunk, ("c", "x", "y", "z"))
        wide = flat(dqkv)
        some = lambda half: lambda wide: (qkv_grads(half, chips, flat(h1), wide),)
        (theirs,) = some(1 - core)(wide)
        more = []
        qkv_sum = Stream(bucket_stream(theirs, lambda: more))
        small = Stream(small_stream(join(sums_attn, sum_qkv), all_bits))
        more += phase([qkv_sum, small], [small], some(core), (wide,))
        phase((), [qkv_sum])
        while qkv_sum.pending is not None or small.pending is not None:
            both = [item for item in (qkv_sum, small) if item.pending is not None]
            phase(both, both)
        grad_w_qkv = place_pieces(qkv_sum.value, meta, (width, 3 * width))
        small = small.value
        grad_w_down, grad_w_up, grad_w_out = unpack(packed, hidden, width)
    else:
        dx, dqkv, sums_attn, sum_qkv = run_final(dphik)
        grad_w_down, grad_w_up, grad_w_out, grad_w_qkv = lax.psum(
            (
                dot_tn(hid, flat(cotangent)), dot_tn(h2, dup), dot_tn(att, dy1_low),
                dot_tn(flat(h1), flat(dqkv)),
            ),
            AXES,
        )
        small = of_stages(Stream(small_stream(join(sums_attn, sum_qkv), all_bits)))
    small = small.reshape(-1)
    cuts = [width * i for i in range(1, 5)]
    cuts += [cuts[-1] + hidden, cuts[-1] + hidden + width, cuts[-1] + hidden + 2 * width]
    b_down_g, b_out_g, gain_f, shift_f, b_up_g, gain_a, shift_a, b_qkv_g = jnp.split(small, cuts)
    return (
        out.reshape(seqs, span, width), dx, gain_a, shift_a, grad_w_qkv, b_qkv_g,
        grad_w_out, b_out_g, gain_f, shift_f, grad_w_up, b_up_g, grad_w_down, b_down_g,
    )


def solution(mesh):
    dp, seq = mesh.shape["dp"], mesh.shape["seq"]
    cut = jax.sharding.Mesh(mesh.devices.reshape(dp, 4, seq // 8, 2), AXES)
    split = P("x", ("z", "y", "c"), None)
    return jax.shard_map(
        shards,
        mesh=cut,
        in_specs=(split, split) + (P(),) * 14,
        out_specs=(split, split) + (P(),) * 12,
        check_vma=False,
    )
```

```python
import functools
import math

import jax
import jax.numpy as jnp
from jax import lax
from jax.experimental import pallas as pl
from jax.experimental.pallas import tpu as pltpu
from jax.sharding import PartitionSpec as P

HEADS = 8
HEAD_DIM = 64
FEATS = 256
PAIRS = HEADS // 2
LANES = 2 * HEAD_DIM
AXES = ("x", "z", "y", "c")
BF = jnp.bfloat16
F32 = jnp.float32
Z_SCALE = HEAD_DIM ** (-0.25)
SQ_SCALE = 0.5 * HEAD_DIM ** (-0.5) / Z_SCALE
EXP_SCALE = Z_SCALE * math.log2(math.e)
EXP_SHIFT = 0.5 * math.log2(FEATS)
STATE_ROWS = PAIRS * LANES
SCAN_ROWS = STATE_ROWS + 32
TILE = 256
MID_TILE = 512
GELU_A = math.sqrt(2.0 / math.pi)
GELU_B = 0.044715
LIMITS = {
    "keys": 56, "local": 56, "middle": 60, "scores": 56, "final": 30, "qkv_grads": 16, "place": 16, "unpack": 16,
}


def dot(a, b):
    return lax.dot_general(a, b, (((1,), (0,)), ((), ())), preferred_element_type=F32)


def dot_nt(a, b):
    return lax.dot_general(a, b, (((1,), (1,)), ((), ())), preferred_element_type=F32)


def dot_tn(a, b):
    return lax.dot_general(a, b, (((0,), (0,)), ((), ())), preferred_element_type=F32)


def lower_half(shape):
    return lax.broadcasted_iota(jnp.int32, shape, 1) < HEAD_DIM


def swap_halves(values):
    return pltpu.roll(values, HEAD_DIM, 1)


def normalise(values):
    center = values - jnp.mean(values, axis=-1, keepdims=True)
    spread = jnp.mean(center * center, axis=-1, keepdims=True)
    scale = lax.rsqrt(spread + 1e-05)
    return center * scale, scale


def normalise_back(grad, unit, scale, gain):
    inner = grad * gain
    first = jnp.mean(inner, axis=-1, keepdims=True)
    second = jnp.mean(inner * unit, axis=-1, keepdims=True)
    return scale * (inner - first - unit * second)


def features(pair, tabs):
    wide = pair.astype(F32)
    square = wide * wide * SQ_SCALE
    high = square.astype(BF).astype(F32)
    low = swap_halves(square - high)
    keep = lower_half(wide.shape)
    even = jnp.where(keep, high, low).astype(BF)
    odd = jnp.where(keep, low, high).astype(BF)
    out = []
    for block, tab in ((even, tabs[0]), (odd, tabs[1])):
        proj = dot_nt(jnp.concatenate([pair, block], axis=1), tab)
        out.append(jnp.exp2(proj * EXP_SCALE - EXP_SHIFT).astype(BF))
    return out


def values_ones(pair):
    keep = lower_half(pair.shape)
    one = jnp.ones_like(pair)
    return jnp.where(keep, pair, one), jnp.where(keep, one, pair)


def causal_rows(first_row, rows, cols):
    return (
        lax.broadcasted_iota(jnp.int32, (rows, cols), 0) + first_row
        >= lax.broadcasted_iota(jnp.int32, (rows, cols), 1)
    )


def state_pair(state, norm, parity):
    wide = jnp.broadcast_to(norm, (HEAD_DIM, norm.shape[1]))
    return jnp.concatenate([state, wide] if parity == 0 else [wide, state], axis=0)


def kv_kernel(x_ref, gain_ref, shift_ref, w_ref, b_ref, tab_ref, h_ref, kv_ref, phik_ref, state_ref):
    width = x_ref.shape[-1]
    unit, _ = normalise(x_ref[0].astype(F32))
    low = (unit * gain_ref[...] + shift_ref[...]).astype(BF)
    h_ref[0] = low
    kv_ref[0] = (dot(low, w_ref[:, width:]) + b_ref[:, width:]).astype(BF)
    tabs = (tab_ref[0], tab_ref[1])
    norms = []
    for pair in range(PAIRS):
        key = kv_ref[0, :, pair * LANES : (pair + 1) * LANES]
        value = kv_ref[0, :, width + pair * LANES : width + (pair + 1) * LANES]
        phi = features(key, tabs)
        ones = values_ones(value)
        full = []
        for head in range(2):
            at = (2 * pair + head) * FEATS
            phik_ref[0, :, at : at + FEATS] = phi[head]
            full.append(dot_tn(ones[head], phi[head]))
        state_ref[0, pair * LANES : pair * LANES + HEAD_DIM, :] = full[0][:HEAD_DIM]
        state_ref[0, pair * LANES + HEAD_DIM : (pair + 1) * LANES, :] = full[1][HEAD_DIM:]
        norms += [full[0][HEAD_DIM : HEAD_DIM + 1], full[1][0:1]]
    state_ref[0, STATE_ROWS : STATE_ROWS + HEADS, :] = jnp.concatenate(norms, axis=0)
    state_ref[0, STATE_ROWS + HEADS :, :] = jnp.zeros((SCAN_ROWS - STATE_ROWS - HEADS, FEATS), F32)


def local_kernel(h_ref, w_ref, b_ref, v_ref, phik_ref, tab_ref, *rest):
    q_ref, phiq_ref, num_ref = rest[-3:]
    query = (dot(h_ref[0], w_ref[...]) + b_ref[...]).astype(BF)
    q_ref[0] = query
    phi = features(query, (tab_ref[0], tab_ref[1]))
    ones = values_ones(v_ref[0])
    span = h_ref.shape[1]
    for head in range(2):
        phiq_ref[0, :, head * FEATS : (head + 1) * FEATS] = phi[head]
        for row in range(0, span, TILE):
            cols = row + TILE
            keys = phik_ref[0, :cols, head * FEATS : (head + 1) * FEATS]
            scores = dot_nt(phi[head][row : row + TILE], keys)
            scores = jnp.where(causal_rows(row, TILE, cols), scores, 0.0).astype(BF)
            num_ref[0, row : row + TILE, head * LANES : (head + 1) * LANES] = dot(scores, ones[head][:cols])


def middle_kernel(
    per, chips, core_ref, x_ref, dy_ref, num_ref, phiq_ref, state_ref, w_out_ref, b_out_ref, gain_ref, shift_ref,
    w_up_ref, b_up_ref, w_down_ref, b_down_ref,
    out_ref, dy1_ref, dnum_ref, dstate_ref, sums_ref, sum_up_ref, *grads,
):
    down_ref, up_ref, wout_ref = grads[-3:]
    step = pl.program_id(0)
    width = x_ref.shape[-1]
    att_parts, den_parts = [], []
    for pair in range(PAIRS):
        nums = []
        for head in range(2):
            at = 2 * pair + head
            rows = pair * LANES + head * HEAD_DIM
            state = state_pair(
                state_ref[0, rows : rows + HEAD_DIM, :].astype(BF),
                state_ref[0, STATE_ROWS + at : STATE_ROWS + at + 1, :].astype(BF),
                head,
            )
            nums.append(
                num_ref[:, at * LANES : (at + 1) * LANES]
                + dot_nt(phiq_ref[:, at * FEATS : (at + 1) * FEATS], state)
            )
        keep = lower_half(nums[0].shape)
        den = swap_halves(jnp.where(keep, nums[1], nums[0]))
        recip = 1.0 / den
        att_parts.append(jnp.where(keep, nums[0], nums[1]) * recip)
        den_parts.append(recip)
    mixed = jnp.concatenate([part.astype(BF) for part in att_parts], axis=1)
    middle = x_ref[...].astype(F32) + dot(mixed, w_out_ref[...]) + b_out_ref[...]
    unit, scale = normalise(middle)
    low = (unit * gain_ref[...] + shift_ref[...]).astype(BF)
    grad_out = dy_ref[...]
    hidden = w_up_ref.shape[1]
    chunk = 1024
    result = middle + b_down_ref[...]
    grad_low = jnp.zeros(middle.shape, F32)

    @pl.when(step == 0)
    def _():
        sums_ref[...] = jnp.zeros_like(sums_ref)
        sum_up_ref[...] = jnp.zeros_like(sum_up_ref)

    for at in range(0, hidden, chunk):
        up = dot(low, w_up_ref[:, at : at + chunk]) + b_up_ref[:, at : at + chunk]
        square = up * up
        tanh = jnp.tanh(up * (GELU_A + GELU_A * GELU_B * square))
        half = 0.5 + 0.5 * tanh
        act = (up * half).astype(BF)
        add_to(down_ref, slice(at, at + chunk), slice(None), step, dot_tn(act, grad_out))
        slope = half + (0.5 * up) * (1.0 - tanh * tanh) * (GELU_A + 3.0 * GELU_A * GELU_B * square)
        result += dot(act, w_down_ref[at : at + chunk, :])
        dup = (dot_nt(grad_out, w_down_ref[at : at + chunk, :]) * slope).astype(BF)
        add_to(up_ref, slice(None), slice(at, at + chunk), step, dot_tn(low, dup))
        grad_low += dot_nt(dup, w_up_ref[:, at : at + chunk])
        sum_up_ref[:, at : at + chunk] += jnp.sum(dup.astype(F32), axis=0, keepdims=True)
    out_ref[...] = result.astype(BF)
    wide = grad_out.astype(F32)
    grad_mid = wide + normalise_back(grad_low, unit, scale, gain_ref[...])
    dy1_ref[...] = grad_mid
    grad_mid_low = grad_mid.astype(BF)
    add_to(wout_ref, slice(None), slice(None), step, dot_tn(mixed, grad_mid_low))
    for row, item in enumerate((wide, grad_mid, grad_low * unit, grad_low)):
        sums_ref[row : row + 1, :] += jnp.sum(item, axis=0, keepdims=True)
    grad_att = dot_nt(grad_mid_low, w_out_ref[...])

    @pl.when(lax.rem(step, per) == 0)
    def _():
        dstate_ref[...] = jnp.zeros_like(dstate_ref)

    for pair in range(PAIRS):
        grad = grad_att[:, pair * LANES : (pair + 1) * LANES] * den_parts[pair]
        keep = lower_half(grad.shape)
        prod = swap_halves(-(grad * att_parts[pair]))
        both = (jnp.where(keep, grad, prod).astype(BF), jnp.where(keep, prod, grad).astype(BF))
        for head in range(2):
            at = 2 * pair + head
            dnum_ref[:, at * LANES : (at + 1) * LANES] = both[head]
            full = dot_tn(both[head], phiq_ref[:, at * FEATS : (at + 1) * FEATS])
            rows = pair * LANES + head * HEAD_DIM
            main = full[:HEAD_DIM] if head == 0 else full[HEAD_DIM:]
            rest = full[HEAD_DIM:] if head == 0 else full[:HEAD_DIM]
            dstate_ref[0, rows : rows + HEAD_DIM, :] += main
            dstate_ref[0, STATE_ROWS + at : STATE_ROWS + at + 1, :] += jnp.sum(rest, axis=0, keepdims=True)

    if len(grads) > 3:

        @pl.when(step == pl.num_programs(0) - 1)
        def _():
            for half, packed_ref in ((1 - core_ref[0], grads[0]), (core_ref[0], grads[1])):
                pack_half(half, chips, packed_ref, down_ref, up_ref, wout_ref)


def add_to(total_ref, rows, cols, step, values):
    total_ref[rows, cols] = jnp.where(step == 0, 0.0, total_ref[rows, cols]) + values


def pack_half(half, chips, packed_ref, down_ref, up_ref, wout_ref):
    rows = down_ref.shape[0] // 2 // chips
    first = half * (down_ref.shape[0] // 2)
    for chip in range(chips):
        for strip in range(down_ref.shape[1] // LANES):
            packed_ref[chip, strip * rows : (strip + 1) * rows, :] = down_ref[
                pl.ds(pl.multiple_of(first + chip * rows, rows), rows), strip * LANES : (strip + 1) * LANES
            ]
    base = rows * (down_ref.shape[1] // LANES)
    for total_ref in (up_ref, wout_ref):
        rows = total_ref.shape[0] // chips
        strips = total_ref.shape[1] // 2 // LANES
        for strip in range(strips):
            col = pl.multiple_of((half * strips + strip) * LANES, LANES)
            for chip in range(chips):
                packed_ref[chip, base : base + rows, :] = total_ref[
                    chip * rows : (chip + 1) * rows, pl.ds(col, LANES)
                ]
            base += rows


def score_back_kernel(
    first, q_ref, v_ref, phiq_ref, phik_ref, dnum_ref, state_ref, norm_ref, tab_ref, *rest
):
    dq_ref, dphik_ref, dv_ref = rest[-3:]
    span = q_ref.shape[1]
    ones = values_ones(v_ref[0])
    back, dvs = [], []
    for head in range(2):
        phiq = phiq_ref[0, :, head * FEATS : (head + 1) * FEATS]
        phik = phik_ref[0, :, head * FEATS : (head + 1) * FEATS]
        dnum = dnum_ref[0, :, head * LANES : (head + 1) * LANES]
        state = state_pair(
            state_ref[0, head * HEAD_DIM : (head + 1) * HEAD_DIM, :].astype(BF),
            norm_ref[0, pl.ds(2 * (first + pl.program_id(0)) + head, 1), :].astype(BF),
            head,
        )
        grads = []
        for row in range(0, span, TILE):
            cols = row + TILE
            mine = dnum[row : row + TILE]
            grad = dot_nt(mine, ones[head][:cols])
            grad = jnp.where(causal_rows(row, TILE, cols), grad, 0.0).astype(BF)
            grad_phi = dot(mine, state) + dot(grad, phik[:cols])
            grads.append((grad_phi * phiq[row : row + TILE].astype(F32)).astype(BF))
        back.append(dot(jnp.concatenate(grads, axis=0), tab_ref[head]))
        dv = []
        for row in range(0, span, TILE):
            count = span - row
            seen = (
                lax.broadcasted_iota(jnp.int32, (TILE, count), 0)
                <= lax.broadcasted_iota(jnp.int32, (TILE, count), 1)
            )
            turned = dot_nt(ones[head][row : row + TILE], dnum[row:])
            turned = jnp.where(seen, turned, 0.0).astype(BF)
            dphik_ref[0, row : row + TILE, head * FEATS : (head + 1) * FEATS] = dot(turned, phiq[row:]).astype(BF)
            scores = dot_nt(phik[row : row + TILE], phiq[row:])
            scores = jnp.where(seen, scores, 0.0).astype(BF)
            dv.append(dot(scores, dnum[row:]))
        dvs.append(jnp.concatenate(dv, axis=0))
    keep = lower_half(dvs[0].shape)
    dv_ref[0] = jnp.where(keep, dvs[0], dvs[1])
    dq_ref[0] = finish_back(back, q_ref[0]).astype(BF)


def finish_back(back, pair):
    keep = lower_half(back[0].shape)
    main = jnp.where(keep, back[0], back[1])
    total = swap_halves(jnp.where(keep, back[1], back[0]))
    return main * Z_SCALE - total * pair.astype(F32) * (HEAD_DIM ** (-0.5))


def final_kernel(
    x_ref, dy1_ref, kv_ref, phik_ref, dq_ref, dphik_ref, dv_ref, later_ref, tab_ref, gain_ref, shift_ref, w_ref,
    *rest,
):
    dx_ref, dqkv_ref, sums_ref, sum_qkv_ref = rest[-4:]
    width = x_ref.shape[-1]
    grad = dot_nt(dq_ref[0], w_ref[:, :width])

    sums_ref[...] = jnp.zeros_like(sums_ref)
    for pair in range(PAIRS):
        key = kv_ref[0, :, pair * LANES : (pair + 1) * LANES]
        value = kv_ref[0, :, width + pair * LANES : width + (pair + 1) * LANES]
        ones = values_ones(value)
        back, dvs = [], []
        for head in range(2):
            at = 2 * pair + head
            rows = pair * LANES + head * HEAD_DIM
            state = later_ref[0, rows : rows + HEAD_DIM, :].astype(BF)
            norm = later_ref[0, STATE_ROWS + at : STATE_ROWS + at + 1, :]
            high = norm.astype(BF)
            low = (norm - high.astype(F32)).astype(BF)
            rest = jnp.concatenate(
                [high.astype(F32), low.astype(F32), jnp.zeros((HEAD_DIM - 2, FEATS), F32)], axis=0
            ).astype(BF)
            full = jnp.concatenate([state, rest] if head == 0 else [rest, state], axis=0)
            phik = phik_ref[0, :, at * FEATS : (at + 1) * FEATS]
            grad_phi = dphik_ref[0, :, at * FEATS : (at + 1) * FEATS].astype(F32) + dot(ones[head], full)
            inner = (grad_phi * phik.astype(F32)).astype(BF)
            back.append(dot(inner, tab_ref[head]))
            dvs.append(dot_nt(phik, full))
        keep = lower_half(dvs[0].shape)
        dk = finish_back(back, key).astype(BF)
        dv = (dv_ref[0, :, pair * LANES : (pair + 1) * LANES] + jnp.where(keep, dvs[0], dvs[1])).astype(BF)
        dqkv_ref[0, :, width + pair * LANES : width + (pair + 1) * LANES] = dk
        dqkv_ref[0, :, 2 * width + pair * LANES : 2 * width + (pair + 1) * LANES] = dv
    dqkv_ref[0, :, :width] = dq_ref[0]
    dkv = dqkv_ref[0, :, width:]
    grad += dot_nt(dkv, w_ref[:, width:])
    unit, scale = normalise(x_ref[0].astype(F32))
    dx_ref[0] = (dy1_ref[0] + normalise_back(grad, unit, scale, gain_ref[...])).astype(BF)
    sums_ref[0:1, :] = jnp.sum(grad * unit, axis=0, keepdims=True)
    sums_ref[1:2, :] = jnp.sum(grad, axis=0, keepdims=True)
    sum_qkv_ref[:, :width] = jnp.sum(dq_ref[0].astype(F32), axis=0, keepdims=True)
    sum_qkv_ref[:, width:] = jnp.sum(dkv.astype(F32), axis=0, keepdims=True)


def put_chunks(out_ref, values):
    chips = out_ref.shape[0]
    rows = values.shape[0] // chips
    for chunk in range(chips):
        for strip in range(values.shape[1] // LANES):
            out_ref[chunk, strip * rows : (strip + 1) * rows, :] = values[
                chunk * rows : (chunk + 1) * rows, strip * LANES : (strip + 1) * LANES
            ]


def qkv_grads_kernel(half_ref, h1_ref, dqkv_ref, out_ref):
    put_chunks(out_ref, dot_tn(h1_ref[...], dqkv_ref[...]))


def place_kernel(counts, rows, meta_ref, *refs):
    out_ref = refs[-1]
    total = sum(counts)
    along = refs[0].shape[1]
    for core in range(2):

        @pl.when(meta_ref[0] == core)
        def _():
            for half in range(2):
                base = out_ref.shape[1] // LANES // 2 * (half ^ core)
                for at in range(total):
                    piece = refs[half * total + at]
                    first = at < counts[0]
                    col = base if first else base + refs[half * total].shape[2] // rows
                    for inner in range(piece.shape[0]):
                        x, y = (at, inner) if first else (inner, at - counts[0])
                        row = (meta_ref[1] ^ x) * counts[1] + (meta_ref[2] ^ y)
                        for last in range(along):
                            chip = row * along + (meta_ref[3] ^ last)
                            where = pl.ds(pl.multiple_of(chip * rows, rows), rows)
                            for strip in range(piece.shape[2] // rows):
                                out_ref[where, (col + strip) * LANES : (col + strip + 1) * LANES] = piece[
                                    inner, last, strip * rows : (strip + 1) * rows, :
                                ]


def unpack_kernel(packed_ref, *out_refs):
    row = 0
    block = packed_ref.shape[0]
    for out_ref in out_refs:
        rows = out_ref.shape[0] // block
        for strip in range(out_ref.shape[1] // LANES):
            for chunk in range(block):
                out_ref[chunk * rows : (chunk + 1) * rows, strip * LANES : (strip + 1) * LANES] = packed_ref[
                    chunk, row : row + rows, :
                ]
            row += rows


def whole(shape):
    return pl.BlockSpec(shape, lambda *_: (0,) * len(shape))


def params(count, name):
    return pltpu.CompilerParams(
        dimension_semantics=("arbitrary",) * count if count else None, vmem_limit_bytes=LIMITS[name] * 1024 * 1024
    )


def shape(dims, kind):
    return jax.ShapeDtypeStruct(dims, kind)


def place_of():
    place = 0
    for axis in AXES:
        place = place * lax.axis_size(axis) + lax.axis_index(axis)
    return place


def send(values, mask):
    count = math.prod(lax.axis_size(axis) for axis in AXES)
    return lax.ppermute(values, AXES, [(i, i ^ mask) for i in range(count)])


def bit_of(bit):
    return (place_of() >> bit) & 1


def swap_with(values, bit):
    return send(values, 1 << bit)


def axis_bits(axis):
    at = 0
    for other in reversed(AXES):
        size = lax.axis_size(other).bit_length() - 1
        if other == axis:
            return list(range(at, at + size))
        at += size


def value_of(bits):
    place = place_of()
    return sum(((place >> b) & 1) << i for i, b in enumerate(bits))


def mask_of(bits, value):
    return sum(((value >> i) & 1) << b for i, b in enumerate(bits))


def place_pieces(own, meta, dims):
    both = own[0] + own[1] + own[2]
    chips = len(own[0]) * len(own[1]) * own[0][0].shape[1]
    return pl.pallas_call(
        functools.partial(place_kernel, (len(own[0]), len(own[1])), dims[0] // chips),
        in_specs=[pl.BlockSpec(memory_space=pltpu.SMEM)] + [pl.BlockSpec(memory_space=pltpu.VMEM)] * len(both),
        out_specs=pl.BlockSpec(memory_space=pltpu.VMEM),
        out_shape=shape(dims, F32),
        compiler_params=params(0, "place"),
        name="place",
    )(meta, *both)


def scan_stream(values, bits, split, reverse):
    bit = bits[0]
    mine = bit_of(bit)
    far = (mine == 0) if reverse else (mine == 1)
    if split:
        half = values.shape[0] // 2
        kept = lax.dynamic_slice_in_dim(values, mine * half, half, 0)
        (got,) = yield [(lax.dynamic_slice_in_dim(values, (1 - mine) * half, half, 0), 1 << bit)]
        before = yield from scan_stream(kept + got, bits[1:], split - 1, reverse)
        ours = before + jnp.where(far, got, 0.0)
        (theirs,) = yield [(before + jnp.where(far, 0.0, kept), 1 << bit)]
        return jnp.concatenate(
            [jnp.where(mine == 0, ours, theirs), jnp.where(mine == 0, theirs, ours)], axis=0
        )
    (got,) = yield [(values, 1 << bit)]
    part = jnp.where(far, got, 0.0)
    if len(bits) == 1:
        return part
    rest = yield from scan_stream(values + got, bits[1:], 0, reverse)
    return part + rest


def chunks(parts, axis, bits, rows=None):
    mine = value_of(bits)
    out = []
    for value in range(1 << len(bits)):
        cut = []
        for part in parts:
            start, size = [0] * part.ndim, list(part.shape)
            start[axis], size[axis] = mine ^ value, 1
            if rows:
                start[-2], size[-2] = rows
            cut.append(lax.dynamic_slice(part, start, size))
        out.append(jnp.squeeze(add_all(cut), axis))
    return out


def add_all(items):
    return functools.reduce(jnp.add, items)


def to_partners(items, bits):
    return [(item, mask_of(bits, value + 1)) for value, item in enumerate(items)]


def to_all(item, bits):
    return to_partners([item] * ((1 << len(bits)) - 1), bits)


def scatter_stream(theirs, mine):
    x, y, z = axis_bits("x"), axis_bits("y"), axis_bits("z")
    (got,) = yield [(theirs, 1)]
    parts = [mine() if callable(mine) else mine, got]
    cut = parts[0].shape[1] // 2
    parts = [item.reshape(1 << len(x), 1 << len(y), 1 << len(z), *item.shape[1:]) for item in parts]
    a, b = chunks(parts, 0, x, (0, cut)), chunks(parts, 1, y, (cut, cut))
    got = yield to_partners(a[1:], x) + to_partners(b[1:], y)
    a = chunks(a[:1] + got[: len(a) - 1], 0, y)
    b = chunks(b[:1] + got[-(len(b) - 1) :], 0, x)
    got = yield to_partners(a[1:], y) + to_partners(b[1:], x)
    parts = [a[:1] + got[: len(a) - 1], b[:1] + got[-(len(b) - 1) :]]
    both = jnp.concatenate([add_all(part) for part in parts], axis=1)
    both = chunks([both], 0, z)
    got = yield to_partners(both[1:], z)
    return add_all(both[:1] + got)


def bucket_stream(theirs, mine):
    x, y, z = axis_bits("x"), axis_bits("y"), axis_bits("z")
    chunk = yield from scatter_stream(theirs, mine)
    got = yield to_all(chunk, z)
    cut = chunk.shape[0] // 2
    a, b = [jnp.stack([item[at : at + cut] for item in [chunk] + got]) for at in (0, cut)]
    got = yield to_all(a, y) + to_all(b, x)
    count = (1 << len(y)) - 1
    a, b = jnp.stack([a] + got[:count]), jnp.stack([b] + got[count:])
    got = yield to_all(a, x) + to_all(b, y)
    count = (1 << len(x)) - 1
    a, b = [a] + got[:count], [b] + got[count:]
    got = yield [(item, 1) for item in a + b]
    return a, b, got


def small_stream(values, bits):
    for bit in bits:
        (got,) = yield [(values, 1 << bit)]
        values = values + got
    return values


class Stream:
    def __init__(self, chain):
        self.chain, self.value, self.flying = chain, None, None
        self.pending = next(chain)

    def feed(self, got):
        self.flying = None
        try:
            self.pending = self.chain.send(got)
        except StopIteration as end:
            self.pending, self.value = None, end.value


def phase(start=(), wait=(), work=None, inputs=()):
    ready = [[item for item, _ in stream.pending] for stream in start]
    ready, inputs = lax.optimization_barrier((ready, tuple(inputs)))
    for stream, items in zip(start, ready):
        stream.flying = [send(item, mask) for item, (_, mask) in zip(items, stream.pending)]
    done = tuple(work(*inputs)) if work else ()
    got, done = lax.optimization_barrier(([stream.flying for stream in wait], done))
    for stream, items in zip(wait, got):
        stream.feed(list(items))
    return done


def of_stages(stream, wait_too=()):
    while stream.pending is not None:
        phase([stream], [stream])
    return stream.value


def half_of(half):
    return half.astype(jnp.int32).reshape(1)


def qkv_grads(half, chips, h1, dqkv):
    rows, width = h1.shape
    block = 2 * LANES
    steps = dqkv.shape[1] // 2 // block
    own = width * block // chips // LANES
    return pl.pallas_call(
        qkv_grads_kernel,
        grid_spec=pltpu.PrefetchScalarGridSpec(
            num_scalar_prefetch=1,
            grid=(steps,),
            in_specs=[
                pl.BlockSpec((rows, width), lambda j, h: (0, 0)),
                pl.BlockSpec((rows, block), lambda j, h: (0, h[0] * steps + j)),
            ],
            out_specs=pl.BlockSpec((chips, own, LANES), lambda j, h: (0, j, 0)),
        ),
        out_shape=shape((chips, own * steps, LANES), F32),
        compiler_params=params(1, "qkv_grads"),
        name="qkv_grads",
    )(half_of(half), h1, dqkv)


def unpack(packed, hidden, width):
    devices = packed.shape[0]
    block = 4
    per = devices // 2 // block
    rows = width // (devices // 2) * block
    return pl.pallas_call(
        unpack_kernel,
        grid=(devices // block,),
        in_specs=[pl.BlockSpec((block,) + packed.shape[1:], lambda t: (t, 0, 0))],
        out_specs=[
            pl.BlockSpec((hidden * block // devices, width), lambda t: (t, 0)),
            pl.BlockSpec((rows, hidden // 2), lambda t: (t % per, t // per)),
            pl.BlockSpec((rows, width // 2), lambda t: (t % per, t // per)),
        ],
        out_shape=[shape((hidden, width), F32), shape((width, hidden), F32), shape((width, width), F32)],
        compiler_params=params(1, "unpack"),
        name="unpack",
    )(packed)


def seq_block(seq, span, width, at=0):
    return pl.BlockSpec((1, span, width), lambda p: (seq, 0, at + p))


def run_local(seq, h1, w_qkv, b_qkv, kv, phi_k, tab_in, *old):
    seqs, span, width = h1.shape
    block = functools.partial(seq_block, seq, span)
    return pl.pallas_call(
        local_kernel,
        grid=(PAIRS,),
        in_specs=[
            pl.BlockSpec((1, span, width), lambda p: (seq, 0, 0)), pl.BlockSpec((width, LANES), lambda p: (0, p)),
            pl.BlockSpec((1, LANES), lambda p: (0, p)), block(LANES, PAIRS), block(2 * FEATS),
            whole((2, FEATS, 2 * LANES)),
        ]
        + [pl.BlockSpec(memory_space=pl.ANY)] * len(old),
        out_specs=[block(LANES), block(2 * FEATS), block(2 * LANES)],
        out_shape=[
            shape((seqs, span, width), BF), shape((seqs, span, HEADS * FEATS), BF),
            shape((seqs, span, HEADS * LANES), F32),
        ],
        input_output_aliases={6 + i: i for i in range(len(old))},
        compiler_params=params(1, "local"),
        name="local",
    )(h1, w_qkv, b_qkv, kv, phi_k, tab_in, *old)


def run_scores(seq, first, count, q, kv, phi_q, phi_k, dnum, before, tab_back, *old):
    seqs, span, width = q.shape
    block = lambda w, at=0: seq_block(seq, span, w, at + first)
    return pl.pallas_call(
        functools.partial(score_back_kernel, first),
        grid=(count,),
        in_specs=[
            block(LANES), block(LANES, PAIRS), block(2 * FEATS), block(2 * FEATS), block(2 * LANES),
            pl.BlockSpec((1, LANES, FEATS), lambda p: (seq, first + p, 0)),
            pl.BlockSpec((1, HEADS, FEATS), lambda p: (seq, STATE_ROWS // HEADS, 0)),
            whole((2, FEATS, LANES)),
        ]
        + [pl.BlockSpec(memory_space=pl.ANY)] * len(old),
        out_specs=[block(LANES), block(2 * FEATS), block(LANES)],
        out_shape=[
            shape((seqs, span, width), BF), shape((seqs, span, HEADS * FEATS), BF),
            shape((seqs, span, width), F32),
        ],
        input_output_aliases={8 + i: i for i in range(len(old))},
        compiler_params=params(1, "scores"),
        name="scores",
    )(q, kv, phi_q, phi_k, dnum, before, before, tab_back, *old)


def run_keys(x, gain, bias, w_qkv, b_qkv, tab_in):
    seqs, span, width = x.shape
    three = lambda d: pl.BlockSpec((1,) + d, lambda s: (s, 0, 0))
    return pl.pallas_call(
        kv_kernel,
        grid=(seqs,),
        in_specs=[
            three((span, width)), whole((1, width)), whole((1, width)), whole((width, 3 * width)),
            whole((1, 3 * width)), whole((2, FEATS, 2 * LANES)),
        ],
        out_specs=[
            three((span, width)), three((span, 2 * width)), three((span, HEADS * FEATS)), three((SCAN_ROWS, FEATS)),
        ],
        out_shape=[
            shape((seqs, span, width), BF), shape((seqs, span, 2 * width), BF),
            shape((seqs, span, HEADS * FEATS), BF), shape((seqs, SCAN_ROWS, FEATS), F32),
        ],
        compiler_params=params(1, "keys"),
        name="keys",
    )(x, gain, bias, w_qkv, b_qkv, tab_in)


def run_middle(seqs, chips, core, x, dy, num, phi_q, before, w_out, b_out, gain, bias, w_up, b_up, w_down, b_down):
    rows, width = x.shape
    hidden = w_up.shape[1]
    per = rows // seqs // MID_TILE
    tile = lambda w: pl.BlockSpec((MID_TILE, w), lambda t, c: (t, 0))
    of_seq = lambda d: pl.BlockSpec((1,) + d, lambda t, c: (t // per, 0, 0))
    once = lambda d: pl.BlockSpec(d, lambda t, c: (0,) * len(d), pipeline_mode=pl.Buffered(1))
    sums = [(hidden, width), (width, hidden), (width, width)]
    packed = (hidden * width * 2 + width * width) // 2 // max(chips, 1) // LANES
    grads = [(chips, packed, LANES)] * 2 if chips else sums
    return pl.pallas_call(
        functools.partial(middle_kernel, per, chips),
        grid_spec=pltpu.PrefetchScalarGridSpec(
            num_scalar_prefetch=1,
            grid=(seqs * per,),
            in_specs=[
                tile(width), tile(width), tile(HEADS * LANES), tile(HEADS * FEATS), of_seq((SCAN_ROWS, FEATS)),
                once((width, width)), once((1, width)), once((1, width)), once((1, width)),
                once((width, hidden)), once((1, hidden)), once((hidden, width)), once((1, width)),
            ],
            out_specs=[
                tile(width), tile(width), tile(HEADS * LANES), of_seq((SCAN_ROWS, FEATS)),
                once((8, width)), once((1, hidden)),
            ]
            + [once(item) for item in grads],
            scratch_shapes=[pltpu.VMEM(item, F32) for item in sums] if chips else [],
        ),
        out_shape=[
            shape((rows, width), BF), shape((rows, width), F32), shape((rows, HEADS * LANES), BF),
            shape((seqs, SCAN_ROWS, FEATS), F32), shape((8, width), F32), shape((1, hidden), F32),
        ]
        + [shape(item, F32) for item in grads],
        compiler_params=params(1, "middle"),
        name="middle",
    )(half_of(core), x, dy, num, phi_q, before, w_out, b_out, gain, bias, w_up, b_up, w_down, b_down)


def run_final(seq, x, dy1, kv, phi_k, dq, dphik, dv, later, tab_back, gain, bias, w_qkv, *old):
    seqs, span, width = x.shape
    three = lambda d: pl.BlockSpec((1,) + d, lambda t: (seq, 0, 0))
    return pl.pallas_call(
        final_kernel,
        grid=(1,),
        in_specs=[
            three((span, width)), three((span, width)), three((span, 2 * width)), three((span, HEADS * FEATS)),
            three((span, width)), three((span, HEADS * FEATS)), three((span, width)), three((SCAN_ROWS, FEATS)),
            whole((2, FEATS, LANES)), whole((1, width)), whole((1, width)), whole((width, 3 * width)),
        ]
        + [pl.BlockSpec(memory_space=pl.ANY)] * len(old),
        out_specs=[three((span, width)), three((span, 3 * width)), whole((8, width)), whole((1, 3 * width))],
        out_shape=[
            shape((seqs, span, width), BF), shape((seqs, span, 3 * width), BF), shape((8, width), F32),
            shape((1, 3 * width), F32),
        ],
        input_output_aliases={12 + i: i for i in range(len(old))},
        compiler_params=params(1, "final"),
        name="final",
    )(x, dy1, kv, phi_k, dq, dphik, dv, later, tab_back, gain, bias, w_qkv, *old)


def shards(
    tokens, cotangent, gain_attn, shift_attn, w_qkv, b_qkv, w_out, b_out,
    gain_ffn, shift_ffn, w_up, b_up, w_down, b_down, tables, pick,
):
    seqs, span, width = tokens.shape
    hidden = w_up.shape[1]
    rows = seqs * span
    table = lax.dynamic_index_in_dim(tables, pick[0] % 2, 0, keepdims=False)
    none = jnp.zeros_like(table)
    minus = jnp.full((FEATS, LANES), -1.0, BF)
    tab_in = jnp.stack(
        [jnp.concatenate([table, none, minus], axis=1), jnp.concatenate([none, table, minus], axis=1)]
    )
    one = jnp.ones_like(table)
    tab_back = jnp.stack([jnp.concatenate([table, one], axis=1), jnp.concatenate([one, table], axis=1)])
    row = lambda a: a.reshape(1, -1)
    seq_bits = axis_bits("c") + axis_bits("y") + axis_bits("z")

    h1, kv, phi_k, state = run_keys(tokens, row(gain_attn), row(shift_attn), w_qkv, row(b_qkv), tab_in)

    scan = Stream(scan_stream(state.reshape(seqs * SCAN_ROWS, FEATS), seq_bits, len(seq_bits) - 1, False))
    phase([scan], [scan])
    local = None
    for seq in range(seqs):
        work = lambda kv, phi_k, *old: run_local(seq, h1, w_qkv, row(b_qkv), kv, phi_k, tab_in, *old)
        local = phase([scan], [scan], work, (kv, phi_k) + tuple(local or ()))
        if seq == 0:
            phase([scan], [scan])
    q, phi_q, num = local
    before = of_stages(scan).reshape(seqs, SCAN_ROWS, FEATS)

    flat = lambda a: a.reshape(rows, a.shape[-1])
    chips = lax.axis_size("x") * lax.axis_size("y") * lax.axis_size("z")
    fits = width % (16 * chips) == 0
    core = bit_of(0)
    meta = jnp.stack([lax.axis_index(axis) for axis in ("c", "x", "y", "z")]).astype(jnp.int32)
    out, dy1, dnum, dstate, sums, sum_up, *grads = run_middle(
        seqs, chips if fits else 0, core, flat(tokens), flat(cotangent), flat(num), flat(phi_q), before, w_out,
        row(b_out), row(gain_ffn), row(shift_ffn), w_up, row(b_up), w_down, row(b_down),
    )
    scan = Stream(scan_stream(dstate.reshape(seqs * SCAN_ROWS, FEATS), seq_bits, len(seq_bits) - 1, True))
    def back(seq, first, count):
        return lambda dnum, *old: run_scores(
            seq, first, count, q, kv, phi_q, phi_k, dnum.reshape(seqs, span, -1), before, tab_back, *old
        )

    def last(seq):
        return lambda dphik, *old: run_final(
            seq, tokens, dy1.reshape(seqs, span, width), kv, phi_k, dq, dphik, dv, later, tab_back,
            row(gain_attn), row(shift_attn), w_qkv, *old
        )

    half_pairs = PAIRS // 2
    if fits:
        theirs, mine = grads
        ffn = Stream(scatter_stream(theirs, mine))
        phase([scan, ffn], [scan])
        old = phase([scan], [scan, ffn], back(0, 0, half_pairs), (dnum,))
        phase([scan])
        phase([ffn], [scan])
        old = phase([scan], [scan], back(0, half_pairs, half_pairs), (dnum,) + tuple(old))
        phase([scan], [scan])
        old = phase([scan], [scan, ffn], back(1, 0, half_pairs), (dnum,) + tuple(old))
        phase([scan, ffn], [scan])
        old = phase((), [ffn], back(1, half_pairs, half_pairs), (dnum,) + tuple(old))
        later = scan.value
    else:
        old = phase([scan], [scan], back(0, 0, PAIRS), (dnum,))
        old = phase([scan], [scan], back(1, 0, PAIRS), (dnum,) + tuple(old))
        later = of_stages(scan)
    dq, dphik, dv = old
    later = later.reshape(seqs, SCAN_ROWS, FEATS)

    def join(*items):
        sums_attn, sum_qkv = items[0] + items[2], items[1] + items[3]
        return jnp.concatenate(
            [sums[:4].reshape(-1), sum_up.reshape(-1), sums_attn[:2].reshape(-1), sum_qkv.reshape(-1)]
        ).reshape(-1, LANES)

    all_bits = [bit for axis in reversed(AXES) for bit in axis_bits(axis)]
    if fits:
        some = lambda half, dqkv: qkv_grads(half, chips, flat(h1), flat(dqkv))

        def both(dphik):
            dx, dqkv, *parts = last(0)(dphik)
            dx, dqkv, *more = last(1)(dphik, dx, dqkv)
            theirs = some(1 - core, dqkv)
            return dx, dqkv, theirs, *parts, *more

        dx, dqkv, theirs, *parts = phase([ffn], [ffn], both, (dphik,))
        more = []
        qkv_sum = Stream(bucket_stream(theirs, lambda: more[0]))
        packed = lax.all_gather(ffn.value, ("c", "x", "y", "z"))
        small = Stream(small_stream(join(*parts), all_bits))
        more += phase([qkv_sum, small], [small], lambda dqkv: (some(core, dqkv),), (dqkv,))
        phase((), [qkv_sum])
        while qkv_sum.pending is not None or small.pending is not None:
            both = [item for item in (qkv_sum, small) if item.pending is not None]
            phase(both, both)
        grad_w_qkv = place_pieces(qkv_sum.value, meta, (width, 3 * width))
        small = small.value
        grad_w_down, grad_w_up, grad_w_out = unpack(packed, hidden, width)
    else:
        dx, dqkv, *parts = last(0)(dphik)
        dx, dqkv, *more = last(1)(dphik, dx, dqkv)
        grad_w_down, grad_w_up, grad_w_out, grad_w_qkv = lax.psum(
            (
                *grads, dot_tn(flat(h1), flat(dqkv)),
            ),
            AXES,
        )
        small = of_stages(Stream(small_stream(join(*parts, *more), all_bits)))
    small = small.reshape(-1)
    cuts = [width * i for i in range(1, 5)]
    cuts += [cuts[-1] + hidden, cuts[-1] + hidden + width, cuts[-1] + hidden + 2 * width]
    b_down_g, b_out_g, gain_f, shift_f, b_up_g, gain_a, shift_a, b_qkv_g = jnp.split(small, cuts)
    return (
        out.reshape(seqs, span, width), dx, gain_a, shift_a, grad_w_qkv, b_qkv_g,
        grad_w_out, b_out_g, gain_f, shift_f, grad_w_up, b_up_g, grad_w_down, b_down_g,
    )


def solution(mesh):
    dp, seq = mesh.shape["dp"], mesh.shape["seq"]
    cut = jax.sharding.Mesh(mesh.devices.reshape(dp, 4, seq // 8, 2), AXES)
    split = P("x", ("z", "y", "c"), None)
    return jax.shard_map(
        shards,
        mesh=cut,
        in_specs=(split, split) + (P(),) * 14,
        out_specs=(split, split) + (P(),) * 12,
        check_vma=False,
    )
```

```python
import functools
import math

import jax
import jax.numpy as jnp
from jax import lax
from jax.experimental import pallas as pl
from jax.experimental.pallas import tpu as pltpu
from jax.sharding import PartitionSpec as P

HEADS = 8
HEAD_DIM = 64
FEATS = 256
PAIRS = HEADS // 2
LANES = 2 * HEAD_DIM
AXES = ("x", "z", "y", "c")
BF = jnp.bfloat16
F32 = jnp.float32
Z_SCALE = HEAD_DIM ** (-0.25)
SQ_SCALE = 0.5 * HEAD_DIM ** (-0.5) / Z_SCALE
EXP_SCALE = Z_SCALE * math.log2(math.e)
EXP_SHIFT = 0.5 * math.log2(FEATS)
STATE_ROWS = PAIRS * LANES
SCAN_ROWS = STATE_ROWS + 32
TILE = 256
MID_TILE = 512
GELU_A = math.sqrt(2.0 / math.pi)
GELU_B = 0.044715
LIMITS = {
    "keys": 56, "local": 56, "middle": 60, "scores": 56, "final": 30, "qkv_grads": 16, "place": 16, "unpack": 16,
}


def dot(a, b):
    return lax.dot_general(a, b, (((1,), (0,)), ((), ())), preferred_element_type=F32)


def dot_nt(a, b):
    return lax.dot_general(a, b, (((1,), (1,)), ((), ())), preferred_element_type=F32)


def dot_tn(a, b):
    return lax.dot_general(a, b, (((0,), (0,)), ((), ())), preferred_element_type=F32)


def lower_half(shape):
    return lax.broadcasted_iota(jnp.int32, shape, 1) < HEAD_DIM


def swap_halves(values):
    return pltpu.roll(values, HEAD_DIM, 1)


def normalise(values):
    center = values - jnp.mean(values, axis=-1, keepdims=True)
    spread = jnp.mean(center * center, axis=-1, keepdims=True)
    scale = lax.rsqrt(spread + 1e-05)
    return center * scale, scale


def normalise_back(grad, unit, scale, gain):
    inner = grad * gain
    first = jnp.mean(inner, axis=-1, keepdims=True)
    second = jnp.mean(inner * unit, axis=-1, keepdims=True)
    return scale * (inner - first - unit * second)


def features(pair, tabs):
    wide = pair.astype(F32)
    square = wide * wide * SQ_SCALE
    high = square.astype(BF).astype(F32)
    low = swap_halves(square - high)
    keep = lower_half(wide.shape)
    even = jnp.where(keep, high, low).astype(BF)
    odd = jnp.where(keep, low, high).astype(BF)
    out = []
    for block, tab in ((even, tabs[0]), (odd, tabs[1])):
        proj = dot_nt(jnp.concatenate([pair, block], axis=1), tab)
        out.append(jnp.exp2(proj * EXP_SCALE - EXP_SHIFT).astype(BF))
    return out


def values_ones(pair):
    keep = lower_half(pair.shape)
    one = jnp.ones_like(pair)
    return jnp.where(keep, pair, one), jnp.where(keep, one, pair)


def causal_rows(first_row, rows, cols):
    return (
        lax.broadcasted_iota(jnp.int32, (rows, cols), 0) + first_row
        >= lax.broadcasted_iota(jnp.int32, (rows, cols), 1)
    )


def state_pair(state, norm, parity):
    wide = jnp.broadcast_to(norm, (HEAD_DIM, norm.shape[1]))
    return jnp.concatenate([state, wide] if parity == 0 else [wide, state], axis=0)


def kv_kernel(x_ref, gain_ref, shift_ref, w_ref, b_ref, tab_ref, h_ref, kv_ref, phik_ref, state_ref):
    width = x_ref.shape[-1]
    unit, _ = normalise(x_ref[0].astype(F32))
    low = (unit * gain_ref[...] + shift_ref[...]).astype(BF)
    h_ref[0] = low
    kv_ref[0] = (dot(low, w_ref[:, width:]) + b_ref[:, width:]).astype(BF)
    tabs = (tab_ref[0], tab_ref[1])
    norms = []
    for pair in range(PAIRS):
        key = kv_ref[0, :, pair * LANES : (pair + 1) * LANES]
        value = kv_ref[0, :, width + pair * LANES : width + (pair + 1) * LANES]
        phi = features(key, tabs)
        ones = values_ones(value)
        full = []
        for head in range(2):
            at = (2 * pair + head) * FEATS
            phik_ref[0, :, at : at + FEATS] = phi[head]
            full.append(dot_tn(ones[head], phi[head]))
        state_ref[0, pair * LANES : pair * LANES + HEAD_DIM, :] = full[0][:HEAD_DIM]
        state_ref[0, pair * LANES + HEAD_DIM : (pair + 1) * LANES, :] = full[1][HEAD_DIM:]
        norms += [full[0][HEAD_DIM : HEAD_DIM + 1], full[1][0:1]]
    state_ref[0, STATE_ROWS : STATE_ROWS + HEADS, :] = jnp.concatenate(norms, axis=0)
    state_ref[0, STATE_ROWS + HEADS :, :] = jnp.zeros((SCAN_ROWS - STATE_ROWS - HEADS, FEATS), F32)


def local_kernel(h_ref, w_ref, b_ref, v_ref, phik_ref, tab_ref, *rest):
    q_ref, phiq_ref, num_ref = rest[-3:]
    query = (dot(h_ref[0], w_ref[...]) + b_ref[...]).astype(BF)
    q_ref[0] = query
    phi = features(query, (tab_ref[0], tab_ref[1]))
    ones = values_ones(v_ref[0])
    span = h_ref.shape[1]
    for head in range(2):
        phiq_ref[0, :, head * FEATS : (head + 1) * FEATS] = phi[head]
        for row in range(0, span, TILE):
            cols = row + TILE
            keys = phik_ref[0, :cols, head * FEATS : (head + 1) * FEATS]
            scores = dot_nt(phi[head][row : row + TILE], keys)
            scores = jnp.where(causal_rows(row, TILE, cols), scores, 0.0).astype(BF)
            num_ref[0, row : row + TILE, head * LANES : (head + 1) * LANES] = dot(scores, ones[head][:cols])


def middle_kernel(
    per, chips, core_ref, x_ref, dy_ref, num_ref, phiq_ref, state_ref, w_out_ref, b_out_ref, gain_ref, shift_ref,
    w_up_from, b_up_ref, w_down_from, b_down_ref,
    out_ref, dy1_ref, dnum_ref, dstate_ref, sums_ref, sum_up_ref, *rest,
):
    *grads, w_up_ref, w_down_ref, w_sems = rest
    down_ref, up_ref, wout_ref = grads[2:5] if chips else grads
    loads = [
        pltpu.make_async_copy(source, place, w_sems.at[at])
        for at, (source, place) in enumerate(((w_up_from, w_up_ref), (w_down_from, w_down_ref)))
    ]

    @pl.when(pl.program_id(0) == 0)
    def _():
        for load in loads:
            load.start()

    step = pl.program_id(0)
    width = x_ref.shape[-1]
    att_parts, den_parts = [], []
    for pair in range(PAIRS):
        nums = []
        for head in range(2):
            at = 2 * pair + head
            rows = pair * LANES + head * HEAD_DIM
            state = state_pair(
                state_ref[0, rows : rows + HEAD_DIM, :].astype(BF),
                state_ref[0, STATE_ROWS + at : STATE_ROWS + at + 1, :].astype(BF),
                head,
            )
            nums.append(
                num_ref[:, at * LANES : (at + 1) * LANES]
                + dot_nt(phiq_ref[:, at * FEATS : (at + 1) * FEATS], state)
            )
        keep = lower_half(nums[0].shape)
        den = swap_halves(jnp.where(keep, nums[1], nums[0]))
        recip = 1.0 / den
        att_parts.append(jnp.where(keep, nums[0], nums[1]) * recip)
        den_parts.append(recip)
    mixed = jnp.concatenate([part.astype(BF) for part in att_parts], axis=1)
    middle = x_ref[...].astype(F32) + dot(mixed, w_out_ref[...]) + b_out_ref[...]
    unit, scale = normalise(middle)
    low = (unit * gain_ref[...] + shift_ref[...]).astype(BF)
    grad_out = dy_ref[...]
    hidden = w_up_ref.shape[1]
    chunk = 1024

    @pl.when(step == 0)
    def _():
        for load in loads:
            load.wait()

    result = middle + b_down_ref[...]
    grad_low = jnp.zeros(middle.shape, F32)

    @pl.when(step == 0)
    def _():
        sums_ref[...] = jnp.zeros_like(sums_ref)
        sum_up_ref[...] = jnp.zeros_like(sum_up_ref)

    for at in range(0, hidden, chunk):
        up = dot(low, w_up_ref[:, at : at + chunk]) + b_up_ref[:, at : at + chunk]
        square = up * up
        tanh = jnp.tanh(up * (GELU_A + GELU_A * GELU_B * square))
        half = 0.5 + 0.5 * tanh
        act = (up * half).astype(BF)
        add_to(down_ref, slice(at, at + chunk), slice(None), step, dot_tn(act, grad_out))
        slope = half + (0.5 * up) * (1.0 - tanh * tanh) * (GELU_A + 3.0 * GELU_A * GELU_B * square)
        result += dot(act, w_down_ref[at : at + chunk, :])
        dup = (dot_nt(grad_out, w_down_ref[at : at + chunk, :]) * slope).astype(BF)
        add_to(up_ref, slice(None), slice(at, at + chunk), step, dot_tn(low, dup))
        grad_low += dot_nt(dup, w_up_ref[:, at : at + chunk])
        sum_up_ref[:, at : at + chunk] += jnp.sum(dup.astype(F32), axis=0, keepdims=True)
    out_ref[...] = result.astype(BF)
    if chips:
        packed_ref, sems = grads[5:]
        behind = packed_ref.shape[2] * 2 * hidden // (2 * hidden + middle.shape[1])
        parts = [
            (half, first, count)
            for first, count in ((0, behind), (behind, packed_ref.shape[2] - behind))
            for half in range(2)
        ]
        stores = [
            pltpu.make_async_copy(
                packed_ref.at[half, :, pl.ds(first, count), :],
                grads[half].at[:, pl.ds(first, count), :],
                sems.at[at],
            )
            for at, (half, first, count) in enumerate(parts)
        ]

        @pl.when(step == pl.num_programs(0) - 1)
        def _():
            for half in range(2):
                pack_half(core_ref[0] if half else 1 - core_ref[0], chips, packed_ref.at[half], 0, down_ref, up_ref)
                stores[half].start()

    wide = grad_out.astype(F32)
    grad_mid = wide + normalise_back(grad_low, unit, scale, gain_ref[...])
    dy1_ref[...] = grad_mid
    grad_mid_low = grad_mid.astype(BF)
    add_to(wout_ref, slice(None), slice(None), step, dot_tn(mixed, grad_mid_low))
    for row, item in enumerate((wide, grad_mid, grad_low * unit, grad_low)):
        sums_ref[row : row + 1, :] += jnp.sum(item, axis=0, keepdims=True)
    grad_att = dot_nt(grad_mid_low, w_out_ref[...])

    @pl.when(lax.rem(step, per) == 0)
    def _():
        dstate_ref[...] = jnp.zeros_like(dstate_ref)

    for pair in range(PAIRS):
        grad = grad_att[:, pair * LANES : (pair + 1) * LANES] * den_parts[pair]
        keep = lower_half(grad.shape)
        prod = swap_halves(-(grad * att_parts[pair]))
        both = (jnp.where(keep, grad, prod).astype(BF), jnp.where(keep, prod, grad).astype(BF))
        for head in range(2):
            at = 2 * pair + head
            dnum_ref[:, at * LANES : (at + 1) * LANES] = both[head]
            full = dot_tn(both[head], phiq_ref[:, at * FEATS : (at + 1) * FEATS])
            rows = pair * LANES + head * HEAD_DIM
            main = full[:HEAD_DIM] if head == 0 else full[HEAD_DIM:]
            rest = full[HEAD_DIM:] if head == 0 else full[:HEAD_DIM]
            dstate_ref[0, rows : rows + HEAD_DIM, :] += main
            dstate_ref[0, STATE_ROWS + at : STATE_ROWS + at + 1, :] += jnp.sum(rest, axis=0, keepdims=True)

    if chips:

        @pl.when(step == pl.num_programs(0) - 1)
        def _():
            for half in range(2):
                pack_half(core_ref[0] if half else 1 - core_ref[0], chips, packed_ref.at[half], behind, None, wout_ref)
                stores[2 + half].start()
            for store in stores:
                store.wait()


def add_to(total_ref, rows, cols, step, values):
    total_ref[rows, cols] = jnp.where(step == 0, 0.0, total_ref[rows, cols]) + values


def pack_half(half, chips, packed_ref, base, down_ref, *wide_refs):
    if down_ref is not None:
        rows = down_ref.shape[0] // 2 // chips
        first = half * (down_ref.shape[0] // 2)
        for chip in range(chips):
            for strip in range(down_ref.shape[1] // LANES):
                packed_ref[chip, base + strip * rows : base + (strip + 1) * rows, :] = down_ref[
                    pl.ds(pl.multiple_of(first + chip * rows, rows), rows), strip * LANES : (strip + 1) * LANES
                ]
        base += rows * (down_ref.shape[1] // LANES)
    for total_ref in wide_refs:
        rows = total_ref.shape[0] // chips
        strips = total_ref.shape[1] // 2 // LANES
        for strip in range(strips):
            col = pl.multiple_of((half * strips + strip) * LANES, LANES)
            for chip in range(chips):
                packed_ref[chip, base : base + rows, :] = total_ref[
                    chip * rows : (chip + 1) * rows, pl.ds(col, LANES)
                ]
            base += rows


def score_back_kernel(
    first, q_ref, v_ref, phiq_ref, phik_ref, dnum_ref, state_ref, norm_ref, tab_ref, *rest
):
    dq_ref, dphik_ref, dv_ref = rest[-3:]
    span = q_ref.shape[1]
    ones = values_ones(v_ref[0])
    back, dvs = [], []
    for head in range(2):
        phiq = phiq_ref[0, :, head * FEATS : (head + 1) * FEATS]
        phik = phik_ref[0, :, head * FEATS : (head + 1) * FEATS]
        dnum = dnum_ref[0, :, head * LANES : (head + 1) * LANES]
        state = state_pair(
            state_ref[0, head * HEAD_DIM : (head + 1) * HEAD_DIM, :].astype(BF),
            norm_ref[0, pl.ds(2 * (first + pl.program_id(0)) + head, 1), :].astype(BF),
            head,
        )
        grads = []
        for row in range(0, span, TILE):
            cols = row + TILE
            mine = dnum[row : row + TILE]
            grad = dot_nt(mine, ones[head][:cols])
            grad = jnp.where(causal_rows(row, TILE, cols), grad, 0.0).astype(BF)
            grad_phi = dot(mine, state) + dot(grad, phik[:cols])
            grads.append((grad_phi * phiq[row : row + TILE].astype(F32)).astype(BF))
        back.append(dot(jnp.concatenate(grads, axis=0), tab_ref[head]))
        dv = []
        for row in range(0, span, TILE):
            count = span - row
            seen = (
                lax.broadcasted_iota(jnp.int32, (TILE, count), 0)
                <= lax.broadcasted_iota(jnp.int32, (TILE, count), 1)
            )
            turned = dot_nt(ones[head][row : row + TILE], dnum[row:])
            turned = jnp.where(seen, turned, 0.0).astype(BF)
            dphik_ref[0, row : row + TILE, head * FEATS : (head + 1) * FEATS] = dot(turned, phiq[row:]).astype(BF)
            scores = dot_nt(phik[row : row + TILE], phiq[row:])
            scores = jnp.where(seen, scores, 0.0).astype(BF)
            dv.append(dot(scores, dnum[row:]))
        dvs.append(jnp.concatenate(dv, axis=0))
    keep = lower_half(dvs[0].shape)
    dv_ref[0] = jnp.where(keep, dvs[0], dvs[1])
    dq_ref[0] = finish_back(back, q_ref[0]).astype(BF)


def finish_back(back, pair):
    keep = lower_half(back[0].shape)
    main = jnp.where(keep, back[0], back[1])
    total = swap_halves(jnp.where(keep, back[1], back[0]))
    return main * Z_SCALE - total * pair.astype(F32) * (HEAD_DIM ** (-0.5))


def final_kernel(
    x_ref, dy1_ref, kv_ref, phik_ref, dq_ref, dphik_ref, dv_ref, later_ref, tab_ref, gain_ref, shift_ref, w_ref,
    *rest,
):
    dx_ref, dqkv_ref, sums_ref, sum_qkv_ref = rest[-4:]
    width = x_ref.shape[-1]
    grad = dot_nt(dq_ref[0], w_ref[:, :width])

    sums_ref[...] = jnp.zeros_like(sums_ref)
    for pair in range(PAIRS):
        key = kv_ref[0, :, pair * LANES : (pair + 1) * LANES]
        value = kv_ref[0, :, width + pair * LANES : width + (pair + 1) * LANES]
        ones = values_ones(value)
        back, dvs = [], []
        for head in range(2):
            at = 2 * pair + head
            rows = pair * LANES + head * HEAD_DIM
            state = later_ref[0, rows : rows + HEAD_DIM, :].astype(BF)
            norm = later_ref[0, STATE_ROWS + at : STATE_ROWS + at + 1, :]
            high = norm.astype(BF)
            low = (norm - high.astype(F32)).astype(BF)
            rest = jnp.concatenate(
                [high.astype(F32), low.astype(F32), jnp.zeros((HEAD_DIM - 2, FEATS), F32)], axis=0
            ).astype(BF)
            full = jnp.concatenate([state, rest] if head == 0 else [rest, state], axis=0)
            phik = phik_ref[0, :, at * FEATS : (at + 1) * FEATS]
            grad_phi = dphik_ref[0, :, at * FEATS : (at + 1) * FEATS].astype(F32) + dot(ones[head], full)
            inner = (grad_phi * phik.astype(F32)).astype(BF)
            back.append(dot(inner, tab_ref[head]))
            dvs.append(dot_nt(phik, full))
        keep = lower_half(dvs[0].shape)
        dk = finish_back(back, key).astype(BF)
        dv = (dv_ref[0, :, pair * LANES : (pair + 1) * LANES] + jnp.where(keep, dvs[0], dvs[1])).astype(BF)
        dqkv_ref[0, :, width + pair * LANES : width + (pair + 1) * LANES] = dk
        dqkv_ref[0, :, 2 * width + pair * LANES : 2 * width + (pair + 1) * LANES] = dv
    dqkv_ref[0, :, :width] = dq_ref[0]
    dkv = dqkv_ref[0, :, width:]
    grad += dot_nt(dkv, w_ref[:, width:])
    unit, scale = normalise(x_ref[0].astype(F32))
    dx_ref[0] = (dy1_ref[0] + normalise_back(grad, unit, scale, gain_ref[...])).astype(BF)
    sums_ref[0:1, :] = jnp.sum(grad * unit, axis=0, keepdims=True)
    sums_ref[1:2, :] = jnp.sum(grad, axis=0, keepdims=True)
    sum_qkv_ref[:, :width] = jnp.sum(dq_ref[0].astype(F32), axis=0, keepdims=True)
    sum_qkv_ref[:, width:] = jnp.sum(dkv.astype(F32), axis=0, keepdims=True)


def put_chunks(out_ref, values):
    chips = out_ref.shape[0]
    rows = values.shape[0] // chips
    for chunk in range(chips):
        for strip in range(values.shape[1] // LANES):
            out_ref[chunk, strip * rows : (strip + 1) * rows, :] = values[
                chunk * rows : (chunk + 1) * rows, strip * LANES : (strip + 1) * LANES
            ]


def qkv_grads_kernel(half_ref, h1_ref, dqkv_ref, out_ref):
    put_chunks(out_ref, dot_tn(h1_ref[...], dqkv_ref[...]))


def place_kernel(counts, rows, meta_ref, *refs):
    out_ref = refs[-1]
    total = sum(counts)
    along = refs[0].shape[1]
    for core in range(2):

        @pl.when(meta_ref[0] == core)
        def _():
            for half in range(2):
                base = out_ref.shape[1] // LANES // 2 * (half ^ core)
                for at in range(total):
                    piece = refs[half * total + at]
                    first = at < counts[0]
                    col = base if first else base + refs[half * total].shape[2] // rows
                    for inner in range(piece.shape[0]):
                        x, y = (at, inner) if first else (inner, at - counts[0])
                        row = (meta_ref[1] ^ x) * counts[1] + (meta_ref[2] ^ y)
                        for last in range(along):
                            chip = row * along + (meta_ref[3] ^ last)
                            where = pl.ds(pl.multiple_of(chip * rows, rows), rows)
                            for strip in range(piece.shape[2] // rows):
                                out_ref[where, (col + strip) * LANES : (col + strip + 1) * LANES] = piece[
                                    inner, last, strip * rows : (strip + 1) * rows, :
                                ]


def unpack_kernel(packed_ref, *out_refs):
    row = 0
    block = packed_ref.shape[0]
    for out_ref in out_refs:
        rows = out_ref.shape[0] // block
        for strip in range(out_ref.shape[1] // LANES):
            for chunk in range(block):
                out_ref[chunk * rows : (chunk + 1) * rows, strip * LANES : (strip + 1) * LANES] = packed_ref[
                    chunk, row : row + rows, :
                ]
            row += rows


def whole(shape):
    return pl.BlockSpec(shape, lambda *_: (0,) * len(shape))


def params(count, name):
    return pltpu.CompilerParams(
        dimension_semantics=("arbitrary",) * count if count else None, vmem_limit_bytes=LIMITS[name] * 1024 * 1024
    )


def shape(dims, kind):
    return jax.ShapeDtypeStruct(dims, kind)


def place_of():
    place = 0
    for axis in AXES:
        place = place * lax.axis_size(axis) + lax.axis_index(axis)
    return place


def send(values, mask):
    count = math.prod(lax.axis_size(axis) for axis in AXES)
    return lax.ppermute(values, AXES, [(i, i ^ mask) for i in range(count)])


def bit_of(bit):
    return (place_of() >> bit) & 1


def swap_with(values, bit):
    return send(values, 1 << bit)


def axis_bits(axis):
    at = 0
    for other in reversed(AXES):
        size = lax.axis_size(other).bit_length() - 1
        if other == axis:
            return list(range(at, at + size))
        at += size


def value_of(bits):
    place = place_of()
    return sum(((place >> b) & 1) << i for i, b in enumerate(bits))


def mask_of(bits, value):
    return sum(((value >> i) & 1) << b for i, b in enumerate(bits))


def place_pieces(own, meta, dims):
    both = own[0] + own[1] + own[2]
    chips = len(own[0]) * len(own[1]) * own[0][0].shape[1]
    return pl.pallas_call(
        functools.partial(place_kernel, (len(own[0]), len(own[1])), dims[0] // chips),
        in_specs=[pl.BlockSpec(memory_space=pltpu.SMEM)] + [pl.BlockSpec(memory_space=pltpu.VMEM)] * len(both),
        out_specs=pl.BlockSpec(memory_space=pltpu.VMEM),
        out_shape=shape(dims, F32),
        compiler_params=params(0, "place"),
        name="place",
    )(meta, *both)


def scan_stream(values, bits, split, reverse):
    bit = bits[0]
    mine = bit_of(bit)
    far = (mine == 0) if reverse else (mine == 1)
    if split:
        half = values.shape[0] // 2
        kept = lax.dynamic_slice_in_dim(values, mine * half, half, 0)
        (got,) = yield [(lax.dynamic_slice_in_dim(values, (1 - mine) * half, half, 0), 1 << bit)]
        before = yield from scan_stream(kept + got, bits[1:], split - 1, reverse)
        ours = before + jnp.where(far, got, 0.0)
        (theirs,) = yield [(before + jnp.where(far, 0.0, kept), 1 << bit)]
        return jnp.concatenate(
            [jnp.where(mine == 0, ours, theirs), jnp.where(mine == 0, theirs, ours)], axis=0
        )
    (got,) = yield [(values, 1 << bit)]
    part = jnp.where(far, got, 0.0)
    if len(bits) == 1:
        return part
    rest = yield from scan_stream(values + got, bits[1:], 0, reverse)
    return part + rest


def cut_part(part, axis, at, rows):
    start, size = [0] * part.ndim, list(part.shape)
    start[axis], size[axis] = at, 1
    if rows:
        start[-2], size[-2] = rows
    return jnp.squeeze(lax.dynamic_slice(part, start, size), axis)


def chunks(parts, axis, bits, rows=None):
    mine = value_of(bits)
    own = [cut_part(part, axis, mine, rows) for part in parts]
    others = [
        add_all([cut_part(part, axis, mine ^ value, rows) for part in parts]) for value in range(1, 1 << len(bits))
    ]
    return own, others


def add_all(items):
    return functools.reduce(jnp.add, items)


def to_partners(items, bits):
    return [(item, mask_of(bits, value + 1)) for value, item in enumerate(items)]


def to_all(item, bits):
    return to_partners([item] * ((1 << len(bits)) - 1), bits)


def scatter_stream(theirs, mine):
    x, y, z = axis_bits("x"), axis_bits("y"), axis_bits("z")
    (got,) = yield [(theirs, 1)]
    parts = [mine() if callable(mine) else mine, got]
    cut = parts[0].shape[1] // 2
    parts = [item.reshape(1 << len(x), 1 << len(y), 1 << len(z), *item.shape[1:]) for item in parts]
    (a, a_out), (b, b_out) = chunks(parts, 0, x, (0, cut)), chunks(parts, 1, y, (cut, cut))
    got = yield to_partners(a_out, x) + to_partners(b_out, y)
    a, a_out = chunks(a + got[: len(a_out)], 0, y)
    b, b_out = chunks(b + got[-len(b_out) :], 0, x)
    got = yield to_partners(a_out, y) + to_partners(b_out, x)
    parts = [a + got[: len(a_out)], b + got[-len(b_out) :]]
    both = jnp.concatenate([add_all(part) for part in parts], axis=1)
    own, out = chunks([both], 0, z)
    got = yield to_partners(out, z)
    return add_all(own + got)


def bucket_stream(theirs, mine):
    x, y, z = axis_bits("x"), axis_bits("y"), axis_bits("z")
    chunk = yield from scatter_stream(theirs, mine)
    got = yield to_all(chunk, z)
    cut = chunk.shape[0] // 2
    a, b = [jnp.stack([item[at : at + cut] for item in [chunk] + got]) for at in (0, cut)]
    got = yield to_all(a, y) + to_all(b, x)
    count = (1 << len(y)) - 1
    a, b = jnp.stack([a] + got[:count]), jnp.stack([b] + got[count:])
    got = yield to_all(a, x) + to_all(b, y)
    count = (1 << len(x)) - 1
    a, b = [a] + got[:count], [b] + got[count:]
    got = yield [(item, 1) for item in a + b]
    return a, b, got


def small_stream(values, bits):
    for bit in bits:
        (got,) = yield [(values, 1 << bit)]
        values = values + got
    return values


class Stream:
    def __init__(self, chain):
        self.chain, self.value, self.flying = chain, None, None
        self.pending = next(chain)

    def feed(self, got):
        self.flying = None
        try:
            self.pending = self.chain.send(got)
        except StopIteration as end:
            self.pending, self.value = None, end.value


def phase(start=(), wait=(), work=None, inputs=()):
    ready = [[item for item, _ in stream.pending] for stream in start]
    ready, inputs = lax.optimization_barrier((ready, tuple(inputs)))
    for stream, items in zip(start, ready):
        stream.flying = [send(item, mask) for item, (_, mask) in zip(items, stream.pending)]
    done = tuple(work(*inputs)) if work else ()
    got, done = lax.optimization_barrier(([stream.flying for stream in wait], done))
    for stream, items in zip(wait, got):
        stream.feed(list(items))
    return done


def of_stages(stream, wait_too=()):
    while stream.pending is not None:
        phase([stream], [stream])
    return stream.value


def half_of(half):
    return half.astype(jnp.int32).reshape(1)


def qkv_grads(half, chips, h1, dqkv):
    rows, width = h1.shape
    block = 2 * LANES
    steps = dqkv.shape[1] // 2 // block
    own = width * block // chips // LANES
    return pl.pallas_call(
        qkv_grads_kernel,
        grid_spec=pltpu.PrefetchScalarGridSpec(
            num_scalar_prefetch=1,
            grid=(steps,),
            in_specs=[
                pl.BlockSpec((rows, width), lambda j, h: (0, 0)),
                pl.BlockSpec((rows, block), lambda j, h: (0, h[0] * steps + j)),
            ],
            out_specs=pl.BlockSpec((chips, own, LANES), lambda j, h: (0, j, 0)),
        ),
        out_shape=shape((chips, own * steps, LANES), F32),
        compiler_params=params(1, "qkv_grads"),
        name="qkv_grads",
    )(half_of(half), h1, dqkv)


def unpack(packed, hidden, width):
    devices = packed.shape[0]
    block = 4
    per = devices // 2 // block
    rows = width // (devices // 2) * block
    return pl.pallas_call(
        unpack_kernel,
        grid=(devices // block,),
        in_specs=[pl.BlockSpec((block,) + packed.shape[1:], lambda t: (t, 0, 0))],
        out_specs=[
            pl.BlockSpec((hidden * block // devices, width), lambda t: (t, 0)),
            pl.BlockSpec((rows, hidden // 2), lambda t: (t % per, t // per)),
            pl.BlockSpec((rows, width // 2), lambda t: (t % per, t // per)),
        ],
        out_shape=[shape((hidden, width), F32), shape((width, hidden), F32), shape((width, width), F32)],
        compiler_params=params(1, "unpack"),
        name="unpack",
    )(packed)


def seq_block(seq, span, width, at=0):
    return pl.BlockSpec((1, span, width), lambda p: (seq, 0, at + p))


def run_local(seq, h1, w_qkv, b_qkv, kv, phi_k, tab_in, *old):
    seqs, span, width = h1.shape
    block = functools.partial(seq_block, seq, span)
    return pl.pallas_call(
        local_kernel,
        grid=(PAIRS,),
        in_specs=[
            pl.BlockSpec((1, span, width), lambda p: (seq, 0, 0)), pl.BlockSpec((width, LANES), lambda p: (0, p)),
            pl.BlockSpec((1, LANES), lambda p: (0, p)), block(LANES, PAIRS), block(2 * FEATS),
            whole((2, FEATS, 2 * LANES)),
        ]
        + [pl.BlockSpec(memory_space=pl.ANY)] * len(old),
        out_specs=[block(LANES), block(2 * FEATS), block(2 * LANES)],
        out_shape=[
            shape((seqs, span, width), BF), shape((seqs, span, HEADS * FEATS), BF),
            shape((seqs, span, HEADS * LANES), F32),
        ],
        input_output_aliases={6 + i: i for i in range(len(old))},
        compiler_params=params(1, "local"),
        name="local",
    )(h1, w_qkv, b_qkv, kv, phi_k, tab_in, *old)


def run_scores(seq, first, count, q, kv, phi_q, phi_k, dnum, before, tab_back, *old):
    seqs, span, width = q.shape
    block = lambda w, at=0: seq_block(seq, span, w, at + first)
    return pl.pallas_call(
        functools.partial(score_back_kernel, first),
        grid=(count,),
        in_specs=[
            block(LANES), block(LANES, PAIRS), block(2 * FEATS), block(2 * FEATS), block(2 * LANES),
            pl.BlockSpec((1, LANES, FEATS), lambda p: (seq, first + p, 0)),
            pl.BlockSpec((1, HEADS, FEATS), lambda p: (seq, STATE_ROWS // HEADS, 0)),
            whole((2, FEATS, LANES)),
        ]
        + [pl.BlockSpec(memory_space=pl.ANY)] * len(old),
        out_specs=[block(LANES), block(2 * FEATS), block(LANES)],
        out_shape=[
            shape((seqs, span, width), BF), shape((seqs, span, HEADS * FEATS), BF),
            shape((seqs, span, width), F32),
        ],
        input_output_aliases={8 + i: i for i in range(len(old))},
        compiler_params=params(1, "scores"),
        name="scores",
    )(q, kv, phi_q, phi_k, dnum, before, before, tab_back, *old)


def run_keys(x, gain, bias, w_qkv, b_qkv, tab_in):
    seqs, span, width = x.shape
    three = lambda d: pl.BlockSpec((1,) + d, lambda s: (s, 0, 0))
    return pl.pallas_call(
        kv_kernel,
        grid=(seqs,),
        in_specs=[
            three((span, width)), whole((1, width)), whole((1, width)), whole((width, 3 * width)),
            whole((1, 3 * width)), whole((2, FEATS, 2 * LANES)),
        ],
        out_specs=[
            three((span, width)), three((span, 2 * width)), three((span, HEADS * FEATS)), three((SCAN_ROWS, FEATS)),
        ],
        out_shape=[
            shape((seqs, span, width), BF), shape((seqs, span, 2 * width), BF),
            shape((seqs, span, HEADS * FEATS), BF), shape((seqs, SCAN_ROWS, FEATS), F32),
        ],
        compiler_params=params(1, "keys"),
        name="keys",
    )(x, gain, bias, w_qkv, b_qkv, tab_in)


def run_middle(seqs, chips, core, x, dy, num, phi_q, before, w_out, b_out, gain, bias, w_up, b_up, w_down, b_down):
    rows, width = x.shape
    hidden = w_up.shape[1]
    per = rows // seqs // MID_TILE
    tile = lambda w: pl.BlockSpec((MID_TILE, w), lambda t, c: (t, 0))
    of_seq = lambda d: pl.BlockSpec((1,) + d, lambda t, c: (t // per, 0, 0))
    once = lambda d: pl.BlockSpec(d, lambda t, c: (0,) * len(d), pipeline_mode=pl.Buffered(1))
    sums = [(hidden, width), (width, hidden), (width, width)]
    packed = (hidden * width * 2 + width * width) // 2 // max(chips, 1) // LANES
    grads = [(chips, packed, LANES)] * 2 if chips else sums
    anywhere = pl.BlockSpec(memory_space=pl.ANY)
    scratch = [pltpu.VMEM((width, hidden), BF), pltpu.VMEM((hidden, width), BF), pltpu.SemaphoreType.DMA((2,))]
    if chips:
        scratch = [
            *(pltpu.VMEM(item, F32) for item in sums), pltpu.VMEM((2, chips, packed, LANES), F32),
            pltpu.SemaphoreType.DMA((4,)), *scratch,
        ]
    return pl.pallas_call(
        functools.partial(middle_kernel, per, chips),
        grid_spec=pltpu.PrefetchScalarGridSpec(
            num_scalar_prefetch=1,
            grid=(seqs * per,),
            in_specs=[
                tile(width), tile(width), tile(HEADS * LANES), tile(HEADS * FEATS), of_seq((SCAN_ROWS, FEATS)),
                once((width, width)), once((1, width)), once((1, width)), once((1, width)),
                anywhere, once((1, hidden)), anywhere, once((1, width)),
            ],
            out_specs=[
                tile(width), tile(width), tile(HEADS * LANES), of_seq((SCAN_ROWS, FEATS)),
                once((8, width)), once((1, hidden)),
            ]
            + [anywhere if chips else once(item) for item in grads],
            scratch_shapes=scratch,
        ),
        out_shape=[
            shape((rows, width), BF), shape((rows, width), F32), shape((rows, HEADS * LANES), BF),
            shape((seqs, SCAN_ROWS, FEATS), F32), shape((8, width), F32), shape((1, hidden), F32),
        ]
        + [shape(item, F32) for item in grads],
        compiler_params=params(1, "middle"),
        name="middle",
    )(half_of(core), x, dy, num, phi_q, before, w_out, b_out, gain, bias, w_up, b_up, w_down, b_down)


def run_final(seq, x, dy1, kv, phi_k, dq, dphik, dv, later, tab_back, gain, bias, w_qkv, *old):
    seqs, span, width = x.shape
    three = lambda d: pl.BlockSpec((1,) + d, lambda t: (seq, 0, 0))
    return pl.pallas_call(
        final_kernel,
        grid=(1,),
        in_specs=[
            three((span, width)), three((span, width)), three((span, 2 * width)), three((span, HEADS * FEATS)),
            three((span, width)), three((span, HEADS * FEATS)), three((span, width)), three((SCAN_ROWS, FEATS)),
            whole((2, FEATS, LANES)), whole((1, width)), whole((1, width)), whole((width, 3 * width)),
        ]
        + [pl.BlockSpec(memory_space=pl.ANY)] * len(old),
        out_specs=[three((span, width)), three((span, 3 * width)), whole((8, width)), whole((1, 3 * width))],
        out_shape=[
            shape((seqs, span, width), BF), shape((seqs, span, 3 * width), BF), shape((8, width), F32),
            shape((1, 3 * width), F32),
        ],
        input_output_aliases={12 + i: i for i in range(len(old))},
        compiler_params=params(1, "final"),
        name="final",
    )(x, dy1, kv, phi_k, dq, dphik, dv, later, tab_back, gain, bias, w_qkv, *old)


def shards(
    tokens, cotangent, gain_attn, shift_attn, w_qkv, b_qkv, w_out, b_out,
    gain_ffn, shift_ffn, w_up, b_up, w_down, b_down, tables, pick,
):
    seqs, span, width = tokens.shape
    hidden = w_up.shape[1]
    rows = seqs * span
    table = lax.dynamic_index_in_dim(tables, pick[0] % 2, 0, keepdims=False)
    none = jnp.zeros_like(table)
    minus = jnp.full((FEATS, LANES), -1.0, BF)
    tab_in = jnp.stack(
        [jnp.concatenate([table, none, minus], axis=1), jnp.concatenate([none, table, minus], axis=1)]
    )
    one = jnp.ones_like(table)
    tab_back = jnp.stack([jnp.concatenate([table, one], axis=1), jnp.concatenate([one, table], axis=1)])
    row = lambda a: a.reshape(1, -1)
    seq_bits = axis_bits("c") + axis_bits("y") + axis_bits("z")

    h1, kv, phi_k, state = run_keys(tokens, row(gain_attn), row(shift_attn), w_qkv, row(b_qkv), tab_in)

    scan = Stream(scan_stream(state.reshape(seqs * SCAN_ROWS, FEATS), seq_bits, len(seq_bits) - 1, False))
    phase([scan], [scan])
    local = None
    for seq in range(seqs):
        work = lambda kv, phi_k, *old: run_local(seq, h1, w_qkv, row(b_qkv), kv, phi_k, tab_in, *old)
        local = phase([scan], [scan], work, (kv, phi_k) + tuple(local or ()))
        if seq == 0:
            phase([scan], [scan])
    q, phi_q, num = local
    before = of_stages(scan).reshape(seqs, SCAN_ROWS, FEATS)

    flat = lambda a: a.reshape(rows, a.shape[-1])
    chips = lax.axis_size("x") * lax.axis_size("y") * lax.axis_size("z")
    fits = width % (16 * chips) == 0
    core = bit_of(0)
    meta = jnp.stack([lax.axis_index(axis) for axis in ("c", "x", "y", "z")]).astype(jnp.int32)
    out, dy1, dnum, dstate, sums, sum_up, *grads = run_middle(
        seqs, chips if fits else 0, core, flat(tokens), flat(cotangent), flat(num), flat(phi_q), before, w_out,
        row(b_out), row(gain_ffn), row(shift_ffn), w_up, row(b_up), w_down, row(b_down),
    )
    scan = Stream(scan_stream(dstate.reshape(seqs * SCAN_ROWS, FEATS), seq_bits, len(seq_bits) - 1, True))
    def back(seq, first, count):
        return lambda dnum, *old: run_scores(
            seq, first, count, q, kv, phi_q, phi_k, dnum.reshape(seqs, span, -1), before, tab_back, *old
        )

    def last(seq):
        return lambda dphik, *old: run_final(
            seq, tokens, dy1.reshape(seqs, span, width), kv, phi_k, dq, dphik, dv, later, tab_back,
            row(gain_attn), row(shift_attn), w_qkv, *old
        )

    half_pairs = PAIRS // 2
    if fits:
        theirs, mine = grads
        ffn = Stream(scatter_stream(theirs, mine))
        phase([scan], [scan])
        old = phase([scan, ffn], [scan, ffn], back(0, 0, half_pairs), (dnum,))
        phase([scan])
        phase([ffn], [scan])
        old = phase([scan], [scan], back(0, half_pairs, half_pairs), (dnum,) + tuple(old))
        phase([scan], [scan])
        old = phase([scan], [ffn], back(1, 0, half_pairs), (dnum,) + tuple(old))
        old = phase([ffn], [scan], back(1, half_pairs, half_pairs), (dnum,) + tuple(old))
        phase([scan], [scan, ffn])
        later = scan.value
    else:
        old = phase([scan], [scan], back(0, 0, PAIRS), (dnum,))
        old = phase([scan], [scan], back(1, 0, PAIRS), (dnum,) + tuple(old))
        later = of_stages(scan)
    dq, dphik, dv = old
    later = later.reshape(seqs, SCAN_ROWS, FEATS)

    def join(*items):
        sums_attn, sum_qkv = items[0] + items[2], items[1] + items[3]
        return jnp.concatenate(
            [sums[:4].reshape(-1), sum_up.reshape(-1), sums_attn[:2].reshape(-1), sum_qkv.reshape(-1)]
        ).reshape(-1, LANES)

    all_bits = [bit for axis in reversed(AXES) for bit in axis_bits(axis)]
    if fits:
        some = lambda half, dqkv: qkv_grads(half, chips, flat(h1), flat(dqkv))

        def both(dphik):
            dx, dqkv, *parts = last(0)(dphik)
            dx, dqkv, *more = last(1)(dphik, dx, dqkv)
            theirs = some(1 - core, dqkv)
            return dx, dqkv, theirs, *parts, *more

        dx, dqkv, theirs, *parts = phase([ffn], [ffn], both, (dphik,))
        more = []
        qkv_sum = Stream(bucket_stream(theirs, lambda: more[0]))
        packed = lax.all_gather(ffn.value, ("c", "x", "y", "z"))
        small = Stream(small_stream(join(*parts), all_bits))
        more += phase([qkv_sum, small], [small], lambda dqkv: (some(core, dqkv),), (dqkv,))
        phase((), [qkv_sum])
        while qkv_sum.pending is not None or small.pending is not None:
            both = [item for item in (qkv_sum, small) if item.pending is not None]
            phase(both, both)
        grad_w_qkv = place_pieces(qkv_sum.value, meta, (width, 3 * width))
        small = small.value
        grad_w_down, grad_w_up, grad_w_out = unpack(packed, hidden, width)
    else:
        dx, dqkv, *parts = last(0)(dphik)
        dx, dqkv, *more = last(1)(dphik, dx, dqkv)
        grad_w_down, grad_w_up, grad_w_out, grad_w_qkv = lax.psum(
            (
                *grads, dot_tn(flat(h1), flat(dqkv)),
            ),
            AXES,
        )
        small = of_stages(Stream(small_stream(join(*parts, *more), all_bits)))
    small = small.reshape(-1)
    cuts = [width * i for i in range(1, 5)]
    cuts += [cuts[-1] + hidden, cuts[-1] + hidden + width, cuts[-1] + hidden + 2 * width]
    b_down_g, b_out_g, gain_f, shift_f, b_up_g, gain_a, shift_a, b_qkv_g = jnp.split(small, cuts)
    return (
        out.reshape(seqs, span, width), dx, gain_a, shift_a, grad_w_qkv, b_qkv_g,
        grad_w_out, b_out_g, gain_f, shift_f, grad_w_up, b_up_g, grad_w_down, b_down_g,
    )


def solution(mesh):
    dp, seq = mesh.shape["dp"], mesh.shape["seq"]
    cut = jax.sharding.Mesh(mesh.devices.reshape(dp, 4, seq // 8, 2), AXES)
    split = P("x", ("z", "y", "c"), None)
    return jax.shard_map(
        shards,
        mesh=cut,
        in_specs=(split, split) + (P(),) * 14,
        out_specs=(split, split) + (P(),) * 12,
        check_vma=False,
    )
```

```python
import functools
import math

import jax
import jax.numpy as jnp
from jax import lax
from jax.experimental import pallas as pl
from jax.experimental.pallas import tpu as pltpu
from jax.sharding import PartitionSpec as P

HEADS = 8
HEAD_DIM = 64
FEATS = 256
PAIRS = HEADS // 2
LANES = 2 * HEAD_DIM
AXES = ("x", "z", "y", "c")
BF = jnp.bfloat16
F32 = jnp.float32
Z_SCALE = HEAD_DIM ** (-0.25)
SQ_SCALE = 0.5 * HEAD_DIM ** (-0.5) / Z_SCALE
EXP_SCALE = Z_SCALE * math.log2(math.e)
EXP_SHIFT = 0.5 * math.log2(FEATS)
STATE_ROWS = PAIRS * LANES
SCAN_ROWS = STATE_ROWS + 32
TILE = 256
MID_TILE = 512
GELU_A = math.sqrt(2.0 / math.pi)
GELU_B = 0.044715
LIMITS = {
    "keys": 56, "local": 56, "middle": 60, "scores": 56, "final": 30, "qkv_grads": 16, "place": 16, "unpack": 16,
}


def dot(a, b):
    return lax.dot_general(a, b, (((1,), (0,)), ((), ())), preferred_element_type=F32)


def dot_nt(a, b):
    return lax.dot_general(a, b, (((1,), (1,)), ((), ())), preferred_element_type=F32)


def dot_tn(a, b):
    return lax.dot_general(a, b, (((0,), (0,)), ((), ())), preferred_element_type=F32)


def lower_half(shape):
    return lax.broadcasted_iota(jnp.int32, shape, 1) < HEAD_DIM


def swap_halves(values):
    return pltpu.roll(values, HEAD_DIM, 1)


def normalise(values):
    center = values - jnp.mean(values, axis=-1, keepdims=True)
    spread = jnp.mean(center * center, axis=-1, keepdims=True)
    scale = lax.rsqrt(spread + 1e-05)
    return center * scale, scale


def normalise_back(grad, unit, scale, gain):
    inner = grad * gain
    first = jnp.mean(inner, axis=-1, keepdims=True)
    second = jnp.mean(inner * unit, axis=-1, keepdims=True)
    return scale * (inner - first - unit * second)


def features(pair, tabs):
    wide = pair.astype(F32)
    square = wide * wide * SQ_SCALE
    high = square.astype(BF).astype(F32)
    low = swap_halves(square - high)
    keep = lower_half(wide.shape)
    even = jnp.where(keep, high, low).astype(BF)
    odd = jnp.where(keep, low, high).astype(BF)
    out = []
    for block, tab in ((even, tabs[0]), (odd, tabs[1])):
        proj = dot_nt(jnp.concatenate([pair, block], axis=1), tab)
        out.append(jnp.exp2(proj * EXP_SCALE - EXP_SHIFT).astype(BF))
    return out


def values_ones(pair):
    keep = lower_half(pair.shape)
    one = jnp.ones_like(pair)
    return jnp.where(keep, pair, one), jnp.where(keep, one, pair)


def causal_rows(first_row, rows, cols):
    return (
        lax.broadcasted_iota(jnp.int32, (rows, cols), 0) + first_row
        >= lax.broadcasted_iota(jnp.int32, (rows, cols), 1)
    )


def state_pair(state, norm, parity):
    wide = jnp.broadcast_to(norm, (HEAD_DIM, norm.shape[1]))
    return jnp.concatenate([state, wide] if parity == 0 else [wide, state], axis=0)


def kv_kernel(x_ref, gain_ref, shift_ref, w_ref, b_ref, tab_ref, h_ref, kv_ref, phik_ref, state_ref):
    width = x_ref.shape[-1]
    unit, _ = normalise(x_ref[0].astype(F32))
    low = (unit * gain_ref[...] + shift_ref[...]).astype(BF)
    h_ref[0] = low
    kv_ref[0] = (dot(low, w_ref[:, width:]) + b_ref[...][None, width:]).astype(BF)
    tabs = (tab_ref[0], tab_ref[1])
    norms = []
    for pair in range(PAIRS):
        key = kv_ref[0, :, pair * LANES : (pair + 1) * LANES]
        value = kv_ref[0, :, width + pair * LANES : width + (pair + 1) * LANES]
        phi = features(key, tabs)
        ones = values_ones(value)
        full = []
        for head in range(2):
            at = (2 * pair + head) * FEATS
            phik_ref[0, :, at : at + FEATS] = phi[head]
            full.append(dot_tn(ones[head], phi[head]))
        state_ref[0, pair * LANES : pair * LANES + HEAD_DIM, :] = full[0][:HEAD_DIM]
        state_ref[0, pair * LANES + HEAD_DIM : (pair + 1) * LANES, :] = full[1][HEAD_DIM:]
        norms += [full[0][HEAD_DIM : HEAD_DIM + 1], full[1][0:1]]
    state_ref[0, STATE_ROWS : STATE_ROWS + HEADS, :] = jnp.concatenate(norms, axis=0)
    state_ref[0, STATE_ROWS + HEADS :, :] = jnp.zeros((SCAN_ROWS - STATE_ROWS - HEADS, FEATS), F32)


def local_kernel(h_ref, w_ref, b_ref, v_ref, phik_ref, tab_ref, *rest):
    q_ref, phiq_ref, num_ref = rest[-3:]
    query = (dot(h_ref[0], w_ref[...]) + b_ref[...]).astype(BF)
    q_ref[0] = query
    phi = features(query, (tab_ref[0], tab_ref[1]))
    ones = values_ones(v_ref[0])
    span = h_ref.shape[1]
    for head in range(2):
        phiq_ref[0, :, head * FEATS : (head + 1) * FEATS] = phi[head]
        for row in range(0, span, TILE):
            cols = row + TILE
            keys = phik_ref[0, :cols, head * FEATS : (head + 1) * FEATS]
            scores = dot_nt(phi[head][row : row + TILE], keys)
            scores = jnp.where(causal_rows(row, TILE, cols), scores, 0.0).astype(BF)
            num_ref[0, row : row + TILE, head * LANES : (head + 1) * LANES] = dot(scores, ones[head][:cols])


def middle_kernel(
    per, chips, core_ref, x_ref, dy_ref, num_ref, phiq_ref, state_ref, w_out_ref, b_out_ref, gain_ref, shift_ref,
    w_up_from, b_up_ref, w_down_from, b_down_ref,
    out_ref, dy1_ref, dnum_ref, dstate_ref, sums_ref, sum_up_ref, *rest,
):
    *grads, w_up_ref, w_down_ref, w_sems = rest
    down_ref, up_ref, wout_ref = grads[2:5] if chips else grads
    loads = [
        pltpu.make_async_copy(source, place, w_sems.at[at])
        for at, (source, place) in enumerate(((w_up_from, w_up_ref), (w_down_from, w_down_ref)))
    ]

    @pl.when(pl.program_id(0) == 0)
    def _():
        for load in loads:
            load.start()

    step = pl.program_id(0)
    width = x_ref.shape[-1]
    att_parts, den_parts = [], []
    for pair in range(PAIRS):
        nums = []
        for head in range(2):
            at = 2 * pair + head
            rows = pair * LANES + head * HEAD_DIM
            state = state_pair(
                state_ref[0, rows : rows + HEAD_DIM, :].astype(BF),
                state_ref[0, STATE_ROWS + at : STATE_ROWS + at + 1, :].astype(BF),
                head,
            )
            nums.append(
                num_ref[:, at * LANES : (at + 1) * LANES]
                + dot_nt(phiq_ref[:, at * FEATS : (at + 1) * FEATS], state)
            )
        keep = lower_half(nums[0].shape)
        den = swap_halves(jnp.where(keep, nums[1], nums[0]))
        recip = 1.0 / den
        att_parts.append(jnp.where(keep, nums[0], nums[1]) * recip)
        den_parts.append(recip)
    mixed = jnp.concatenate([part.astype(BF) for part in att_parts], axis=1)
    middle = x_ref[...].astype(F32) + dot(mixed, w_out_ref[...]) + b_out_ref[...]
    unit, scale = normalise(middle)
    low = (unit * gain_ref[...] + shift_ref[...]).astype(BF)
    grad_out = dy_ref[...]
    hidden = w_up_ref.shape[1]
    chunk = 1024

    @pl.when(step == 0)
    def _():
        for load in loads:
            load.wait()

    result = middle + b_down_ref[...]
    grad_low = jnp.zeros(middle.shape, F32)

    @pl.when(step == 0)
    def _():
        sums_ref[...] = jnp.zeros_like(sums_ref)
        sum_up_ref[...] = jnp.zeros_like(sum_up_ref)

    for at in range(0, hidden, chunk):
        up = dot(low, w_up_ref[:, at : at + chunk]) + b_up_ref[:, at : at + chunk]
        square = up * up
        tanh = jnp.tanh(up * (GELU_A + GELU_A * GELU_B * square))
        half = 0.5 + 0.5 * tanh
        act = (up * half).astype(BF)
        add_to(down_ref, slice(at, at + chunk), slice(None), step, dot_tn(act, grad_out))
        slope = half + (0.5 * up) * (1.0 - tanh * tanh) * (GELU_A + 3.0 * GELU_A * GELU_B * square)
        result += dot(act, w_down_ref[at : at + chunk, :])
        dup = (dot_nt(grad_out, w_down_ref[at : at + chunk, :]) * slope).astype(BF)
        add_to(up_ref, slice(None), slice(at, at + chunk), step, dot_tn(low, dup))
        grad_low += dot_nt(dup, w_up_ref[:, at : at + chunk])
        sum_up_ref[:, at : at + chunk] += jnp.sum(dup.astype(F32), axis=0, keepdims=True)
    out_ref[...] = result.astype(BF)
    if chips:
        packed_ref, sems = grads[5:]
        behind = packed_ref.shape[2] * 2 * hidden // (2 * hidden + middle.shape[1])
        parts = [
            (half, first, count)
            for first, count in ((0, behind), (behind, packed_ref.shape[2] - behind))
            for half in range(2)
        ]
        stores = [
            pltpu.make_async_copy(
                packed_ref.at[half, :, pl.ds(first, count), :],
                grads[half].at[:, pl.ds(first, count), :],
                sems.at[at],
            )
            for at, (half, first, count) in enumerate(parts)
        ]

        @pl.when(step == pl.num_programs(0) - 1)
        def _():
            for half in range(2):
                pack_half(core_ref[0] if half else 1 - core_ref[0], chips, packed_ref.at[half], 0, down_ref, up_ref)
                stores[half].start()

    wide = grad_out.astype(F32)
    grad_mid = wide + normalise_back(grad_low, unit, scale, gain_ref[...])
    dy1_ref[...] = grad_mid
    grad_mid_low = grad_mid.astype(BF)
    add_to(wout_ref, slice(None), slice(None), step, dot_tn(mixed, grad_mid_low))
    for row, item in enumerate((wide, grad_mid, grad_low * unit, grad_low)):
        sums_ref[row : row + 1, :] += jnp.sum(item, axis=0, keepdims=True)
    grad_att = dot_nt(grad_mid_low, w_out_ref[...])

    @pl.when(lax.rem(step, per) == 0)
    def _():
        dstate_ref[...] = jnp.zeros_like(dstate_ref)

    for pair in range(PAIRS):
        grad = grad_att[:, pair * LANES : (pair + 1) * LANES] * den_parts[pair]
        keep = lower_half(grad.shape)
        prod = swap_halves(-(grad * att_parts[pair]))
        both = (jnp.where(keep, grad, prod).astype(BF), jnp.where(keep, prod, grad).astype(BF))
        for head in range(2):
            at = 2 * pair + head
            dnum_ref[:, at * LANES : (at + 1) * LANES] = both[head]
            full = dot_tn(both[head], phiq_ref[:, at * FEATS : (at + 1) * FEATS])
            rows = pair * LANES + head * HEAD_DIM
            main = full[:HEAD_DIM] if head == 0 else full[HEAD_DIM:]
            rest = full[HEAD_DIM:] if head == 0 else full[:HEAD_DIM]
            dstate_ref[0, rows : rows + HEAD_DIM, :] += main
            dstate_ref[0, STATE_ROWS + at : STATE_ROWS + at + 1, :] += jnp.sum(rest, axis=0, keepdims=True)

    if chips:

        @pl.when(step == pl.num_programs(0) - 1)
        def _():
            for half in range(2):
                pack_half(core_ref[0] if half else 1 - core_ref[0], chips, packed_ref.at[half], behind, None, wout_ref)
                stores[2 + half].start()
            for store in stores:
                store.wait()


def add_to(total_ref, rows, cols, step, values):
    total_ref[rows, cols] = jnp.where(step == 0, 0.0, total_ref[rows, cols]) + values


def pack_half(half, chips, packed_ref, base, down_ref, *wide_refs):
    if down_ref is not None:
        rows = down_ref.shape[0] // 2 // chips
        first = half * (down_ref.shape[0] // 2)
        for chip in range(chips):
            for strip in range(down_ref.shape[1] // LANES):
                packed_ref[chip, base + strip * rows : base + (strip + 1) * rows, :] = down_ref[
                    pl.ds(pl.multiple_of(first + chip * rows, rows), rows), strip * LANES : (strip + 1) * LANES
                ]
        base += rows * (down_ref.shape[1] // LANES)
    for total_ref in wide_refs:
        rows = total_ref.shape[0] // chips
        strips = total_ref.shape[1] // 2 // LANES
        for strip in range(strips):
            col = pl.multiple_of((half * strips + strip) * LANES, LANES)
            for chip in range(chips):
                packed_ref[chip, base : base + rows, :] = total_ref[
                    chip * rows : (chip + 1) * rows, pl.ds(col, LANES)
                ]
            base += rows


def score_back_kernel(
    first, q_ref, v_ref, phiq_ref, phik_ref, dnum_ref, state_ref, norm_ref, tab_ref, *rest
):
    dq_ref, dphik_ref, dv_ref = rest[-3:]
    span = q_ref.shape[1]
    ones = values_ones(v_ref[0])
    back, dvs = [], []
    for head in range(2):
        phiq = phiq_ref[0, :, head * FEATS : (head + 1) * FEATS]
        phik = phik_ref[0, :, head * FEATS : (head + 1) * FEATS]
        dnum = dnum_ref[0, :, head * LANES : (head + 1) * LANES]
        state = state_pair(
            state_ref[0, head * HEAD_DIM : (head + 1) * HEAD_DIM, :].astype(BF),
            norm_ref[0, pl.ds(2 * (first + pl.program_id(0)) + head, 1), :].astype(BF),
            head,
        )
        grads = []
        for row in range(0, span, TILE):
            cols = row + TILE
            mine = dnum[row : row + TILE]
            grad = dot_nt(mine, ones[head][:cols])
            grad = jnp.where(causal_rows(row, TILE, cols), grad, 0.0).astype(BF)
            grad_phi = dot(mine, state) + dot(grad, phik[:cols])
            grads.append((grad_phi * phiq[row : row + TILE].astype(F32)).astype(BF))
        back.append(dot(jnp.concatenate(grads, axis=0), tab_ref[head]))
        dv = []
        for row in range(0, span, TILE):
            count = span - row
            seen = (
                lax.broadcasted_iota(jnp.int32, (TILE, count), 0)
                <= lax.broadcasted_iota(jnp.int32, (TILE, count), 1)
            )
            turned = dot_nt(ones[head][row : row + TILE], dnum[row:])
            turned = jnp.where(seen, turned, 0.0).astype(BF)
            dphik_ref[0, row : row + TILE, head * FEATS : (head + 1) * FEATS] = dot(turned, phiq[row:]).astype(BF)
            scores = dot_nt(phik[row : row + TILE], phiq[row:])
            scores = jnp.where(seen, scores, 0.0).astype(BF)
            dv.append(dot(scores, dnum[row:]))
        dvs.append(jnp.concatenate(dv, axis=0))
    keep = lower_half(dvs[0].shape)
    dv_ref[0] = jnp.where(keep, dvs[0], dvs[1])
    dq_ref[0] = finish_back(back, q_ref[0]).astype(BF)


def finish_back(back, pair):
    keep = lower_half(back[0].shape)
    main = jnp.where(keep, back[0], back[1])
    total = swap_halves(jnp.where(keep, back[1], back[0]))
    return main * Z_SCALE - total * pair.astype(F32) * (HEAD_DIM ** (-0.5))


def final_kernel(
    x_ref, dy1_ref, kv_ref, phik_ref, dq_ref, dphik_ref, dv_ref, later_ref, tab_ref, gain_ref, shift_ref, w_ref,
    *rest,
):
    dx_ref, dqkv_ref, sums_ref, sum_qkv_ref = rest[-4:]
    width = x_ref.shape[-1]
    grad = dot_nt(dq_ref[0], w_ref[:, :width])

    sums_ref[...] = jnp.zeros_like(sums_ref)
    for pair in range(PAIRS):
        key = kv_ref[0, :, pair * LANES : (pair + 1) * LANES]
        value = kv_ref[0, :, width + pair * LANES : width + (pair + 1) * LANES]
        ones = values_ones(value)
        back, dvs = [], []
        for head in range(2):
            at = 2 * pair + head
            rows = pair * LANES + head * HEAD_DIM
            state = later_ref[0, rows : rows + HEAD_DIM, :].astype(BF)
            norm = later_ref[0, STATE_ROWS + at : STATE_ROWS + at + 1, :]
            high = norm.astype(BF)
            low = (norm - high.astype(F32)).astype(BF)
            rest = jnp.concatenate(
                [high.astype(F32), low.astype(F32), jnp.zeros((HEAD_DIM - 2, FEATS), F32)], axis=0
            ).astype(BF)
            full = jnp.concatenate([state, rest] if head == 0 else [rest, state], axis=0)
            phik = phik_ref[0, :, at * FEATS : (at + 1) * FEATS]
            grad_phi = dphik_ref[0, :, at * FEATS : (at + 1) * FEATS].astype(F32) + dot(ones[head], full)
            inner = (grad_phi * phik.astype(F32)).astype(BF)
            back.append(dot(inner, tab_ref[head]))
            dvs.append(dot_nt(phik, full))
        keep = lower_half(dvs[0].shape)
        dk = finish_back(back, key).astype(BF)
        dv = (dv_ref[0, :, pair * LANES : (pair + 1) * LANES] + jnp.where(keep, dvs[0], dvs[1])).astype(BF)
        dqkv_ref[0, :, width + pair * LANES : width + (pair + 1) * LANES] = dk
        dqkv_ref[0, :, 2 * width + pair * LANES : 2 * width + (pair + 1) * LANES] = dv
    dqkv_ref[0, :, :width] = dq_ref[0]
    dkv = dqkv_ref[0, :, width:]
    grad += dot_nt(dkv, w_ref[:, width:])
    unit, scale = normalise(x_ref[0].astype(F32))
    dx_ref[0] = (dy1_ref[0] + normalise_back(grad, unit, scale, gain_ref[...])).astype(BF)
    sums_ref[0:1, :] = jnp.sum(grad * unit, axis=0, keepdims=True)
    sums_ref[1:2, :] = jnp.sum(grad, axis=0, keepdims=True)
    sum_qkv_ref[:, :width] = jnp.sum(dq_ref[0].astype(F32), axis=0, keepdims=True)
    sum_qkv_ref[:, width:] = jnp.sum(dkv.astype(F32), axis=0, keepdims=True)


def put_chunks(out_ref, values):
    chips = out_ref.shape[0]
    rows = values.shape[0] // chips
    for chunk in range(chips):
        for strip in range(values.shape[1] // LANES):
            out_ref[chunk, strip * rows : (strip + 1) * rows, :] = values[
                chunk * rows : (chunk + 1) * rows, strip * LANES : (strip + 1) * LANES
            ]


def qkv_grads_kernel(half_ref, h1_ref, dqkv_ref, out_ref):
    put_chunks(out_ref, dot_tn(h1_ref[...], dqkv_ref[...]))


def place_kernel(counts, rows, meta_ref, *refs):
    out_ref = refs[-1]
    total = sum(counts)
    along = refs[0].shape[1]
    for core in range(2):

        @pl.when(meta_ref[0] == core)
        def _():
            for half in range(2):
                base = out_ref.shape[1] // LANES // 2 * (half ^ core)
                for at in range(total):
                    piece = refs[half * total + at]
                    first = at < counts[0]
                    col = base if first else base + refs[half * total].shape[2] // rows
                    for inner in range(piece.shape[0]):
                        x, y = (at, inner) if first else (inner, at - counts[0])
                        row = (meta_ref[1] ^ x) * counts[1] + (meta_ref[2] ^ y)
                        for last in range(along):
                            chip = row * along + (meta_ref[3] ^ last)
                            where = pl.ds(pl.multiple_of(chip * rows, rows), rows)
                            for strip in range(piece.shape[2] // rows):
                                out_ref[where, (col + strip) * LANES : (col + strip + 1) * LANES] = piece[
                                    inner, last, strip * rows : (strip + 1) * rows, :
                                ]


def unpack_kernel(packed_ref, *out_refs):
    row = 0
    block = packed_ref.shape[0]
    for out_ref in out_refs:
        rows = out_ref.shape[0] // block
        for strip in range(out_ref.shape[1] // LANES):
            for chunk in range(block):
                out_ref[chunk * rows : (chunk + 1) * rows, strip * LANES : (strip + 1) * LANES] = packed_ref[
                    chunk, row : row + rows, :
                ]
            row += rows


def whole(shape):
    return pl.BlockSpec(shape, lambda *_: (0,) * len(shape))


def params(count, name):
    return pltpu.CompilerParams(
        dimension_semantics=("arbitrary",) * count if count else None, vmem_limit_bytes=LIMITS[name] * 1024 * 1024
    )


def shape(dims, kind):
    return jax.ShapeDtypeStruct(dims, kind)


def place_of():
    place = 0
    for axis in AXES:
        place = place * lax.axis_size(axis) + lax.axis_index(axis)
    return place


def send(values, mask):
    count = math.prod(lax.axis_size(axis) for axis in AXES)
    return lax.ppermute(values, AXES, [(i, i ^ mask) for i in range(count)])


def bit_of(bit):
    return (place_of() >> bit) & 1


def swap_with(values, bit):
    return send(values, 1 << bit)


def axis_bits(axis):
    at = 0
    for other in reversed(AXES):
        size = lax.axis_size(other).bit_length() - 1
        if other == axis:
            return list(range(at, at + size))
        at += size


def value_of(bits):
    place = place_of()
    return sum(((place >> b) & 1) << i for i, b in enumerate(bits))


def mask_of(bits, value):
    return sum(((value >> i) & 1) << b for i, b in enumerate(bits))


def place_pieces(own, meta, dims):
    both = own[0] + own[1] + own[2]
    chips = len(own[0]) * len(own[1]) * own[0][0].shape[1]
    return pl.pallas_call(
        functools.partial(place_kernel, (len(own[0]), len(own[1])), dims[0] // chips),
        in_specs=[pl.BlockSpec(memory_space=pltpu.SMEM)] + [pl.BlockSpec(memory_space=pltpu.VMEM)] * len(both),
        out_specs=pl.BlockSpec(memory_space=pltpu.VMEM),
        out_shape=shape(dims, F32),
        compiler_params=params(0, "place"),
        name="place",
    )(meta, *both)


def scan_stream(values, bits, split, reverse):
    bit = bits[0]
    mine = bit_of(bit)
    far = (mine == 0) if reverse else (mine == 1)
    if split:
        half = values.shape[0] // 2
        kept = lax.dynamic_slice_in_dim(values, mine * half, half, 0)
        (got,) = yield [(lax.dynamic_slice_in_dim(values, (1 - mine) * half, half, 0), 1 << bit)]
        before = yield from scan_stream(kept + got, bits[1:], split - 1, reverse)
        ours = before + jnp.where(far, got, 0.0)
        (theirs,) = yield [(before + jnp.where(far, 0.0, kept), 1 << bit)]
        return jnp.concatenate(
            [jnp.where(mine == 0, ours, theirs), jnp.where(mine == 0, theirs, ours)], axis=0
        )
    (got,) = yield [(values, 1 << bit)]
    part = jnp.where(far, got, 0.0)
    if len(bits) == 1:
        return part
    rest = yield from scan_stream(values + got, bits[1:], 0, reverse)
    return part + rest


def cut_part(part, axis, at, rows):
    start, size = [0] * part.ndim, list(part.shape)
    start[axis], size[axis] = at, 1
    if rows:
        start[-2], size[-2] = rows
    return jnp.squeeze(lax.dynamic_slice(part, start, size), axis)


def chunks(parts, axis, bits, rows=None):
    mine = value_of(bits)
    own = [cut_part(part, axis, mine, rows) for part in parts]
    others = [
        add_all([cut_part(part, axis, mine ^ value, rows) for part in parts]) for value in range(1, 1 << len(bits))
    ]
    return own, others


def add_all(items):
    return functools.reduce(jnp.add, items)


def to_partners(items, bits):
    return [(item, mask_of(bits, value + 1)) for value, item in enumerate(items)]


def to_all(item, bits):
    return to_partners([item] * ((1 << len(bits)) - 1), bits)


def scatter_stream(theirs, mine):
    x, y, z = axis_bits("x"), axis_bits("y"), axis_bits("z")
    (got,) = yield [(theirs, 1)]
    parts = [mine() if callable(mine) else mine, got]
    cut = parts[0].shape[1] // 2
    parts = [item.reshape(1 << len(x), 1 << len(y), 1 << len(z), *item.shape[1:]) for item in parts]
    (a, a_out), (b, b_out) = chunks(parts, 0, x, (0, cut)), chunks(parts, 1, y, (cut, cut))
    got = yield to_partners(a_out, x) + to_partners(b_out, y)
    a, a_out = chunks(a + got[: len(a_out)], 0, y)
    b, b_out = chunks(b + got[-len(b_out) :], 0, x)
    got = yield to_partners(a_out, y) + to_partners(b_out, x)
    parts = [a + got[: len(a_out)], b + got[-len(b_out) :]]
    both = jnp.concatenate([add_all(part) for part in parts], axis=1)
    own, out = chunks([both], 0, z)
    got = yield to_partners(out, z)
    return add_all(own + got)


def bucket_stream(theirs, mine):
    x, y, z = axis_bits("x"), axis_bits("y"), axis_bits("z")
    chunk = yield from scatter_stream(theirs, mine)
    got = yield to_all(chunk, z)
    cut = chunk.shape[0] // 2
    a, b = [jnp.stack([item[at : at + cut] for item in [chunk] + got]) for at in (0, cut)]
    got = yield to_all(a, y) + to_all(b, x)
    count = (1 << len(y)) - 1
    a, b = jnp.stack([a] + got[:count]), jnp.stack([b] + got[count:])
    got = yield to_all(a, x) + to_all(b, y)
    count = (1 << len(x)) - 1
    a, b = [a] + got[:count], [b] + got[count:]
    got = yield [(item, 1) for item in a + b]
    return a, b, got


def small_stream(values, bits):
    for bit in bits:
        (got,) = yield [(values, 1 << bit)]
        values = values + got
    return values


class Stream:
    def __init__(self, chain):
        self.chain, self.value, self.flying = chain, None, None
        self.pending = next(chain)

    def feed(self, got):
        self.flying = None
        try:
            self.pending = self.chain.send(got)
        except StopIteration as end:
            self.pending, self.value = None, end.value


def phase(start=(), wait=(), work=None, inputs=()):
    ready = [[item for item, _ in stream.pending] for stream in start]
    ready, inputs = lax.optimization_barrier((ready, tuple(inputs)))
    for stream, items in zip(start, ready):
        stream.flying = [send(item, mask) for item, (_, mask) in zip(items, stream.pending)]
    done = tuple(work(*inputs)) if work else ()
    got, done = lax.optimization_barrier(([stream.flying for stream in wait], done))
    for stream, items in zip(wait, got):
        stream.feed(list(items))
    return done


def of_stages(stream, wait_too=()):
    while stream.pending is not None:
        phase([stream], [stream])
    return stream.value


def half_of(half):
    return half.astype(jnp.int32).reshape(1)


def qkv_grads(half, chips, h1, dqkv):
    rows, width = h1.shape
    block = 2 * LANES
    steps = dqkv.shape[1] // 2 // block
    own = width * block // chips // LANES
    return pl.pallas_call(
        qkv_grads_kernel,
        grid_spec=pltpu.PrefetchScalarGridSpec(
            num_scalar_prefetch=1,
            grid=(steps,),
            in_specs=[
                pl.BlockSpec((rows, width), lambda j, h: (0, 0)),
                pl.BlockSpec((rows, block), lambda j, h: (0, h[0] * steps + j)),
            ],
            out_specs=pl.BlockSpec((chips, own, LANES), lambda j, h: (0, j, 0)),
        ),
        out_shape=shape((chips, own * steps, LANES), F32),
        compiler_params=params(1, "qkv_grads"),
        name="qkv_grads",
    )(half_of(half), h1, dqkv)


def unpack(packed, hidden, width):
    devices = packed.shape[0]
    block = 4
    per = devices // 2 // block
    rows = width // (devices // 2) * block
    return pl.pallas_call(
        unpack_kernel,
        grid=(devices // block,),
        in_specs=[pl.BlockSpec((block,) + packed.shape[1:], lambda t: (t, 0, 0))],
        out_specs=[
            pl.BlockSpec((hidden * block // devices, width), lambda t: (t, 0)),
            pl.BlockSpec((rows, hidden // 2), lambda t: (t % per, t // per)),
            pl.BlockSpec((rows, width // 2), lambda t: (t % per, t // per)),
        ],
        out_shape=[shape((hidden, width), F32), shape((width, hidden), F32), shape((width, width), F32)],
        compiler_params=params(1, "unpack"),
        name="unpack",
    )(packed)


def seq_block(seq, span, width, at=0):
    return pl.BlockSpec((1, span, width), lambda p: (seq, 0, at + p))


def run_local(seq, h1, w_qkv, b_qkv, kv, phi_k, tab_in, *old):
    seqs, span, width = h1.shape
    block = functools.partial(seq_block, seq, span)
    return pl.pallas_call(
        local_kernel,
        grid=(PAIRS,),
        in_specs=[
            pl.BlockSpec((1, span, width), lambda p: (seq, 0, 0)), pl.BlockSpec((width, LANES), lambda p: (0, p)),
            pl.BlockSpec((1, LANES), lambda p: (0, p)), block(LANES, PAIRS), block(2 * FEATS),
            whole((2, FEATS, 2 * LANES)),
        ]
        + [pl.BlockSpec(memory_space=pl.ANY)] * len(old),
        out_specs=[block(LANES), block(2 * FEATS), block(2 * LANES)],
        out_shape=[
            shape((seqs, span, width), BF), shape((seqs, span, HEADS * FEATS), BF),
            shape((seqs, span, HEADS * LANES), F32),
        ],
        input_output_aliases={6 + i: i for i in range(len(old))},
        compiler_params=params(1, "local"),
        name="local",
    )(h1, w_qkv, b_qkv, kv, phi_k, tab_in, *old)


def run_scores(seq, first, count, q, kv, phi_q, phi_k, dnum, before, tab_back, *old):
    seqs, span, width = q.shape
    block = lambda w, at=0: seq_block(seq, span, w, at + first)
    return pl.pallas_call(
        functools.partial(score_back_kernel, first),
        grid=(count,),
        in_specs=[
            block(LANES), block(LANES, PAIRS), block(2 * FEATS), block(2 * FEATS), block(2 * LANES),
            pl.BlockSpec((1, LANES, FEATS), lambda p: (seq, first + p, 0)),
            pl.BlockSpec((1, HEADS, FEATS), lambda p: (seq, STATE_ROWS // HEADS, 0)),
            whole((2, FEATS, LANES)),
        ]
        + [pl.BlockSpec(memory_space=pl.ANY)] * len(old),
        out_specs=[block(LANES), block(2 * FEATS), block(LANES)],
        out_shape=[
            shape((seqs, span, width), BF), shape((seqs, span, HEADS * FEATS), BF),
            shape((seqs, span, width), F32),
        ],
        input_output_aliases={8 + i: i for i in range(len(old))},
        compiler_params=params(1, "scores"),
        name="scores",
    )(q, kv, phi_q, phi_k, dnum, before, before, tab_back, *old)


def run_keys(x, gain, bias, w_qkv, b_qkv, tab_in):
    seqs, span, width = x.shape
    three = lambda d: pl.BlockSpec((1,) + d, lambda s: (s, 0, 0))
    return pl.pallas_call(
        kv_kernel,
        grid=(seqs,),
        in_specs=[
            three((span, width)), whole((1, width)), whole((1, width)), whole((width, 3 * width)),
            whole((3 * width,)), whole((2, FEATS, 2 * LANES)),
        ],
        out_specs=[
            three((span, width)), three((span, 2 * width)), three((span, HEADS * FEATS)), three((SCAN_ROWS, FEATS)),
        ],
        out_shape=[
            shape((seqs, span, width), BF), shape((seqs, span, 2 * width), BF),
            shape((seqs, span, HEADS * FEATS), BF), shape((seqs, SCAN_ROWS, FEATS), F32),
        ],
        compiler_params=params(1, "keys"),
        name="keys",
    )(x, gain, bias, w_qkv, b_qkv, tab_in)


def run_middle(seqs, chips, core, x, dy, num, phi_q, before, w_out, b_out, gain, bias, w_up, b_up, w_down, b_down):
    rows, width = x.shape
    hidden = w_up.shape[1]
    per = rows // seqs // MID_TILE
    tile = lambda w: pl.BlockSpec((MID_TILE, w), lambda t, c: (t, 0))
    of_seq = lambda d: pl.BlockSpec((1,) + d, lambda t, c: (t // per, 0, 0))
    once = lambda d: pl.BlockSpec(d, lambda t, c: (0,) * len(d), pipeline_mode=pl.Buffered(1))
    sums = [(hidden, width), (width, hidden), (width, width)]
    packed = (hidden * width * 2 + width * width) // 2 // max(chips, 1) // LANES
    grads = [(chips, packed, LANES)] * 2 if chips else sums
    anywhere = pl.BlockSpec(memory_space=pl.ANY)
    scratch = [pltpu.VMEM((width, hidden), BF), pltpu.VMEM((hidden, width), BF), pltpu.SemaphoreType.DMA((2,))]
    if chips:
        scratch = [
            *(pltpu.VMEM(item, F32) for item in sums), pltpu.VMEM((2, chips, packed, LANES), F32),
            pltpu.SemaphoreType.DMA((4,)), *scratch,
        ]
    return pl.pallas_call(
        functools.partial(middle_kernel, per, chips),
        grid_spec=pltpu.PrefetchScalarGridSpec(
            num_scalar_prefetch=1,
            grid=(seqs * per,),
            in_specs=[
                tile(width), tile(width), tile(HEADS * LANES), tile(HEADS * FEATS), of_seq((SCAN_ROWS, FEATS)),
                once((width, width)), once((1, width)), once((1, width)), once((1, width)),
                anywhere, once((1, hidden)), anywhere, once((1, width)),
            ],
            out_specs=[
                tile(width), tile(width), tile(HEADS * LANES), of_seq((SCAN_ROWS, FEATS)),
                once((8, width)), once((1, hidden)),
            ]
            + [anywhere if chips else once(item) for item in grads],
            scratch_shapes=scratch,
        ),
        out_shape=[
            shape((rows, width), BF), shape((rows, width), F32), shape((rows, HEADS * LANES), BF),
            shape((seqs, SCAN_ROWS, FEATS), F32), shape((8, width), F32), shape((1, hidden), F32),
        ]
        + [shape(item, F32) for item in grads],
        compiler_params=params(1, "middle"),
        name="middle",
    )(half_of(core), x, dy, num, phi_q, before, w_out, b_out, gain, bias, w_up, b_up, w_down, b_down)


def run_final(seq, x, dy1, kv, phi_k, dq, dphik, dv, later, tab_back, gain, bias, w_qkv, *old):
    seqs, span, width = x.shape
    three = lambda d: pl.BlockSpec((1,) + d, lambda t: (seq, 0, 0))
    return pl.pallas_call(
        final_kernel,
        grid=(1,),
        in_specs=[
            three((span, width)), three((span, width)), three((span, 2 * width)), three((span, HEADS * FEATS)),
            three((span, width)), three((span, HEADS * FEATS)), three((span, width)), three((SCAN_ROWS, FEATS)),
            whole((2, FEATS, LANES)), whole((1, width)), whole((1, width)), whole((width, 3 * width)),
        ]
        + [pl.BlockSpec(memory_space=pl.ANY)] * len(old),
        out_specs=[three((span, width)), three((span, 3 * width)), whole((8, width)), whole((1, 3 * width))],
        out_shape=[
            shape((seqs, span, width), BF), shape((seqs, span, 3 * width), BF), shape((8, width), F32),
            shape((1, 3 * width), F32),
        ],
        input_output_aliases={12 + i: i for i in range(len(old))},
        compiler_params=params(1, "final"),
        name="final",
    )(x, dy1, kv, phi_k, dq, dphik, dv, later, tab_back, gain, bias, w_qkv, *old)


def shards(
    tokens, cotangent, gain_attn, shift_attn, w_qkv, b_qkv, w_out, b_out,
    gain_ffn, shift_ffn, w_up, b_up, w_down, b_down, tables, pick,
):
    seqs, span, width = tokens.shape
    hidden = w_up.shape[1]
    rows = seqs * span
    table = lax.dynamic_index_in_dim(tables, pick[0] % 2, 0, keepdims=False)
    none = jnp.zeros_like(table)
    minus = jnp.full((FEATS, LANES), -1.0, BF)
    tab_in = jnp.stack(
        [jnp.concatenate([table, none, minus], axis=1), jnp.concatenate([none, table, minus], axis=1)]
    )
    one = jnp.ones_like(table)
    tab_back = jnp.stack([jnp.concatenate([table, one], axis=1), jnp.concatenate([one, table], axis=1)])
    row = lambda a: a.reshape(1, -1)
    seq_bits = axis_bits("c") + axis_bits("y") + axis_bits("z")

    h1, kv, phi_k, state = run_keys(tokens, row(gain_attn), row(shift_attn), w_qkv, b_qkv, tab_in)

    scan = Stream(scan_stream(state.reshape(seqs * SCAN_ROWS, FEATS), seq_bits, len(seq_bits) - 1, False))
    phase([scan], [scan])
    local = None
    for seq in range(seqs):
        work = lambda kv, phi_k, *old: run_local(seq, h1, w_qkv, row(b_qkv), kv, phi_k, tab_in, *old)
        local = phase([scan], [scan], work, (kv, phi_k) + tuple(local or ()))
        if seq == 0:
            phase([scan], [scan])
    q, phi_q, num = local
    before = of_stages(scan).reshape(seqs, SCAN_ROWS, FEATS)

    flat = lambda a: a.reshape(rows, a.shape[-1])
    chips = lax.axis_size("x") * lax.axis_size("y") * lax.axis_size("z")
    fits = width % (16 * chips) == 0
    core = bit_of(0)
    meta = jnp.stack([lax.axis_index(axis) for axis in ("c", "x", "y", "z")]).astype(jnp.int32)
    out, dy1, dnum, dstate, sums, sum_up, *grads = run_middle(
        seqs, chips if fits else 0, core, flat(tokens), flat(cotangent), flat(num), flat(phi_q), before, w_out,
        row(b_out), row(gain_ffn), row(shift_ffn), w_up, row(b_up), w_down, row(b_down),
    )
    scan = Stream(scan_stream(dstate.reshape(seqs * SCAN_ROWS, FEATS), seq_bits, len(seq_bits) - 1, True))
    def back(seq, first, count):
        return lambda dnum, *old: run_scores(
            seq, first, count, q, kv, phi_q, phi_k, dnum.reshape(seqs, span, -1), before, tab_back, *old
        )

    def last(seq):
        return lambda dphik, *old: run_final(
            seq, tokens, dy1.reshape(seqs, span, width), kv, phi_k, dq, dphik, dv, later, tab_back,
            row(gain_attn), row(shift_attn), w_qkv, *old
        )

    half_pairs = PAIRS // 2
    if fits:
        theirs, mine = grads
        ffn = Stream(scatter_stream(theirs, mine))
        phase([scan], [scan])
        old = phase([scan, ffn], [scan, ffn], back(0, 0, half_pairs), (dnum,))
        phase([scan])
        phase([ffn], [scan])
        old = phase([scan], [scan], back(0, half_pairs, half_pairs), (dnum,) + tuple(old))
        phase([scan], [scan])
        old = phase([scan], [scan, ffn], back(1, 0, half_pairs), (dnum,) + tuple(old))
        old = phase([scan, ffn], [scan, ffn], back(1, half_pairs, half_pairs), (dnum,) + tuple(old))
        later = scan.value
    else:
        old = phase([scan], [scan], back(0, 0, PAIRS), (dnum,))
        old = phase([scan], [scan], back(1, 0, PAIRS), (dnum,) + tuple(old))
        later = of_stages(scan)
    dq, dphik, dv = old
    later = later.reshape(seqs, SCAN_ROWS, FEATS)

    def join(*items):
        sums_attn, sum_qkv = items[0] + items[2], items[1] + items[3]
        return jnp.concatenate(
            [sums[:4].reshape(-1), sum_up.reshape(-1), sums_attn[:2].reshape(-1), sum_qkv.reshape(-1)]
        ).reshape(-1, LANES)

    all_bits = [bit for axis in reversed(AXES) for bit in axis_bits(axis)]
    if fits:
        some = lambda half, dqkv: qkv_grads(half, chips, flat(h1), flat(dqkv))

        def both(dphik):
            dx, dqkv, *parts = last(0)(dphik)
            dx, dqkv, *more = last(1)(dphik, dx, dqkv)
            theirs = some(1 - core, dqkv)
            return dx, dqkv, theirs, *parts, *more

        dx, dqkv, theirs, *parts = phase([ffn], [ffn], both, (dphik,))
        more = []
        qkv_sum = Stream(bucket_stream(theirs, lambda: more[0]))
        packed = lax.all_gather(ffn.value, ("c", "x", "y", "z"))
        small = Stream(small_stream(join(*parts), all_bits))
        more += phase([qkv_sum, small], [small], lambda dqkv: (some(core, dqkv),), (dqkv,))
        phase((), [qkv_sum])
        while qkv_sum.pending is not None or small.pending is not None:
            both = [item for item in (qkv_sum, small) if item.pending is not None]
            phase(both, both)
        grad_w_qkv = place_pieces(qkv_sum.value, meta, (width, 3 * width))
        small = small.value
        grad_w_down, grad_w_up, grad_w_out = unpack(packed, hidden, width)
    else:
        dx, dqkv, *parts = last(0)(dphik)
        dx, dqkv, *more = last(1)(dphik, dx, dqkv)
        grad_w_down, grad_w_up, grad_w_out, grad_w_qkv = lax.psum(
            (
                *grads, dot_tn(flat(h1), flat(dqkv)),
            ),
            AXES,
        )
        small = of_stages(Stream(small_stream(join(*parts, *more), all_bits)))
    small = small.reshape(-1)
    cuts = [width * i for i in range(1, 5)]
    cuts += [cuts[-1] + hidden, cuts[-1] + hidden + width, cuts[-1] + hidden + 2 * width]
    b_down_g, b_out_g, gain_f, shift_f, b_up_g, gain_a, shift_a, b_qkv_g = jnp.split(small, cuts)
    return (
        out.reshape(seqs, span, width), dx, gain_a, shift_a, grad_w_qkv, b_qkv_g,
        grad_w_out, b_out_g, gain_f, shift_f, grad_w_up, b_up_g, grad_w_down, b_down_g,
    )


def solution(mesh):
    dp, seq = mesh.shape["dp"], mesh.shape["seq"]
    cut = jax.sharding.Mesh(mesh.devices.reshape(dp, 4, seq // 8, 2), AXES)
    split = P("x", ("z", "y", "c"), None)
    return jax.shard_map(
        shards,
        mesh=cut,
        in_specs=(split, split) + (P(),) * 14,
        out_specs=(split, split) + (P(),) * 12,
        check_vma=False,
    )
```

```python
import functools
import math

import jax
import jax.numpy as jnp
from jax import lax
from jax.experimental import pallas as pl
from jax.experimental.pallas import tpu as pltpu
from jax.sharding import PartitionSpec as P

HEADS = 8
HEAD_DIM = 64
FEATS = 256
PAIRS = HEADS // 2
LANES = 2 * HEAD_DIM
AXES = ("x", "z", "y", "c")
BF = jnp.bfloat16
F32 = jnp.float32
Z_SCALE = HEAD_DIM ** (-0.25)
SQ_SCALE = 0.5 * HEAD_DIM ** (-0.5) / Z_SCALE
EXP_SCALE = Z_SCALE * math.log2(math.e)
EXP_SHIFT = 0.5 * math.log2(FEATS)
STATE_ROWS = PAIRS * LANES
SCAN_ROWS = STATE_ROWS + 32
TILE = 256
MID_TILE = 512
GELU_A = math.sqrt(2.0 / math.pi)
GELU_B = 0.044715
LIMITS = {
    "keys": 56, "local": 56, "middle": 60, "scores": 56, "final": 30, "qkv_grads": 16, "place": 16, "unpack": 16,
}


def dot(a, b):
    return lax.dot_general(a, b, (((1,), (0,)), ((), ())), preferred_element_type=F32)


def dot_nt(a, b):
    return lax.dot_general(a, b, (((1,), (1,)), ((), ())), preferred_element_type=F32)


def dot_tn(a, b):
    return lax.dot_general(a, b, (((0,), (0,)), ((), ())), preferred_element_type=F32)


def lower_half(shape):
    return lax.broadcasted_iota(jnp.int32, shape, 1) < HEAD_DIM


def swap_halves(values):
    return pltpu.roll(values, HEAD_DIM, 1)


def normalise(values):
    center = values - jnp.mean(values, axis=-1, keepdims=True)
    spread = jnp.mean(center * center, axis=-1, keepdims=True)
    scale = lax.rsqrt(spread + 1e-05)
    return center * scale, scale


def normalise_back(grad, unit, scale, gain):
    inner = grad * gain
    first = jnp.mean(inner, axis=-1, keepdims=True)
    second = jnp.mean(inner * unit, axis=-1, keepdims=True)
    return scale * (inner - first - unit * second)


def features(pair, tabs):
    wide = pair.astype(F32)
    square = wide * wide * SQ_SCALE
    high = square.astype(BF).astype(F32)
    low = swap_halves(square - high)
    keep = lower_half(wide.shape)
    even = jnp.where(keep, high, low).astype(BF)
    odd = jnp.where(keep, low, high).astype(BF)
    out = []
    for block, tab in ((even, tabs[0]), (odd, tabs[1])):
        proj = dot_nt(jnp.concatenate([pair, block], axis=1), tab)
        out.append(jnp.exp2(proj * EXP_SCALE - EXP_SHIFT).astype(BF))
    return out


def values_ones(pair):
    keep = lower_half(pair.shape)
    one = jnp.ones_like(pair)
    return jnp.where(keep, pair, one), jnp.where(keep, one, pair)


def causal_rows(first_row, rows, cols):
    return (
        lax.broadcasted_iota(jnp.int32, (rows, cols), 0) + first_row
        >= lax.broadcasted_iota(jnp.int32, (rows, cols), 1)
    )


def state_pair(state, norm, parity):
    wide = jnp.broadcast_to(norm, (HEAD_DIM, norm.shape[1]))
    return jnp.concatenate([state, wide] if parity == 0 else [wide, state], axis=0)


def kv_kernel(x_ref, gain_ref, shift_ref, w_ref, b_ref, tab_ref, h_ref, kv_ref, phik_ref, state_ref):
    width = x_ref.shape[-1]
    unit, _ = normalise(x_ref[0].astype(F32))
    low = (unit * gain_ref[...] + shift_ref[...]).astype(BF)
    h_ref[0] = low
    kv_ref[0] = (dot(low, w_ref[:, width:]) + b_ref[...][None, width:]).astype(BF)
    tabs = (tab_ref[0], tab_ref[1])
    norms = []
    for pair in range(PAIRS):
        key = kv_ref[0, :, pair * LANES : (pair + 1) * LANES]
        value = kv_ref[0, :, width + pair * LANES : width + (pair + 1) * LANES]
        phi = features(key, tabs)
        ones = values_ones(value)
        full = []
        for head in range(2):
            at = (2 * pair + head) * FEATS
            phik_ref[0, :, at : at + FEATS] = phi[head]
            full.append(dot_tn(ones[head], phi[head]))
        state_ref[0, pair * LANES : pair * LANES + HEAD_DIM, :] = full[0][:HEAD_DIM]
        state_ref[0, pair * LANES + HEAD_DIM : (pair + 1) * LANES, :] = full[1][HEAD_DIM:]
        norms += [full[0][HEAD_DIM : HEAD_DIM + 1], full[1][0:1]]
    state_ref[0, STATE_ROWS : STATE_ROWS + HEADS, :] = jnp.concatenate(norms, axis=0)
    state_ref[0, STATE_ROWS + HEADS :, :] = jnp.zeros((SCAN_ROWS - STATE_ROWS - HEADS, FEATS), F32)


def local_kernel(h_ref, w_ref, b_ref, v_ref, phik_ref, tab_ref, *rest):
    q_ref, phiq_ref, num_ref = rest[-3:]
    query = (dot(h_ref[0], w_ref[...]) + b_ref[...]).astype(BF)
    q_ref[0] = query
    phi = features(query, (tab_ref[0], tab_ref[1]))
    ones = values_ones(v_ref[0])
    span = h_ref.shape[1]
    for head in range(2):
        phiq_ref[0, :, head * FEATS : (head + 1) * FEATS] = phi[head]
        for row in range(0, span, TILE):
            cols = row + TILE
            keys = phik_ref[0, :cols, head * FEATS : (head + 1) * FEATS]
            scores = dot_nt(phi[head][row : row + TILE], keys)
            scores = jnp.where(causal_rows(row, TILE, cols), scores, 0.0).astype(BF)
            num_ref[0, row : row + TILE, head * LANES : (head + 1) * LANES] = dot(scores, ones[head][:cols])


def middle_kernel(
    per, chips, core_ref, x_ref, dy_ref, num_ref, phiq_ref, state_ref, w_out_ref, b_out_ref, gain_ref, shift_ref,
    w_up_from, b_up_ref, w_down_from, b_down_ref,
    out_ref, dy1_ref, dnum_ref, dstate_ref, sums_ref, sum_up_ref, *rest,
):
    *grads, w_up_ref, w_down_ref, w_sems = rest
    down_ref, up_ref, wout_ref = grads[2:5] if chips else grads
    loads = [
        pltpu.make_async_copy(source, place, w_sems.at[at])
        for at, (source, place) in enumerate(((w_up_from, w_up_ref), (w_down_from, w_down_ref)))
    ]

    @pl.when(pl.program_id(0) == 0)
    def _():
        for load in loads:
            load.start()

    step = pl.program_id(0)
    width = x_ref.shape[-1]
    att_parts, den_parts = [], []
    for pair in range(PAIRS):
        nums = []
        for head in range(2):
            at = 2 * pair + head
            rows = pair * LANES + head * HEAD_DIM
            state = state_pair(
                state_ref[0, rows : rows + HEAD_DIM, :].astype(BF),
                state_ref[0, STATE_ROWS + at : STATE_ROWS + at + 1, :].astype(BF),
                head,
            )
            nums.append(
                num_ref[:, at * LANES : (at + 1) * LANES]
                + dot_nt(phiq_ref[:, at * FEATS : (at + 1) * FEATS], state)
            )
        keep = lower_half(nums[0].shape)
        den = swap_halves(jnp.where(keep, nums[1], nums[0]))
        recip = 1.0 / den
        att_parts.append(jnp.where(keep, nums[0], nums[1]) * recip)
        den_parts.append(recip)
    mixed = jnp.concatenate([part.astype(BF) for part in att_parts], axis=1)
    middle = x_ref[...].astype(F32) + dot(mixed, w_out_ref[...]) + b_out_ref[...]
    unit, scale = normalise(middle)
    low = (unit * gain_ref[...] + shift_ref[...]).astype(BF)
    grad_out = dy_ref[...]
    hidden = w_up_ref.shape[1]
    chunk = 1024

    @pl.when(step == 0)
    def _():
        for load in loads:
            load.wait()

    result = middle + b_down_ref[...]
    grad_low = jnp.zeros(middle.shape, F32)

    @pl.when(step == 0)
    def _():
        sums_ref[...] = jnp.zeros_like(sums_ref)
        sum_up_ref[...] = jnp.zeros_like(sum_up_ref)

    for at in range(0, hidden, chunk):
        up = dot(low, w_up_ref[:, at : at + chunk]) + b_up_ref[:, at : at + chunk]
        square = up * up
        tanh = jnp.tanh(up * (GELU_A + GELU_A * GELU_B * square))
        half = 0.5 + 0.5 * tanh
        act = (up * half).astype(BF)
        add_to(down_ref, slice(at, at + chunk), slice(None), step, dot_tn(act, grad_out))
        slope = half + (0.5 * up) * (1.0 - tanh * tanh) * (GELU_A + 3.0 * GELU_A * GELU_B * square)
        result += dot(act, w_down_ref[at : at + chunk, :])
        dup = (dot_nt(grad_out, w_down_ref[at : at + chunk, :]) * slope).astype(BF)
        add_to(up_ref, slice(None), slice(at, at + chunk), step, dot_tn(low, dup))
        grad_low += dot_nt(dup, w_up_ref[:, at : at + chunk])
        sum_up_ref[:, at : at + chunk] += jnp.sum(dup.astype(F32), axis=0, keepdims=True)
    out_ref[...] = result.astype(BF)
    if chips:
        packed_ref, sems = grads[5:]
        behind = packed_ref.shape[2] * 2 * hidden // (2 * hidden + middle.shape[1])
        parts = [
            (half, first, count)
            for first, count in ((0, behind), (behind, packed_ref.shape[2] - behind))
            for half in range(2)
        ]
        stores = [
            pltpu.make_async_copy(
                packed_ref.at[half, :, pl.ds(first, count), :],
                grads[half].at[:, pl.ds(first, count), :],
                sems.at[at],
            )
            for at, (half, first, count) in enumerate(parts)
        ]

        @pl.when(step == pl.num_programs(0) - 1)
        def _():
            for half in range(2):
                pack_half(core_ref[0] if half else 1 - core_ref[0], chips, packed_ref.at[half], 0, down_ref, up_ref)
                stores[half].start()

    wide = grad_out.astype(F32)
    grad_mid = wide + normalise_back(grad_low, unit, scale, gain_ref[...])
    dy1_ref[...] = grad_mid
    grad_mid_low = grad_mid.astype(BF)
    add_to(wout_ref, slice(None), slice(None), step, dot_tn(mixed, grad_mid_low))
    for row, item in enumerate((wide, grad_mid, grad_low * unit, grad_low)):
        sums_ref[row : row + 1, :] += jnp.sum(item, axis=0, keepdims=True)
    grad_att = dot_nt(grad_mid_low, w_out_ref[...])

    @pl.when(lax.rem(step, per) == 0)
    def _():
        dstate_ref[...] = jnp.zeros_like(dstate_ref)

    for pair in range(PAIRS):
        grad = grad_att[:, pair * LANES : (pair + 1) * LANES] * den_parts[pair]
        keep = lower_half(grad.shape)
        prod = swap_halves(-(grad * att_parts[pair]))
        both = (jnp.where(keep, grad, prod).astype(BF), jnp.where(keep, prod, grad).astype(BF))
        for head in range(2):
            at = 2 * pair + head
            dnum_ref[:, at * LANES : (at + 1) * LANES] = both[head]
            full = dot_tn(both[head], phiq_ref[:, at * FEATS : (at + 1) * FEATS])
            rows = pair * LANES + head * HEAD_DIM
            main = full[:HEAD_DIM] if head == 0 else full[HEAD_DIM:]
            rest = full[HEAD_DIM:] if head == 0 else full[:HEAD_DIM]
            dstate_ref[0, rows : rows + HEAD_DIM, :] += main
            dstate_ref[0, STATE_ROWS + at : STATE_ROWS + at + 1, :] += jnp.sum(rest, axis=0, keepdims=True)

    if chips:

        @pl.when(step == pl.num_programs(0) - 1)
        def _():
            for half in range(2):
                pack_half(core_ref[0] if half else 1 - core_ref[0], chips, packed_ref.at[half], behind, None, wout_ref)
                stores[2 + half].start()
            for store in stores:
                store.wait()


def add_to(total_ref, rows, cols, step, values):
    total_ref[rows, cols] = jnp.where(step == 0, 0.0, total_ref[rows, cols]) + values


def pack_half(half, chips, packed_ref, base, down_ref, *wide_refs):
    if down_ref is not None:
        rows = down_ref.shape[0] // 2 // chips
        first = half * (down_ref.shape[0] // 2)
        for chip in range(chips):
            for strip in range(down_ref.shape[1] // LANES):
                packed_ref[chip, base + strip * rows : base + (strip + 1) * rows, :] = down_ref[
                    pl.ds(pl.multiple_of(first + chip * rows, rows), rows), strip * LANES : (strip + 1) * LANES
                ]
        base += rows * (down_ref.shape[1] // LANES)
    for total_ref in wide_refs:
        rows = total_ref.shape[0] // chips
        strips = total_ref.shape[1] // 2 // LANES
        for strip in range(strips):
            col = pl.multiple_of((half * strips + strip) * LANES, LANES)
            for chip in range(chips):
                packed_ref[chip, base : base + rows, :] = total_ref[
                    chip * rows : (chip + 1) * rows, pl.ds(col, LANES)
                ]
            base += rows


def score_back_kernel(
    first, q_ref, v_ref, phiq_ref, phik_ref, dnum_ref, state_ref, norm_ref, tab_ref, *rest
):
    dq_ref, dphik_ref, dv_ref = rest[-3:]
    span = q_ref.shape[1]
    ones = values_ones(v_ref[0])
    back, dvs = [], []
    for head in range(2):
        phiq = phiq_ref[0, :, head * FEATS : (head + 1) * FEATS]
        phik = phik_ref[0, :, head * FEATS : (head + 1) * FEATS]
        dnum = dnum_ref[0, :, head * LANES : (head + 1) * LANES]
        state = state_pair(
            state_ref[0, head * HEAD_DIM : (head + 1) * HEAD_DIM, :].astype(BF),
            norm_ref[0, pl.ds(2 * (first + pl.program_id(0)) + head, 1), :].astype(BF),
            head,
        )
        grads = []
        for row in range(0, span, TILE):
            cols = row + TILE
            mine = dnum[row : row + TILE]
            grad = dot_nt(mine, ones[head][:cols])
            grad = jnp.where(causal_rows(row, TILE, cols), grad, 0.0).astype(BF)
            grad_phi = dot(mine, state) + dot(grad, phik[:cols])
            grads.append((grad_phi * phiq[row : row + TILE].astype(F32)).astype(BF))
        back.append(dot(jnp.concatenate(grads, axis=0), tab_ref[head]))
        dv = []
        for row in range(0, span, TILE):
            count = span - row
            seen = (
                lax.broadcasted_iota(jnp.int32, (TILE, count), 0)
                <= lax.broadcasted_iota(jnp.int32, (TILE, count), 1)
            )
            turned = dot_nt(ones[head][row : row + TILE], dnum[row:])
            turned = jnp.where(seen, turned, 0.0).astype(BF)
            dphik_ref[0, row : row + TILE, head * FEATS : (head + 1) * FEATS] = dot(turned, phiq[row:]).astype(BF)
            scores = dot_nt(phik[row : row + TILE], phiq[row:])
            scores = jnp.where(seen, scores, 0.0).astype(BF)
            dv.append(dot(scores, dnum[row:]))
        dvs.append(jnp.concatenate(dv, axis=0))
    keep = lower_half(dvs[0].shape)
    dv_ref[0] = jnp.where(keep, dvs[0], dvs[1])
    dq_ref[0] = finish_back(back, q_ref[0]).astype(BF)


def finish_back(back, pair):
    keep = lower_half(back[0].shape)
    main = jnp.where(keep, back[0], back[1])
    total = swap_halves(jnp.where(keep, back[1], back[0]))
    return main * Z_SCALE - total * pair.astype(F32) * (HEAD_DIM ** (-0.5))


def final_kernel(
    x_ref, dy1_ref, kv_ref, phik_ref, dq_ref, dphik_ref, dv_ref, later_ref, tab_ref, gain_ref, shift_ref, w_ref,
    *rest,
):
    dx_ref, dqkv_ref, sums_ref, sum_qkv_ref = rest[-4:]
    width = x_ref.shape[-1]
    grad = dot_nt(dq_ref[0], w_ref[:, :width])

    sums_ref[...] = jnp.zeros_like(sums_ref)
    for pair in range(PAIRS):
        key = kv_ref[0, :, pair * LANES : (pair + 1) * LANES]
        value = kv_ref[0, :, width + pair * LANES : width + (pair + 1) * LANES]
        ones = values_ones(value)
        back, dvs = [], []
        for head in range(2):
            at = 2 * pair + head
            rows = pair * LANES + head * HEAD_DIM
            state = later_ref[0, rows : rows + HEAD_DIM, :].astype(BF)
            norm = later_ref[0, STATE_ROWS + at : STATE_ROWS + at + 1, :]
            high = norm.astype(BF)
            low = (norm - high.astype(F32)).astype(BF)
            rest = jnp.concatenate(
                [high.astype(F32), low.astype(F32), jnp.zeros((HEAD_DIM - 2, FEATS), F32)], axis=0
            ).astype(BF)
            full = jnp.concatenate([state, rest] if head == 0 else [rest, state], axis=0)
            phik = phik_ref[0, :, at * FEATS : (at + 1) * FEATS]
            grad_phi = dphik_ref[0, :, at * FEATS : (at + 1) * FEATS].astype(F32) + dot(ones[head], full)
            inner = (grad_phi * phik.astype(F32)).astype(BF)
            back.append(dot(inner, tab_ref[head]))
            dvs.append(dot_nt(phik, full))
        keep = lower_half(dvs[0].shape)
        dk = finish_back(back, key).astype(BF)
        dv = (dv_ref[0, :, pair * LANES : (pair + 1) * LANES] + jnp.where(keep, dvs[0], dvs[1])).astype(BF)
        dqkv_ref[0, :, width + pair * LANES : width + (pair + 1) * LANES] = dk
        dqkv_ref[0, :, 2 * width + pair * LANES : 2 * width + (pair + 1) * LANES] = dv
    dqkv_ref[0, :, :width] = dq_ref[0]
    dkv = dqkv_ref[0, :, width:]
    grad += dot_nt(dkv, w_ref[:, width:])
    unit, scale = normalise(x_ref[0].astype(F32))
    dx_ref[0] = (dy1_ref[0] + normalise_back(grad, unit, scale, gain_ref[...])).astype(BF)
    sums_ref[0:1, :] = jnp.sum(grad * unit, axis=0, keepdims=True)
    sums_ref[1:2, :] = jnp.sum(grad, axis=0, keepdims=True)
    sum_qkv_ref[:, :width] = jnp.sum(dq_ref[0].astype(F32), axis=0, keepdims=True)
    sum_qkv_ref[:, width:] = jnp.sum(dkv.astype(F32), axis=0, keepdims=True)


def put_chunks(out_ref, values):
    chips = out_ref.shape[0]
    rows = values.shape[0] // chips
    for chunk in range(chips):
        for strip in range(values.shape[1] // LANES):
            out_ref[chunk, strip * rows : (strip + 1) * rows, :] = values[
                chunk * rows : (chunk + 1) * rows, strip * LANES : (strip + 1) * LANES
            ]


def qkv_grads_kernel(half_ref, h1_ref, dqkv_ref, out_ref):
    put_chunks(out_ref, dot_tn(h1_ref[...], dqkv_ref[...]))


def place_kernel(counts, rows, meta_ref, *refs):
    out_ref = refs[-1]
    total = sum(counts)
    along = refs[0].shape[1]
    for core in range(2):

        @pl.when(meta_ref[0] == core)
        def _():
            for half in range(2):
                base = out_ref.shape[1] // LANES // 2 * (half ^ core)
                for at in range(total):
                    piece = refs[half * total + at]
                    first = at < counts[0]
                    col = base if first else base + refs[half * total].shape[2] // rows
                    for inner in range(piece.shape[0]):
                        x, y = (at, inner) if first else (inner, at - counts[0])
                        row = (meta_ref[1] ^ x) * counts[1] + (meta_ref[2] ^ y)
                        for last in range(along):
                            chip = row * along + (meta_ref[3] ^ last)
                            where = pl.ds(pl.multiple_of(chip * rows, rows), rows)
                            for strip in range(piece.shape[2] // rows):
                                out_ref[where, (col + strip) * LANES : (col + strip + 1) * LANES] = piece[
                                    inner, last, strip * rows : (strip + 1) * rows, :
                                ]


def unpack_kernel(packed_ref, *out_refs):
    row = 0
    block = packed_ref.shape[0]
    for out_ref in out_refs:
        rows = out_ref.shape[0] // block
        for strip in range(out_ref.shape[1] // LANES):
            for chunk in range(block):
                out_ref[chunk * rows : (chunk + 1) * rows, strip * LANES : (strip + 1) * LANES] = packed_ref[
                    chunk, row : row + rows, :
                ]
            row += rows


def whole(shape):
    return pl.BlockSpec(shape, lambda *_: (0,) * len(shape))


def params(count, name):
    return pltpu.CompilerParams(
        dimension_semantics=("arbitrary",) * count if count else None, vmem_limit_bytes=LIMITS[name] * 1024 * 1024
    )


def shape(dims, kind):
    return jax.ShapeDtypeStruct(dims, kind)


def place_of():
    place = 0
    for axis in AXES:
        place = place * lax.axis_size(axis) + lax.axis_index(axis)
    return place


def send(values, mask):
    count = math.prod(lax.axis_size(axis) for axis in AXES)
    return lax.ppermute(values, AXES, [(i, i ^ mask) for i in range(count)])


def bit_of(bit):
    return (place_of() >> bit) & 1


def swap_with(values, bit):
    return send(values, 1 << bit)


def axis_bits(axis):
    at = 0
    for other in reversed(AXES):
        size = lax.axis_size(other).bit_length() - 1
        if other == axis:
            return list(range(at, at + size))
        at += size


def value_of(bits):
    place = place_of()
    return sum(((place >> b) & 1) << i for i, b in enumerate(bits))


def mask_of(bits, value):
    return sum(((value >> i) & 1) << b for i, b in enumerate(bits))


def place_pieces(own, meta, dims):
    both = own[0] + own[1] + own[2]
    chips = len(own[0]) * len(own[1]) * own[0][0].shape[1]
    return pl.pallas_call(
        functools.partial(place_kernel, (len(own[0]), len(own[1])), dims[0] // chips),
        in_specs=[pl.BlockSpec(memory_space=pltpu.SMEM)] + [pl.BlockSpec(memory_space=pltpu.VMEM)] * len(both),
        out_specs=pl.BlockSpec(memory_space=pltpu.VMEM),
        out_shape=shape(dims, F32),
        compiler_params=params(0, "place"),
        name="place",
    )(meta, *both)


def scan_stream(values, bits, split, reverse):
    bit = bits[0]
    mine = bit_of(bit)
    far = (mine == 0) if reverse else (mine == 1)
    if split:
        half = values.shape[0] // 2
        kept = lax.dynamic_slice_in_dim(values, mine * half, half, 0)
        (got,) = yield [(lax.dynamic_slice_in_dim(values, (1 - mine) * half, half, 0), 1 << bit)]
        before = yield from scan_stream(kept + got, bits[1:], split - 1, reverse)
        ours = before + jnp.where(far, got, 0.0)
        (theirs,) = yield [(before + jnp.where(far, 0.0, kept), 1 << bit)]
        return jnp.concatenate(
            [jnp.where(mine == 0, ours, theirs), jnp.where(mine == 0, theirs, ours)], axis=0
        )
    (got,) = yield [(values, 1 << bit)]
    part = jnp.where(far, got, 0.0)
    if len(bits) == 1:
        return part
    rest = yield from scan_stream(values + got, bits[1:], 0, reverse)
    return part + rest


def cut_part(part, axis, at, rows):
    start, size = [0] * part.ndim, list(part.shape)
    start[axis], size[axis] = at, 1
    if rows:
        start[-2], size[-2] = rows
    return jnp.squeeze(lax.dynamic_slice(part, start, size), axis)


def chunks(parts, axis, bits, rows=None):
    mine = value_of(bits)
    own = [cut_part(part, axis, mine, rows) for part in parts]
    others = [
        add_all([cut_part(part, axis, mine ^ value, rows) for part in parts]) for value in range(1, 1 << len(bits))
    ]
    return own, others


def add_all(items):
    return functools.reduce(jnp.add, items)


def to_partners(items, bits):
    return [(item, mask_of(bits, value + 1)) for value, item in enumerate(items)]


def to_all(item, bits):
    return to_partners([item] * ((1 << len(bits)) - 1), bits)


def scatter_stream(theirs, mine):
    x, y, z = axis_bits("x"), axis_bits("y"), axis_bits("z")
    (got,) = yield [(theirs, 1)]
    parts = [mine() if callable(mine) else mine, got]
    cut = parts[0].shape[1] // 2
    parts = [item.reshape(1 << len(x), 1 << len(y), 1 << len(z), *item.shape[1:]) for item in parts]
    (a, a_out), (b, b_out) = chunks(parts, 0, x, (0, cut)), chunks(parts, 1, y, (cut, cut))
    got = yield to_partners(a_out, x) + to_partners(b_out, y)
    a, a_out = chunks(a + got[: len(a_out)], 0, y)
    b, b_out = chunks(b + got[-len(b_out) :], 0, x)
    got = yield to_partners(a_out, y) + to_partners(b_out, x)
    parts = [a + got[: len(a_out)], b + got[-len(b_out) :]]
    both = jnp.concatenate([add_all(part) for part in parts], axis=1)
    own, out = chunks([both], 0, z)
    got = yield to_partners(out, z)
    return add_all(own + got)


def bucket_stream(theirs, mine):
    x, y, z = axis_bits("x"), axis_bits("y"), axis_bits("z")
    chunk = yield from scatter_stream(theirs, mine)
    got = yield to_all(chunk, z)
    cut = chunk.shape[0] // 2
    a, b = [jnp.stack([item[at : at + cut] for item in [chunk] + got]) for at in (0, cut)]
    got = yield to_all(a, y) + to_all(b, x)
    count = (1 << len(y)) - 1
    a, b = jnp.stack([a] + got[:count]), jnp.stack([b] + got[count:])
    got = yield to_all(a, x) + to_all(b, y)
    count = (1 << len(x)) - 1
    a, b = [a] + got[:count], [b] + got[count:]
    got = yield [(item, 1) for item in a + b]
    return a, b, got


def small_stream(values, bits):
    for bit in bits:
        (got,) = yield [(values, 1 << bit)]
        values = values + got
    return values


class Stream:
    def __init__(self, chain):
        self.chain, self.value, self.flying = chain, None, None
        self.pending = next(chain)

    def feed(self, got):
        self.flying = None
        try:
            self.pending = self.chain.send(got)
        except StopIteration as end:
            self.pending, self.value = None, end.value


def phase(start=(), wait=(), work=None, inputs=()):
    ready = [[item for item, _ in stream.pending] for stream in start]
    ready, inputs = lax.optimization_barrier((ready, tuple(inputs)))
    for stream, items in zip(start, ready):
        stream.flying = [send(item, mask) for item, (_, mask) in zip(items, stream.pending)]
    done = tuple(work(*inputs)) if work else ()
    got, done = lax.optimization_barrier(([stream.flying for stream in wait], done))
    for stream, items in zip(wait, got):
        stream.feed(list(items))
    return done


def of_stages(stream, wait_too=()):
    while stream.pending is not None:
        phase([stream], [stream])
    return stream.value


def half_of(half):
    return half.astype(jnp.int32).reshape(1)


def qkv_grads(half, chips, h1, dqkv):
    rows, width = h1.shape
    block = 2 * LANES
    steps = dqkv.shape[1] // 2 // block
    own = width * block // chips // LANES
    return pl.pallas_call(
        qkv_grads_kernel,
        grid_spec=pltpu.PrefetchScalarGridSpec(
            num_scalar_prefetch=1,
            grid=(steps,),
            in_specs=[
                pl.BlockSpec((rows, width), lambda j, h: (0, 0)),
                pl.BlockSpec((rows, block), lambda j, h: (0, h[0] * steps + j)),
            ],
            out_specs=pl.BlockSpec((chips, own, LANES), lambda j, h: (0, j, 0)),
        ),
        out_shape=shape((chips, own * steps, LANES), F32),
        compiler_params=params(1, "qkv_grads"),
        name="qkv_grads",
    )(half_of(half), h1, dqkv)


def unpack(packed, hidden, width):
    devices = packed.shape[0]
    block = 4
    per = devices // 2 // block
    rows = width // (devices // 2) * block
    return pl.pallas_call(
        unpack_kernel,
        grid=(devices // block,),
        in_specs=[pl.BlockSpec((block,) + packed.shape[1:], lambda t: (t, 0, 0))],
        out_specs=[
            pl.BlockSpec((hidden * block // devices, width), lambda t: (t, 0)),
            pl.BlockSpec((rows, hidden // 2), lambda t: (t % per, t // per)),
            pl.BlockSpec((rows, width // 2), lambda t: (t % per, t // per)),
        ],
        out_shape=[shape((hidden, width), F32), shape((width, hidden), F32), shape((width, width), F32)],
        compiler_params=params(1, "unpack"),
        name="unpack",
    )(packed)


def seq_block(seq, span, width, at=0):
    return pl.BlockSpec((1, span, width), lambda p: (seq, 0, at + p))


def run_local(seq, h1, w_qkv, b_qkv, kv, phi_k, tab_in, *old):
    seqs, span, width = h1.shape
    block = functools.partial(seq_block, seq, span)
    return pl.pallas_call(
        local_kernel,
        grid=(PAIRS,),
        in_specs=[
            pl.BlockSpec((1, span, width), lambda p: (seq, 0, 0)), pl.BlockSpec((width, LANES), lambda p: (0, p)),
            pl.BlockSpec((1, LANES), lambda p: (0, p)), block(LANES, PAIRS), block(2 * FEATS),
            whole((2, FEATS, 2 * LANES)),
        ]
        + [pl.BlockSpec(memory_space=pl.ANY)] * len(old),
        out_specs=[block(LANES), block(2 * FEATS), block(2 * LANES)],
        out_shape=[
            shape((seqs, span, width), BF), shape((seqs, span, HEADS * FEATS), BF),
            shape((seqs, span, HEADS * LANES), F32),
        ],
        input_output_aliases={6 + i: i for i in range(len(old))},
        compiler_params=params(1, "local"),
        name="local",
    )(h1, w_qkv, b_qkv, kv, phi_k, tab_in, *old)


def run_scores(seq, first, count, q, kv, phi_q, phi_k, dnum, before, tab_back, *old):
    seqs, span, width = q.shape
    block = lambda w, at=0: seq_block(seq, span, w, at + first)
    return pl.pallas_call(
        functools.partial(score_back_kernel, first),
        grid=(count,),
        in_specs=[
            block(LANES), block(LANES, PAIRS), block(2 * FEATS), block(2 * FEATS), block(2 * LANES),
            pl.BlockSpec((1, LANES, FEATS), lambda p: (seq, first + p, 0)),
            pl.BlockSpec((1, HEADS, FEATS), lambda p: (seq, STATE_ROWS // HEADS, 0)),
            whole((2, FEATS, LANES)),
        ]
        + [pl.BlockSpec(memory_space=pl.ANY)] * len(old),
        out_specs=[block(LANES), block(2 * FEATS), block(LANES)],
        out_shape=[
            shape((seqs, span, width), BF), shape((seqs, span, HEADS * FEATS), BF),
            shape((seqs, span, width), F32),
        ],
        input_output_aliases={8 + i: i for i in range(len(old))},
        compiler_params=params(1, "scores"),
        name="scores",
    )(q, kv, phi_q, phi_k, dnum, before, before, tab_back, *old)


def run_keys(x, gain, bias, w_qkv, b_qkv, tab_in):
    seqs, span, width = x.shape
    three = lambda d: pl.BlockSpec((1,) + d, lambda s: (s, 0, 0))
    return pl.pallas_call(
        kv_kernel,
        grid=(seqs,),
        in_specs=[
            three((span, width)), whole((1, width)), whole((1, width)), whole((width, 3 * width)),
            whole((3 * width,)), whole((2, FEATS, 2 * LANES)),
        ],
        out_specs=[
            three((span, width)), three((span, 2 * width)), three((span, HEADS * FEATS)), three((SCAN_ROWS, FEATS)),
        ],
        out_shape=[
            shape((seqs, span, width), BF), shape((seqs, span, 2 * width), BF),
            shape((seqs, span, HEADS * FEATS), BF), shape((seqs, SCAN_ROWS, FEATS), F32),
        ],
        compiler_params=params(1, "keys"),
        name="keys",
    )(x, gain, bias, w_qkv, b_qkv, tab_in)


def run_middle(seqs, chips, core, x, dy, num, phi_q, before, w_out, b_out, gain, bias, w_up, b_up, w_down, b_down):
    rows, width = x.shape
    hidden = w_up.shape[1]
    per = rows // seqs // MID_TILE
    tile = lambda w: pl.BlockSpec((MID_TILE, w), lambda t, c: (t, 0))
    of_seq = lambda d: pl.BlockSpec((1,) + d, lambda t, c: (t // per, 0, 0))
    once = lambda d: pl.BlockSpec(d, lambda t, c: (0,) * len(d), pipeline_mode=pl.Buffered(1))
    sums = [(hidden, width), (width, hidden), (width, width)]
    packed = (hidden * width * 2 + width * width) // 2 // max(chips, 1) // LANES
    grads = [(chips, packed, LANES)] * 2 if chips else sums
    anywhere = pl.BlockSpec(memory_space=pl.ANY)
    scratch = [pltpu.VMEM((width, hidden), BF), pltpu.VMEM((hidden, width), BF), pltpu.SemaphoreType.DMA((2,))]
    if chips:
        scratch = [
            *(pltpu.VMEM(item, F32) for item in sums), pltpu.VMEM((2, chips, packed, LANES), F32),
            pltpu.SemaphoreType.DMA((4,)), *scratch,
        ]
    return pl.pallas_call(
        functools.partial(middle_kernel, per, chips),
        grid_spec=pltpu.PrefetchScalarGridSpec(
            num_scalar_prefetch=1,
            grid=(seqs * per,),
            in_specs=[
                tile(width), tile(width), tile(HEADS * LANES), tile(HEADS * FEATS), of_seq((SCAN_ROWS, FEATS)),
                once((width, width)), once((1, width)), once((1, width)), once((1, width)),
                anywhere, once((1, hidden)), anywhere, once((1, width)),
            ],
            out_specs=[
                tile(width), tile(width), tile(HEADS * LANES), of_seq((SCAN_ROWS, FEATS)),
                once((8, width)), once((1, hidden)),
            ]
            + [anywhere if chips else once(item) for item in grads],
            scratch_shapes=scratch,
        ),
        out_shape=[
            shape((rows, width), BF), shape((rows, width), F32), shape((rows, HEADS * LANES), BF),
            shape((seqs, SCAN_ROWS, FEATS), F32), shape((8, width), F32), shape((1, hidden), F32),
        ]
        + [shape(item, F32) for item in grads],
        compiler_params=params(1, "middle"),
        name="middle",
    )(half_of(core), x, dy, num, phi_q, before, w_out, b_out, gain, bias, w_up, b_up, w_down, b_down)


def run_final(seq, x, dy1, kv, phi_k, dq, dphik, dv, later, tab_back, gain, bias, w_qkv, *old):
    seqs, span, width = x.shape
    three = lambda d: pl.BlockSpec((1,) + d, lambda t: (seq, 0, 0))
    return pl.pallas_call(
        final_kernel,
        grid=(1,),
        in_specs=[
            three((span, width)), three((span, width)), three((span, 2 * width)), three((span, HEADS * FEATS)),
            three((span, width)), three((span, HEADS * FEATS)), three((span, width)), three((SCAN_ROWS, FEATS)),
            whole((2, FEATS, LANES)), whole((1, width)), whole((1, width)), whole((width, 3 * width)),
        ]
        + [pl.BlockSpec(memory_space=pl.ANY)] * len(old),
        out_specs=[three((span, width)), three((span, 3 * width)), whole((8, width)), whole((1, 3 * width))],
        out_shape=[
            shape((seqs, span, width), BF), shape((seqs, span, 3 * width), BF), shape((8, width), F32),
            shape((1, 3 * width), F32),
        ],
        input_output_aliases={12 + i: i for i in range(len(old))},
        compiler_params=params(1, "final"),
        name="final",
    )(x, dy1, kv, phi_k, dq, dphik, dv, later, tab_back, gain, bias, w_qkv, *old)


def shards(
    tokens, cotangent, gain_attn, shift_attn, w_qkv, b_qkv, w_out, b_out,
    gain_ffn, shift_ffn, w_up, b_up, w_down, b_down, tables, pick,
):
    seqs, span, width = tokens.shape
    hidden = w_up.shape[1]
    rows = seqs * span
    table = lax.dynamic_index_in_dim(tables, pick[0] % 2, 0, keepdims=False)
    none = jnp.zeros_like(table)
    minus = jnp.full((FEATS, LANES), -1.0, BF)
    tab_in = jnp.stack(
        [jnp.concatenate([table, none, minus], axis=1), jnp.concatenate([none, table, minus], axis=1)]
    )
    one = jnp.ones_like(table)
    tab_back = jnp.stack([jnp.concatenate([table, one], axis=1), jnp.concatenate([one, table], axis=1)])
    row = lambda a: a.reshape(1, -1)
    seq_bits = axis_bits("c") + axis_bits("y") + axis_bits("z")

    h1, kv, phi_k, state = run_keys(tokens, row(gain_attn), row(shift_attn), w_qkv, b_qkv, tab_in)

    scan = Stream(scan_stream(state.reshape(seqs * SCAN_ROWS, FEATS), seq_bits, len(seq_bits) - 1, False))
    phase([scan], [scan])
    local = None
    for seq in range(seqs):
        work = lambda kv, phi_k, *old: run_local(seq, h1, w_qkv, row(b_qkv), kv, phi_k, tab_in, *old)
        local = phase([scan], [scan], work, (kv, phi_k) + tuple(local or ()))
        if seq == 0:
            phase([scan], [scan])
    q, phi_q, num = local
    before = of_stages(scan).reshape(seqs, SCAN_ROWS, FEATS)

    flat = lambda a: a.reshape(rows, a.shape[-1])
    chips = lax.axis_size("x") * lax.axis_size("y") * lax.axis_size("z")
    fits = width % (16 * chips) == 0
    core = bit_of(0)
    meta = jnp.stack([lax.axis_index(axis) for axis in ("c", "x", "y", "z")]).astype(jnp.int32)
    out, dy1, dnum, dstate, sums, sum_up, *grads = run_middle(
        seqs, chips if fits else 0, core, flat(tokens), flat(cotangent), flat(num), flat(phi_q), before, w_out,
        row(b_out), row(gain_ffn), row(shift_ffn), w_up, row(b_up), w_down, row(b_down),
    )
    scan = Stream(scan_stream(dstate.reshape(seqs * SCAN_ROWS, FEATS), seq_bits, len(seq_bits) - 1, True))
    def back(seq, first, count):
        return lambda dnum, *old: run_scores(
            seq, first, count, q, kv, phi_q, phi_k, dnum.reshape(seqs, span, -1), before, tab_back, *old
        )

    def last(seq):
        return lambda dphik, *old: run_final(
            seq, tokens, dy1.reshape(seqs, span, width), kv, phi_k, dq, dphik, dv, later, tab_back,
            row(gain_attn), row(shift_attn), w_qkv, *old
        )

    half_pairs = PAIRS // 2
    if fits:
        theirs, mine = grads
        ffn = Stream(scatter_stream(theirs, mine))
        phase([scan], [scan])
        old = phase([scan, ffn], [scan, ffn], back(0, 0, half_pairs), (dnum,))
        phase([scan])
        phase([ffn], [scan])
        old = phase([scan], [scan], back(0, half_pairs, half_pairs), (dnum,) + tuple(old))
        phase([scan], [scan])
        old = phase([scan], [scan, ffn], back(1, 0, half_pairs), (dnum,) + tuple(old))
        old = phase([scan, ffn], [scan, ffn], back(1, half_pairs, half_pairs), (dnum,) + tuple(old))
        later = scan.value
    else:
        old = phase([scan], [scan], back(0, 0, PAIRS), (dnum,))
        old = phase([scan], [scan], back(1, 0, PAIRS), (dnum,) + tuple(old))
        later = of_stages(scan)
    dq, dphik, dv = old
    later = later.reshape(seqs, SCAN_ROWS, FEATS)

    def join(*items):
        sums_attn, sum_qkv = items[0] + items[2], items[1] + items[3]
        return jnp.concatenate(
            [sums[:4].reshape(-1), sum_up.reshape(-1), sums_attn[:2].reshape(-1), sum_qkv.reshape(-1)]
        ).reshape(-1, LANES)

    all_bits = [bit for axis in reversed(AXES) for bit in axis_bits(axis)]
    if fits:
        some = lambda half, dqkv: qkv_grads(half, chips, flat(h1), flat(dqkv))

        def both(dphik):
            dx, dqkv, *parts = last(0)(dphik)
            dx, dqkv, *more = last(1)(dphik, dx, dqkv)
            return dx, some(1 - core, dqkv), some(core, dqkv), *parts, *more

        dx, theirs, mine, *parts = phase([ffn], [ffn], both, (dphik,))
        qkv_sum = Stream(bucket_stream(theirs, mine))
        packed = lax.all_gather(ffn.value, ("c", "x", "y", "z"))
        small = Stream(small_stream(join(*parts), all_bits))
        while qkv_sum.pending is not None or small.pending is not None:
            both = [item for item in (qkv_sum, small) if item.pending is not None]
            phase(both, both)
        grad_w_qkv = place_pieces(qkv_sum.value, meta, (width, 3 * width))
        small = small.value
        grad_w_down, grad_w_up, grad_w_out = unpack(packed, hidden, width)
    else:
        dx, dqkv, *parts = last(0)(dphik)
        dx, dqkv, *more = last(1)(dphik, dx, dqkv)
        grad_w_down, grad_w_up, grad_w_out, grad_w_qkv = lax.psum(
            (
                *grads, dot_tn(flat(h1), flat(dqkv)),
            ),
            AXES,
        )
        small = of_stages(Stream(small_stream(join(*parts, *more), all_bits)))
    small = small.reshape(-1)
    cuts = [width * i for i in range(1, 5)]
    cuts += [cuts[-1] + hidden, cuts[-1] + hidden + width, cuts[-1] + hidden + 2 * width]
    b_down_g, b_out_g, gain_f, shift_f, b_up_g, gain_a, shift_a, b_qkv_g = jnp.split(small, cuts)
    return (
        out.reshape(seqs, span, width), dx, gain_a, shift_a, grad_w_qkv, b_qkv_g,
        grad_w_out, b_out_g, gain_f, shift_f, grad_w_up, b_up_g, grad_w_down, b_down_g,
    )


def solution(mesh):
    dp, seq = mesh.shape["dp"], mesh.shape["seq"]
    cut = jax.sharding.Mesh(mesh.devices.reshape(dp, 4, seq // 8, 2), AXES)
    split = P("x", ("z", "y", "c"), None)
    return jax.shard_map(
        shards,
        mesh=cut,
        in_specs=(split, split) + (P(),) * 14,
        out_specs=(split, split) + (P(),) * 12,
        check_vma=False,
    )
```
